512 devices in a mesh: row: 16 (over y, core), col: 32 (over z, x).
Axes of the slice: x: 4, y: 8, z: 8, core: 2. Of those that a mesh axis runs over, the one named last changes fastest.
Arguments:
- tokens: bfloat16 [256, 512, 256], P('row', 'col'), may hold values from -6 to 6
- input_weight: bfloat16 [256, 1024], replicated, may hold values from -0.375 to 0.375
- kernel: float32 [7, 7, 512], replicated, may hold values from -0.875 to 0.875
- direction_decay_table: float32 [4, 512], replicated, may hold values from 9.765625e-05 to 0.0333333333
- pixel_extra_decay: float32 [256, 512], P('row', 'col'), may hold values from 0 to 0.69
- output_weight: bfloat16 [512, 256], replicated, may hold values from -0.25 to 0.25
Outputs:
- mixed: bfloat16 [256, 512, 256], P('row', 'col')
The draws below stay inside these ranges and needn't reach their ends.
All inputs are finite; a program needn't handle non-finite values.
Results may differ from the reference program's by a relative error of at most 0.0049.
Values may be sent and summed in bfloat16 or wider, within the bound.
No kernel may reach another device: no remote copies, remote signals or barrier semaphores. Data moves between devices by JAX's collectives and lax.ppermute only.
A program may use at most 64 MiB of HBM per device.

```python
import math
import jax
import jax.numpy as jnp
from jax import lax

C = 256
E = 512
H = 256
W = 512


def draw_direction_decay_table(key, part):
    key = jax.random.fold_in(key, 11)
    key_slow, key_fast, key_pick = jax.random.split(key, 3)
    fast_share = 0.3
    chain = jnp.array([W, W, H, H], jnp.float32)[:, None]
    slow = jnp.exp(jax.random.uniform(key_slow, (4, E), jnp.float32, math.log(0.05), math.log(0.5))) / chain
    fast = jax.random.uniform(key_fast, (4, E), jnp.float32, 1.0 / 50.0, 1.0 / 30.0)
    picked = jax.random.uniform(key_pick, (4, E), jnp.float32) < fast_share
    return jnp.where(picked, fast, slow)


def draw_pixel_extra_decay(key, part):
    key = jax.random.fold_in(key, 23)
    key_hit, key_size = jax.random.split(key)
    hits = jax.random.uniform(key_hit, (H, W), jnp.float32) < 4.0 / W
    sizes = jax.random.uniform(key_size, (H, W), jnp.float32, 0.22, 0.69)
    return jnp.where(hits, sizes, 0.0)


def block_levels(key, shape, pieces, least, largest):
    level, own = 1.0, jax.random.fold_in(key, 6)
    for dim, blocks in pieces:
        draws = jnp.exp(jax.random.uniform(jax.random.fold_in(own, dim), (blocks,), jnp.float32, least / len(pieces), largest / len(pieces)))
        level = level * jnp.repeat(draws, shape[dim] // blocks).reshape([-1 if axis == dim else 1 for axis in range(len(shape))])
    return level


def noise(own_key, shape, scale, bound, cuts=(), held_as=jnp.bfloat16):
    values = scale * jax.random.normal(own_key, shape, jnp.float32)
    if cuts:
        values = values * block_levels(own_key, shape, cuts, -0.22, 0.18)
    return jnp.clip(values, -bound, bound).astype(held_as)


def setup_inputs(seed: int = 0) -> dict:
    keys = jax.random.split(jax.random.key(seed), 7)
    tokens = noise(keys[0], (H, W, C), 1.0, 6.0, ((0, 16), (1, 32)))
    input_weight = noise(keys[1], (C, 2 * E), C ** -0.5, 0.375)
    kernel = noise(keys[2], (7, 7, E), 49 ** -0.5, 0.875, (), jnp.float32)
    direction_decay_table = draw_direction_decay_table(jax.random.fold_in(keys[6], 71), 0)
    pixel_extra_decay = draw_pixel_extra_decay(jax.random.fold_in(keys[6], 71), 0)
    output_weight = noise(keys[5], (E, C), E ** -0.5, 0.25)
    return dict(tokens=tokens, input_weight=input_weight, kernel=kernel, direction_decay_table=direction_decay_table, pixel_extra_decay=pixel_extra_decay, output_weight=output_weight)


def combine(former, latter):
    return (former[0] * latter[0], latter[0] * former[1] + latter[1])

def directed(values, decay_logarithm, scan_axis, backward):
    decays = jnp.exp(-decay_logarithm)
    inflow = jnp.sqrt(-jnp.expm1(-2.0 * decay_logarithm)) * values
    return lax.associative_scan(combine, (decays, inflow), reverse=backward, axis=scan_axis)[1]

def stencil(values_pre, taps):
    padded = jnp.pad(values_pre, ((3, 3), (3, 3), (0, 0)))
    summed = jnp.zeros(values_pre.shape, jnp.float32)
    for shift_row in range(7):
        for shift_col in range(7):
            summed = summed + taps[shift_row, shift_col][None, None, :] * padded[shift_row:shift_row + H, shift_col:shift_col + W]
    return summed

def reference(tokens, input_weight, kernel, direction_decay_table, pixel_extra_decay, output_weight):
    block_width = 64 if E % 64 == 0 else E
    blocks = E // block_width

    def one_block(index):
        offset = index * block_width
        w_values = lax.dynamic_slice_in_dim(input_weight, offset, block_width, 1)
        w_gate = lax.dynamic_slice_in_dim(input_weight, offset + E, block_width, 1)
        taps = lax.dynamic_slice_in_dim(kernel, offset, block_width, 2)
        decay_block_slice = lax.dynamic_slice_in_dim(direction_decay_table, offset, block_width, 1)
        values_pre = jnp.dot(tokens, w_values, preferred_element_type=jnp.float32).astype(jnp.bfloat16)
        values = jax.nn.silu(stencil(values_pre.astype(jnp.float32), taps))
        gate_pre = jnp.dot(tokens, w_gate, preferred_element_type=jnp.float32)
        summed = jnp.zeros(values.shape, jnp.float32)
        setups = ((1, False), (1, True), (0, False), (0, True))
        for scan_direction in range(4):
            decay_logarithm = decay_block_slice[scan_direction][None, None, :] + pixel_extra_decay[:, :, None]
            summed = summed + directed(values, decay_logarithm, setups[scan_direction][0], setups[scan_direction][1])
        return (summed * jax.nn.silu(gate_pre)).astype(jnp.bfloat16)
    gated = lax.map(one_block, jnp.arange(blocks, dtype=jnp.int32))
    gated = jnp.moveaxis(gated, 0, 2).reshape(H, W, E)
    mixed = tokens.astype(jnp.float32) + jnp.dot(gated, output_weight, preferred_element_type=jnp.float32)
    return mixed.astype(jnp.bfloat16)
```

```python
import functools

import jax
import jax.numpy as jnp
from jax import lax
from jax.experimental import pallas as pl
from jax.experimental.pallas import tpu as pltpu
from jax.sharding import PartitionSpec as P

T = 16
PX = T * T
PW = 24
LANES = 128
F32 = jnp.float32
BF16 = jnp.bfloat16
VMEM = pltpu.VMEM


def conv_scan_kernel(pad_ref, wv_ref, taps_ref, cst_ref, px_ref,
                     sum_ref, left_ref, right_ref, down_ref, up_ref,
                     v_ref, g_ref, h_ref, val_ref):
    groups = v_ref.shape[0]
    rows = T + 6
    pad = pad_ref[...]
    for half in range(groups // 2):
        p = jnp.dot(pad, wv_ref[:, half * 256:(half + 1) * 256], preferred_element_type=F32)
        p = p.astype(BF16).astype(F32)
        v_ref[2 * half] = p[:, :LANES]
        v_ref[2 * half + 1] = p[:, LANES:]
    px = px_ref[...]
    g_ref[...] = jnp.broadcast_to(px[:, 0:1], (PX, LANES))
    h_ref[...] = jnp.broadcast_to(px[:, 1:2], (PX, LANES))

    def group(ct, carry):
        lanes = pl.ds(pl.multiple_of(ct * LANES, LANES), LANES)
        cst = [cst_ref[pl.ds(k, 1), lanes] for k in range(12)]

        def flow(d, g, h, x):
            q = cst[4 + d] + cst[8 + d] * h
            return cst[d] * g, q * lax.rsqrt(q) * x

        for jt in range(2):
            acc = [jnp.zeros((8, LANES), F32) for _ in range(T)]
            for b in range(7):
                tap = [taps_ref[pl.ds(a * 7 + b, 1), lanes] for a in range(7)]
                tap = [jnp.broadcast_to(t, (8, LANES)) for t in tap]
                for r in range(rows):
                    x = v_ref[ct, pl.ds(r * PW + jt * 8 + b, 8), :]
                    for a in range(7):
                        i = r - a
                        if 0 <= i < T:
                            acc[i] = acc[i] + tap[a] * x
            vals = [x / (1.0 + jnp.exp(-x)) for x in acc]
            for i in range(T):
                val_ref[pl.ds(i * T + jt * 8, 8), :] = vals[i]
            state = jnp.zeros((8, LANES), F32)
            downs = []
            for i in range(T):
                at = pl.ds(i * T + jt * 8, 8)
                d, f = flow(2, g_ref[at, :], h_ref[at, :], vals[i])
                state = d * state + f
                downs.append(state)
            down_ref[ct, pl.ds(jt * 8, 8), :] = state
            state = jnp.zeros((8, LANES), F32)
            for i in reversed(range(T)):
                at = pl.ds(i * T + jt * 8, 8)
                d, f = flow(3, g_ref[at, :], h_ref[at, :], vals[i])
                state = d * state + f
                sum_ref[ct, at, :] = downs[i] + state
            up_ref[ct, pl.ds(jt * 8, 8), :] = state
        for it in range(2):
            state = jnp.zeros((8, LANES), F32)
            lefts = []
            for j in range(T):
                at = pl.ds(it * 8 * T + j, 8, stride=T)
                d, f = flow(0, g_ref[at, :], h_ref[at, :], val_ref[at, :])
                state = d * state + f
                lefts.append(state)
            left_ref[ct, pl.ds(it * 8, 8), :] = state
            state = jnp.zeros((8, LANES), F32)
            for j in reversed(range(T)):
                at = pl.ds(it * 8 * T + j, 8, stride=T)
                d, f = flow(1, g_ref[at, :], h_ref[at, :], val_ref[at, :])
                state = d * state + f
                sum_ref[ct, at, :] = sum_ref[ct, at, :] + (lefts[j] + state)
            right_ref[ct, pl.ds(it * 8, 8), :] = state
        return carry

    lax.fori_loop(0, groups, group, 0)


def finish_kernel(place_ref, rc_ref, rr_ref, cst_ref, px_ref, sum_ref, gate_ref, tok_ref, wo_ref,
                  out_ref, acc_ref, g_ref, enter_ref, gated_ref):
    groups = acc_ref.shape[0]
    px = px_ref[...]
    g_ref[...] = jnp.broadcast_to(px[:, 0:1], (PX, LANES))

    def enter(recv_ref, me, first):
        count = recv_ref.shape[0]
        for side in range(2):
            order = range(count) if side == 0 else reversed(range(count))
            whole = [cst_ref[pl.ds(12 + first + side, 1), ct * LANES:(ct + 1) * LANES]
                     for ct in range(groups)]
            state = [[jnp.zeros((8, LANES), F32) for _ in range(2)] for _ in range(groups)]
            for k in order:
                take = k < me if side == 0 else k > me
                block = recv_ref[k].astype(F32)
                tail = block[64:72]
                for it in range(2):
                    decay = tail[:, 64 * it:64 * it + 1] + tail[:, 64 * it + 32:64 * it + 33]
                    decay = jnp.broadcast_to(decay, (8, LANES))
                    for ct in range(groups):
                        at = ct * T + it * 8
                        new = (whole[ct] * decay) * state[ct][it] + block[at:at + 8]
                        state[ct][it] = jnp.where(take, new, state[ct][it])
            for ct in range(groups):
                for it in range(2):
                    enter_ref[first + side, ct, pl.ds(it * 8, 8), :] = state[ct][it]

    enter(rc_ref, place_ref[1], 0)
    enter(rr_ref, place_ref[0], 2)

    def group(ct, carry):
        lanes = pl.ds(pl.multiple_of(ct * LANES, LANES), LANES)
        base = [cst_ref[pl.ds(k, 1), lanes] for k in range(4)]
        for it in range(2):
            left = enter_ref[0, ct, pl.ds(it * 8, 8), :]
            right = enter_ref[1, ct, pl.ds(it * 8, 8), :]
            lefts = []
            for j in range(T):
                left = left * (base[0] * g_ref[pl.ds(it * 8 * T + j, 8, stride=T), :])
                lefts.append(left)
            for j in reversed(range(T)):
                at = pl.ds(it * 8 * T + j, 8, stride=T)
                right = right * (base[1] * g_ref[at, :])
                acc_ref[ct, at, :] = lefts[j] + right
        for jt in range(2):
            down = enter_ref[2, ct, pl.ds(jt * 8, 8), :]
            up = enter_ref[3, ct, pl.ds(jt * 8, 8), :]
            downs = []
            for i in range(T):
                down = down * (base[2] * g_ref[pl.ds(i * T + jt * 8, 8), :])
                downs.append(down)
            for i in reversed(range(T)):
                at = pl.ds(i * T + jt * 8, 8)
                up = up * (base[3] * g_ref[at, :])
                acc_ref[ct, at, :] = acc_ref[ct, at, :] + sum_ref[ct, at, :] + (downs[i] + up)
        gated_ref[:, lanes] = (acc_ref[ct] * gate_ref[:, lanes]).astype(BF16)
        return carry

    lax.fori_loop(0, groups, group, 0)
    mixed = jnp.dot(gated_ref[...], wo_ref[...], preferred_element_type=F32)
    out_ref[...] = (tok_ref[...].astype(F32) + mixed).astype(BF16)


def neighbours(x, axis, first, last):
    size = lax.axis_size(axis)
    up = [(i, i + 1) for i in range(size - 1)]
    down = [(i + 1, i) for i in range(size - 1)]
    return lax.ppermute(last, axis, up), lax.ppermute(first, axis, down)


def tail_block(product):
    high = product.astype(BF16)
    low = (product - high.astype(F32)).astype(BF16)
    parts = [jnp.broadcast_to(p[:, None], (8, 32))
             for p in (high[:8], low[:8], high[8:], low[8:])]
    return jnp.concatenate(parts, axis=1)


def exchange(former, latter, tail, axis):
    count = lax.axis_size(axis)
    peer = lax.broadcasted_iota(jnp.int32, (count, 1, 1), 0)
    states = jnp.where(peer > lax.axis_index(axis),
                       former.reshape(1, 64, LANES).astype(BF16), latter.reshape(1, 64, LANES).astype(BF16))
    tails = jnp.broadcast_to(tail[None], (count, 8, LANES))
    return lax.all_to_all(jnp.concatenate([states, tails], axis=1), axis, 0, 0, tiled=True)


def body(tokens, input_weight, kernel, direction_decay_table, pixel_extra_decay, output_weight):
    width = output_weight.shape[0]
    groups = width // LANES
    channels = tokens.shape[2]
    table, extra = direction_decay_table, pixel_extra_decay
    above, below = neighbours(tokens, "row", tokens[:3], tokens[T - 3:])
    tall = jnp.concatenate([above, tokens, below], axis=0)
    before, after = neighbours(tall, "col", tall[:, :3], tall[:, T - 3:])
    pad = jnp.concatenate([before, tall, after, jnp.zeros((T + 6, 2, channels), BF16)], axis=1)
    pad = pad.reshape((T + 6) * PW, channels)

    cst = jnp.concatenate([jnp.exp(-table), -jnp.expm1(-2.0 * table), jnp.exp(-2.0 * table),
                           jnp.exp(-float(T) * table)], axis=0)
    px = jnp.stack([jnp.exp(-extra), -jnp.expm1(-2.0 * extra)], axis=-1).reshape(PX, 2)
    flat = tokens.reshape(PX, channels)
    gate = jax.nn.silu(jnp.dot(flat, input_weight[:, width:], preferred_element_type=F32))

    spec = pl.BlockSpec(memory_space=VMEM)
    edge = jax.ShapeDtypeStruct((groups, T, LANES), F32)
    local, left, right, down, up = pl.pallas_call(
        conv_scan_kernel,
        out_shape=(jax.ShapeDtypeStruct((groups, PX, LANES), F32), edge, edge, edge, edge),
        in_specs=[spec] * 5,
        out_specs=(spec,) * 5,
        scratch_shapes=[VMEM((groups, (T + 6) * PW, LANES), F32), VMEM((PX, LANES), F32),
                        VMEM((PX, LANES), F32), VMEM((PX, LANES), F32)],
        compiler_params=pltpu.CompilerParams(vmem_limit_bytes=24 * 2**20),
        name="conv_scan",
    )(pad, input_weight[:, :width], kernel.reshape(49, width), cst, px)

    from_cols = exchange(left, right, tail_block(jnp.exp(-jnp.sum(extra, axis=1))), "col")
    from_rows = exchange(down, up, tail_block(jnp.exp(-jnp.sum(extra, axis=0))), "row")
    place = jnp.stack([lax.axis_index("row"), lax.axis_index("col")]).astype(jnp.int32)

    mixed = pl.pallas_call(
        finish_kernel,
        out_shape=jax.ShapeDtypeStruct((PX, channels), BF16),
        in_specs=[pl.BlockSpec(memory_space=pltpu.SMEM)] + [spec] * 8,
        out_specs=spec,
        scratch_shapes=[VMEM((groups, PX, LANES), F32), VMEM((PX, LANES), F32),
                        VMEM((4, groups, T, LANES), F32), VMEM((PX, width), BF16)],
        compiler_params=pltpu.CompilerParams(vmem_limit_bytes=24 * 2**20),
        name="finish",
    )(place, from_cols, from_rows, cst, px, local, gate, flat, output_weight)
    return mixed.reshape(T, T, channels)


def solution(mesh):
    return jax.shard_map(
        body,
        mesh=mesh,
        in_specs=(P("row", "col", None), P(), P(), P(), P("row", "col"), P()),
        out_specs=P("row", "col", None),
        check_vma=False,
    )
```

```python
import jax
import jax.numpy as jnp
from jax import lax
from jax.experimental import pallas as pl
from jax.experimental.pallas import tpu as pltpu
from jax.sharding import PartitionSpec as P

T = 16
PX = T * T
PW = 24
LANES = 128
XS = 4
FAR = 8
F32 = jnp.float32
BF16 = jnp.bfloat16
VMEM = pltpu.VMEM


def conv_scan_kernel(pad_ref, wv_ref, taps_ref, cst_ref, px_ref, tails_ref,
                     sum_ref, near_ref,
                     v_ref, g_ref, h_ref, val_ref, end_ref):
    groups = v_ref.shape[0]
    rows = T + 6
    pad = pad_ref[...]
    for half in range(groups // 2):
        p = jnp.dot(pad, wv_ref[:, half * 256:(half + 1) * 256], preferred_element_type=F32)
        p = p.astype(BF16).astype(F32)
        v_ref[2 * half] = p[:, :LANES]
        v_ref[2 * half + 1] = p[:, LANES:]
    px = px_ref[...]
    g_ref[...] = jnp.broadcast_to(px[:, 0:1], (PX, LANES))
    h_ref[...] = jnp.broadcast_to(px[:, 1:2], (PX, LANES))

    def group(ct, carry):
        lanes = pl.ds(pl.multiple_of(ct * LANES, LANES), LANES)
        cst = [cst_ref[pl.ds(k, 1), lanes] for k in range(12)]

        def flow(d, g, h, x):
            q = cst[4 + d] + cst[8 + d] * h
            return cst[d] * g, q * lax.rsqrt(q) * x

        for jt in range(2):
            acc = [jnp.zeros((8, LANES), F32) for _ in range(T)]
            for b in range(7):
                tap = [taps_ref[pl.ds(a * 7 + b, 1), lanes] for a in range(7)]
                tap = [jnp.broadcast_to(t, (8, LANES)) for t in tap]
                for r in range(rows):
                    x = v_ref[ct, pl.ds(r * PW + jt * 8 + b, 8), :]
                    for a in range(7):
                        i = r - a
                        if 0 <= i < T:
                            acc[i] = acc[i] + tap[a] * x
            vals = [x / (1.0 + jnp.exp(-x)) for x in acc]
            for i in range(T):
                val_ref[pl.ds(i * T + jt * 8, 8), :] = vals[i]
            state = jnp.zeros((8, LANES), F32)
            downs = []
            for i in range(T):
                at = pl.ds(i * T + jt * 8, 8)
                d, f = flow(2, g_ref[at, :], h_ref[at, :], vals[i])
                state = d * state + f
                downs.append(state)
            end_ref[1, pl.ds(0 + ct * T + jt * 8, 8), :] = state
            state = jnp.zeros((8, LANES), F32)
            for i in reversed(range(T)):
                at = pl.ds(i * T + jt * 8, 8)
                d, f = flow(3, g_ref[at, :], h_ref[at, :], vals[i])
                state = d * state + f
                sum_ref[ct, at, :] = downs[i] + state
            end_ref[1, pl.ds(64 + ct * T + jt * 8, 8), :] = state
        for it in range(2):
            state = jnp.zeros((8, LANES), F32)
            lefts = []
            for j in range(T):
                at = pl.ds(it * 8 * T + j, 8, stride=T)
                d, f = flow(0, g_ref[at, :], h_ref[at, :], val_ref[at, :])
                state = d * state + f
                lefts.append(state)
            end_ref[0, pl.ds(0 + ct * T + it * 8, 8), :] = state
            state = jnp.zeros((8, LANES), F32)
            for j in reversed(range(T)):
                at = pl.ds(it * 8 * T + j, 8, stride=T)
                d, f = flow(1, g_ref[at, :], h_ref[at, :], val_ref[at, :])
                state = d * state + f
                sum_ref[ct, at, :] = sum_ref[ct, at, :] + (lefts[j] + state)
            end_ref[0, pl.ds(64 + ct * T + it * 8, 8), :] = state
        return carry

    lax.fori_loop(0, groups, group, 0)
    for peer in range(2 * XS):
        near_ref[peer, 0:128] = end_ref[peer // XS].astype(BF16)
        near_ref[peer, 128:144] = tails_ref[peer // XS]


def line_decay(block, at):
    decay = jnp.broadcast_to(block[128:144, at:at + 1], (T, LANES))
    return jnp.concatenate([decay] * 4, axis=0)


def pair_decay(block, at, gap):
    return line_decay(block, at) + line_decay(block, at + gap)


def totals_kernel(place_ref, near_ref, whole_ref, far_ref):
    core, y = place_ref[0] % 2, place_ref[0] // 2
    x, z = place_ref[1] % XS, place_ref[1] // XS
    lane = lax.broadcasted_iota(jnp.int32, (T, LANES), 1)

    def spread(first, second):
        parts = []
        for d in (first, second):
            high = d[:T].astype(BF16).astype(F32)
            parts += [high, d[:T] - high]
        return jnp.where(lane < 32, parts[0], jnp.where(
            lane < 64, parts[1], jnp.where(lane < 96, parts[2], parts[3]))).astype(BF16)

    @pl.when(core == 0)
    def _():
        ahead, back = whole_ref[0], whole_ref[1]
        products = []
        for k in range(2):
            blocks = [near_ref[k * XS + i].astype(F32) for i in range(XS)]
            decays = [pair_decay(b, 0, 64) for b in blocks]
            former, product = blocks[0][:64], decays[0]
            for i in range(1, XS):
                former = ahead * decays[i] * former + blocks[i][:64]
                product = product * decays[i]
            latter = blocks[XS - 1][64:128]
            for i in reversed(range(XS - 1)):
                latter = back * decays[i] * latter + blocks[i][64:128]
            products.append(product)
            former, latter = former.astype(BF16), latter.astype(BF16)
            for peer in range(FAR):
                far_ref[peer, 64 * k:64 * k + 64] = jnp.where(peer > z, former, latter)
        tail = spread(products[0], products[1])
        for peer in range(FAR):
            far_ref[peer, 128:144] = tail

    @pl.when(core == 1)
    def _():
        first, second = near_ref[x].astype(F32), near_ref[XS + x].astype(F32)
        decays = [pair_decay(first, 0, 64), pair_decay(second, 0, 64)]
        former = (whole_ref[2] * decays[1] * first[:64] + second[:64]).astype(BF16)
        latter = (whole_ref[3] * decays[0] * second[64:128] + first[64:128]).astype(BF16)
        product = decays[0] * decays[1]
        tail = spread(product, product)
        for peer in range(FAR):
            far_ref[peer, 0:64] = jnp.where(peer > y, former, latter)
            far_ref[peer, 64:128] = jnp.zeros((64, LANES), BF16)
            far_ref[peer, 128:144] = tail


def enter_kernel(place_ref, near_ref, far_ref, whole_ref, keep_ref, give_ref):
    core, y = place_ref[0] % 2, place_ref[0] // 2
    x, z = place_ref[1] % XS, place_ref[1] // XS

    def far_states(me, k, ahead, back):
        blocks = [far_ref[i].astype(F32) for i in range(FAR)]
        decays = [pair_decay(b, 64 * k, 32) for b in blocks]
        fore = jnp.zeros((64, LANES), F32)
        aft = jnp.zeros((64, LANES), F32)
        for i in range(FAR - 1):
            fore = jnp.where(i < me, ahead * decays[i] * fore + blocks[i][64 * k:64 * k + 64], fore)
        for i in reversed(range(1, FAR)):
            aft = jnp.where(i > me, back * decays[i] * aft + blocks[i][64 * k:64 * k + 64], aft)
        return fore, aft

    @pl.when(core == 0)
    def _():
        ahead, back = whole_ref[0], whole_ref[1]
        ahead_far, back_far = ahead, back
        for _ in range(2):
            ahead_far, back_far = ahead_far * ahead_far, back_far * back_far
        for k in range(2):
            fore, aft = far_states(z, k, ahead_far, back_far)
            blocks = [near_ref[k * XS + i].astype(F32) for i in range(XS)]
            decays = [pair_decay(b, 0, 64) for b in blocks]
            for i in range(XS - 1):
                fore = jnp.where(i < x, ahead * decays[i] * fore + blocks[i][:64], fore)
            for i in reversed(range(1, XS)):
                aft = jnp.where(i > x, back * decays[i] * aft + blocks[i][64:128], aft)
            if k == 0:
                keep_ref[0:64], keep_ref[64:128] = fore, aft
            else:
                give_ref[0:64], give_ref[64:128] = fore.astype(BF16), aft.astype(BF16)

    @pl.when(core == 1)
    def _():
        ahead, back = whole_ref[2], whole_ref[3]
        fore, aft = far_states(y, 0, ahead * ahead, back * back)
        first, second = near_ref[x].astype(F32), near_ref[XS + x].astype(F32)
        give_ref[0:64] = fore.astype(BF16)
        give_ref[64:128] = (back * pair_decay(second, 0, 64) * aft + second[64:128]).astype(BF16)
        keep_ref[0:64] = ahead * pair_decay(first, 0, 64) * fore + first[:64]
        keep_ref[64:128] = aft


def finish_kernel(place_ref, keep_ref, got_ref, cst_ref, px_ref, sum_ref, gate_ref, tok_ref, wo_ref,
                  out_ref, acc_ref, g_ref, enter_ref, gated_ref):
    groups = acc_ref.shape[0]
    px = px_ref[...]
    g_ref[...] = jnp.broadcast_to(px[:, 0:1], (PX, LANES))
    first = place_ref[0] % 2 == 0
    keep, got = keep_ref[...], got_ref[...].astype(F32)
    enter_ref[0:128] = jnp.where(first, keep, got)
    enter_ref[128:256] = jnp.where(first, got, keep)

    def entering(d, ct, half):
        return enter_ref[pl.ds(64 * d + ct * T + half * 8, 8), :]

    def group(ct, carry):
        lanes = pl.ds(pl.multiple_of(ct * LANES, LANES), LANES)
        base = [cst_ref[pl.ds(k, 1), lanes] for k in range(4)]
        for it in range(2):
            left, right = entering(0, ct, it), entering(1, ct, it)
            lefts = []
            for j in range(T):
                left = left * (base[0] * g_ref[pl.ds(it * 8 * T + j, 8, stride=T), :])
                lefts.append(left)
            for j in reversed(range(T)):
                at = pl.ds(it * 8 * T + j, 8, stride=T)
                right = right * (base[1] * g_ref[at, :])
                acc_ref[ct, at, :] = lefts[j] + right
        for jt in range(2):
            down, up = entering(2, ct, jt), entering(3, ct, jt)
            downs = []
            for i in range(T):
                down = down * (base[2] * g_ref[pl.ds(i * T + jt * 8, 8), :])
                downs.append(down)
            for i in reversed(range(T)):
                at = pl.ds(i * T + jt * 8, 8)
                up = up * (base[3] * g_ref[at, :])
                acc_ref[ct, at, :] = acc_ref[ct, at, :] + sum_ref[ct, at, :] + (downs[i] + up)
        gated_ref[:, lanes] = (acc_ref[ct] * gate_ref[:, lanes]).astype(BF16)
        return carry

    lax.fori_loop(0, groups, group, 0)
    mixed = jnp.dot(gated_ref[...], wo_ref[...], preferred_element_type=F32)
    out_ref[...] = (tok_ref[...].astype(F32) + mixed).astype(BF16)


def neighbours(x_first, x_last, axis):
    size = lax.axis_size(axis)
    up = [(i, i + 1) for i in range(size - 1)]
    down = [(i + 1, i) for i in range(size - 1)]
    return lax.ppermute(x_last, axis, up), lax.ppermute(x_first, axis, down)


def tail_block(product):
    high = product.astype(BF16)
    low = (product - high.astype(F32)).astype(BF16)
    lane = lax.broadcasted_iota(jnp.int32, (T, LANES), 1)
    return jnp.where(lane < 64, high[:, None], low[:, None])


def near_groups(rows, cols):
    return [[(2 * y + k) * cols + XS * z + x for k in range(2) for x in range(XS)]
            for y in range(rows // 2) for z in range(cols // XS)]


def far_groups(rows, cols):
    along_z = [[2 * y * cols + XS * z + x for z in range(cols // XS)]
               for y in range(rows // 2) for x in range(XS)]
    along_y = [[(2 * y + 1) * cols + c for y in range(rows // 2)] for c in range(cols)]
    return along_z + along_y


def swap(x, groups):
    return lax.all_to_all(x, ("row", "col"), 0, 0, axis_index_groups=groups, tiled=True)


def body(tokens, input_weight, kernel, direction_decay_table, pixel_extra_decay, output_weight):
    width = output_weight.shape[0]
    groups = width // LANES
    channels = tokens.shape[2]
    rows, cols = lax.axis_size("row"), lax.axis_size("col")
    table, extra = direction_decay_table, pixel_extra_decay
    above, below = neighbours(tokens[:3], tokens[T - 3:], "row")

    def strip(at):
        return jnp.concatenate([above[:, at], tokens[:, at], below[:, at]], axis=0)

    before, after = neighbours(strip(slice(0, 3)), strip(slice(T - 3, T)), "col")
    pad = jnp.concatenate([before, strip(slice(None)), after,
                           jnp.zeros((T + 6, PW - T - 6, channels), BF16)], axis=1)
    pad = pad.reshape((T + 6) * PW, channels)

    cst = jnp.concatenate([jnp.exp(-table), -jnp.expm1(-2.0 * table), jnp.exp(-2.0 * table)], axis=0)
    whole = jnp.exp(-float(T) * table).reshape(4, groups, 1, LANES)
    whole = jnp.broadcast_to(whole, (4, groups, T, LANES)).reshape(4, groups * T, LANES)
    px = jnp.stack([jnp.exp(-extra), -jnp.expm1(-2.0 * extra)], axis=-1).reshape(PX, 2)
    tails = jnp.stack([tail_block(jnp.exp(-jnp.sum(extra, axis=1))),
                       tail_block(jnp.exp(-jnp.sum(extra, axis=0)))])
    place = jnp.stack([lax.axis_index("row"), lax.axis_index("col")]).astype(jnp.int32)
    flat = tokens.reshape(PX, channels)
    gate = jax.nn.silu(jnp.dot(flat, input_weight[:, width:], preferred_element_type=F32))
    pad, gate, whole, place = lax.optimization_barrier((pad, gate, whole, place))

    spec = pl.BlockSpec(memory_space=VMEM)
    smem = pl.BlockSpec(memory_space=pltpu.SMEM)
    params = pltpu.CompilerParams(vmem_limit_bytes=16 * 2**20)
    block = jax.ShapeDtypeStruct((2 * XS, 144, LANES), BF16)
    local, near = pl.pallas_call(
        conv_scan_kernel,
        out_shape=(jax.ShapeDtypeStruct((groups, PX, LANES), F32), block),
        in_specs=[spec] * 6,
        out_specs=(spec, spec),
        scratch_shapes=[VMEM((groups, (T + 6) * PW, LANES), F32), VMEM((PX, LANES), F32),
                        VMEM((PX, LANES), F32), VMEM((PX, LANES), F32), VMEM((2, 128, LANES), F32)],
        compiler_params=params,
        name="conv_scan",
    )(pad, input_weight[:, :width], kernel.reshape(49, width), cst, px, tails)
    near = swap(near, near_groups(rows, cols))

    far = pl.pallas_call(
        totals_kernel,
        out_shape=jax.ShapeDtypeStruct((FAR, 144, LANES), BF16),
        in_specs=[smem, spec, spec],
        out_specs=spec,
        compiler_params=params,
        name="totals",
    )(place, near, whole)
    far = swap(far, far_groups(rows, cols))

    keep, give = pl.pallas_call(
        enter_kernel,
        out_shape=(jax.ShapeDtypeStruct((128, LANES), F32), jax.ShapeDtypeStruct((128, LANES), BF16)),
        in_specs=[smem, spec, spec, spec],
        out_specs=(spec, spec),
        compiler_params=params,
        name="enter",
    )(place, near, far, whole)
    got = lax.ppermute(give, "row", [(i, i ^ 1) for i in range(rows)])

    mixed = pl.pallas_call(
        finish_kernel,
        out_shape=jax.ShapeDtypeStruct((PX, channels), BF16),
        in_specs=[smem] + [spec] * 8,
        out_specs=spec,
        scratch_shapes=[VMEM((groups, PX, LANES), F32), VMEM((PX, LANES), F32),
                        VMEM((256, LANES), F32), VMEM((PX, width), BF16)],
        compiler_params=params,
        name="finish",
    )(place, keep, got, cst, px, local, gate, flat, output_weight)
    return mixed.reshape(T, T, channels)


def solution(mesh):
    return jax.shard_map(
        body,
        mesh=mesh,
        in_specs=(P("row", "col", None), P(), P(), P(), P("row", "col"), P()),
        out_specs=P("row", "col", None),
        check_vma=False,
    )
```

```python
import jax
import jax.numpy as jnp
from jax import lax
from jax.experimental import pallas as pl
from jax.experimental.pallas import tpu as pltpu
from jax.sharding import PartitionSpec as P

T = 16
PX = T * T
PW = 24
LANES = 128
XS = 4
FAR = 8
F32 = jnp.float32
BF16 = jnp.bfloat16
VMEM = pltpu.VMEM


def project(x, wv_ref, store):
    for half in range(wv_ref.shape[1] // 256):
        p = jnp.dot(x, wv_ref[:, half * 256:(half + 1) * 256], preferred_element_type=F32)
        p = p.astype(BF16).astype(F32)
        store(2 * half, p[:, :LANES])
        store(2 * half + 1, p[:, LANES:])


def add_taps(acc, v_ref, taps_ref, ct, lanes, jt, shifts):
    for b in shifts:
        tap = [taps_ref[pl.ds(a * 7 + b, 1), lanes] for a in range(7)]
        tap = [jnp.broadcast_to(t, (8, LANES)) for t in tap]
        for r in range(T + 6):
            x = v_ref[ct, pl.ds(r * PW + jt * 8 + b, 8), :]
            for a in range(7):
                i = r - a
                if 0 <= i < T:
                    acc[i] = tap[a] * x if acc[i] is None else acc[i] + tap[a] * x
    return acc


def inner_kernel(above_ref, tok_ref, below_ref, wv_ref, taps_ref, v_ref, acc_ref):
    groups = v_ref.shape[0]
    for ref, first in ((above_ref, 0), (tok_ref, 3), (below_ref, T + 3)):
        count = ref.shape[0] // T

        def store(ct, p, first=first, count=count):
            for i in range(count):
                v_ref[ct, pl.ds((first + i) * PW + 3, T), :] = p[i * T:(i + 1) * T]

        project(ref[...], wv_ref, store)

    def group(ct, carry):
        lanes = pl.ds(pl.multiple_of(ct * LANES, LANES), LANES)
        for jt in range(2):
            acc = add_taps([None] * T, v_ref, taps_ref, ct, lanes, jt, range(3, 7) if jt == 0 else range(4))
            for i in range(T):
                acc_ref[ct, pl.ds(i * T + jt * 8, 8), :] = acc[i]
        return carry

    lax.fori_loop(0, groups, group, 0)


def conv_scan_kernel(before_ref, after_ref, wv_ref, taps_ref, cst_ref, px_ref, tails_ref, own_ref, acc_ref,
                     v_ref, sum_ref, near_ref, g_ref, h_ref, val_ref, end_ref):
    del own_ref
    groups = v_ref.shape[0]
    for ref, first in ((before_ref, 0), (after_ref, T + 3)):

        def store(ct, p, first=first):
            for j in range(3):
                v_ref[ct, pl.ds(first + j, PW, stride=PW), :] = p[j * PW:(j + 1) * PW]

        project(ref[...], wv_ref, store)
    px = px_ref[...]
    g_ref[...] = jnp.broadcast_to(px[:, 0:1], (PX, LANES))
    h_ref[...] = jnp.broadcast_to(px[:, 1:2], (PX, LANES))

    def group(ct, carry):
        lanes = pl.ds(pl.multiple_of(ct * LANES, LANES), LANES)
        cst = [cst_ref[pl.ds(k, 1), lanes] for k in range(12)]

        def flow(d, g, h, x):
            q = cst[4 + d] + cst[8 + d] * h
            return cst[d] * g, q * lax.rsqrt(q) * x

        for jt in range(2):
            acc = [acc_ref[ct, pl.ds(i * T + jt * 8, 8), :] for i in range(T)]
            acc = add_taps(acc, v_ref, taps_ref, ct, lanes, jt, range(3) if jt == 0 else range(4, 7))
            vals = [x / (1.0 + jnp.exp(-x)) for x in acc]
            for i in range(T):
                val_ref[pl.ds(i * T + jt * 8, 8), :] = vals[i]
            state = jnp.zeros((8, LANES), F32)
            downs = []
            for i in range(T):
                at = pl.ds(i * T + jt * 8, 8)
                d, f = flow(2, g_ref[at, :], h_ref[at, :], vals[i])
                state = d * state + f
                downs.append(state)
            end_ref[1, pl.ds(0 + ct * T + jt * 8, 8), :] = state
            state = jnp.zeros((8, LANES), F32)
            for i in reversed(range(T)):
                at = pl.ds(i * T + jt * 8, 8)
                d, f = flow(3, g_ref[at, :], h_ref[at, :], vals[i])
                state = d * state + f
                sum_ref[ct, at, :] = downs[i] + state
            end_ref[1, pl.ds(64 + ct * T + jt * 8, 8), :] = state
        for it in range(2):
            state = jnp.zeros((8, LANES), F32)
            lefts = []
            for j in range(T):
                at = pl.ds(it * 8 * T + j, 8, stride=T)
                d, f = flow(0, g_ref[at, :], h_ref[at, :], val_ref[at, :])
                state = d * state + f
                lefts.append(state)
            end_ref[0, pl.ds(0 + ct * T + it * 8, 8), :] = state
            state = jnp.zeros((8, LANES), F32)
            for j in reversed(range(T)):
                at = pl.ds(it * 8 * T + j, 8, stride=T)
                d, f = flow(1, g_ref[at, :], h_ref[at, :], val_ref[at, :])
                state = d * state + f
                sum_ref[ct, at, :] = sum_ref[ct, at, :] + (lefts[j] + state)
            end_ref[0, pl.ds(64 + ct * T + it * 8, 8), :] = state
        return carry

    lax.fori_loop(0, groups, group, 0)
    for peer in range(2 * XS):
        near_ref[peer, 0:128] = end_ref[peer // XS].astype(BF16)
        near_ref[peer, 128:144] = tails_ref[peer // XS]


def line_decay(block, at):
    decay = jnp.broadcast_to(block[128:144, at:at + 1], (T, LANES))
    return jnp.concatenate([decay] * 4, axis=0)


def pair_decay(block, at, gap):
    return line_decay(block, at) + line_decay(block, at + gap)


def totals_kernel(place_ref, near_ref, whole_ref, far_ref):
    core, y = place_ref[0] % 2, place_ref[0] // 2
    x, z = place_ref[1] % XS, place_ref[1] // XS
    lane = lax.broadcasted_iota(jnp.int32, (T, LANES), 1)

    def spread(first, second):
        parts = []
        for d in (first, second):
            high = d[:T].astype(BF16).astype(F32)
            parts += [high, d[:T] - high]
        return jnp.where(lane < 32, parts[0], jnp.where(
            lane < 64, parts[1], jnp.where(lane < 96, parts[2], parts[3]))).astype(BF16)

    @pl.when(core == 0)
    def _():
        ahead, back = whole_ref[0], whole_ref[1]
        products = []
        for k in range(2):
            blocks = [near_ref[k * XS + i].astype(F32) for i in range(XS)]
            decays = [pair_decay(b, 0, 64) for b in blocks]
            former, product = blocks[0][:64], decays[0]
            for i in range(1, XS):
                former = ahead * decays[i] * former + blocks[i][:64]
                product = product * decays[i]
            latter = blocks[XS - 1][64:128]
            for i in reversed(range(XS - 1)):
                latter = back * decays[i] * latter + blocks[i][64:128]
            products.append(product)
            former, latter = former.astype(BF16), latter.astype(BF16)
            for peer in range(FAR):
                far_ref[peer, 64 * k:64 * k + 64] = jnp.where(peer > z, former, latter)
        tail = spread(products[0], products[1])
        for peer in range(FAR):
            far_ref[peer, 128:144] = tail

    @pl.when(core == 1)
    def _():
        first, second = near_ref[x].astype(F32), near_ref[XS + x].astype(F32)
        decays = [pair_decay(first, 0, 64), pair_decay(second, 0, 64)]
        former = (whole_ref[2] * decays[1] * first[:64] + second[:64]).astype(BF16)
        latter = (whole_ref[3] * decays[0] * second[64:128] + first[64:128]).astype(BF16)
        product = decays[0] * decays[1]
        tail = spread(product, product)
        for peer in range(FAR):
            far_ref[peer, 0:64] = jnp.where(peer > y, former, latter)
            far_ref[peer, 64:128] = jnp.zeros((64, LANES), BF16)
            far_ref[peer, 128:144] = tail


def enter_kernel(place_ref, near_ref, far_ref, whole_ref, keep_ref, give_ref):
    core, y = place_ref[0] % 2, place_ref[0] // 2
    x, z = place_ref[1] % XS, place_ref[1] // XS

    def far_states(me, k, ahead, back):
        blocks = [far_ref[i].astype(F32) for i in range(FAR)]
        decays = [pair_decay(b, 64 * k, 32) for b in blocks]
        fore = jnp.zeros((64, LANES), F32)
        aft = jnp.zeros((64, LANES), F32)
        for i in range(FAR - 1):
            fore = jnp.where(i < me, ahead * decays[i] * fore + blocks[i][64 * k:64 * k + 64], fore)
        for i in reversed(range(1, FAR)):
            aft = jnp.where(i > me, back * decays[i] * aft + blocks[i][64 * k:64 * k + 64], aft)
        return fore, aft

    @pl.when(core == 0)
    def _():
        ahead, back = whole_ref[0], whole_ref[1]
        ahead_far, back_far = ahead, back
        for _ in range(2):
            ahead_far, back_far = ahead_far * ahead_far, back_far * back_far
        for k in range(2):
            fore, aft = far_states(z, k, ahead_far, back_far)
            blocks = [near_ref[k * XS + i].astype(F32) for i in range(XS)]
            decays = [pair_decay(b, 0, 64) for b in blocks]
            for i in range(XS - 1):
                fore = jnp.where(i < x, ahead * decays[i] * fore + blocks[i][:64], fore)
            for i in reversed(range(1, XS)):
                aft = jnp.where(i > x, back * decays[i] * aft + blocks[i][64:128], aft)
            if k == 0:
                keep_ref[0:64], keep_ref[64:128] = fore, aft
            else:
                give_ref[0:64], give_ref[64:128] = fore.astype(BF16), aft.astype(BF16)

    @pl.when(core == 1)
    def _():
        ahead, back = whole_ref[2], whole_ref[3]
        fore, aft = far_states(y, 0, ahead * ahead, back * back)
        first, second = near_ref[x].astype(F32), near_ref[XS + x].astype(F32)
        give_ref[0:64] = fore.astype(BF16)
        give_ref[64:128] = (back * pair_decay(second, 0, 64) * aft + second[64:128]).astype(BF16)
        keep_ref[0:64] = ahead * pair_decay(first, 0, 64) * fore + first[:64]
        keep_ref[64:128] = aft


def decay_rows(kind, first, cst_ref, g_ref, store):
    def group(ct, carry):
        lanes = pl.ds(pl.multiple_of(ct * LANES, LANES), LANES)
        ahead, back = cst_ref[pl.ds(2 * kind, 1), lanes], cst_ref[pl.ds(2 * kind + 1, 1), lanes]
        for half in range(2):
            fore = first(0, ct, half)
            aft = first(1, ct, half)

            def at(n):
                return pl.ds(half * 8 * T + n, 8, stride=T) if kind == 0 else pl.ds(n * T + half * 8, 8)

            fores = []
            for n in range(T):
                fore = fore * (ahead * g_ref[at(n), :])
                fores.append(fore)
            for n in reversed(range(T)):
                aft = aft * (back * g_ref[at(n), :])
                store(ct, at(n), fores[n] + aft)
        return carry

    lax.fori_loop(0, 4, group, 0)


def own_axis_kernel(place_ref, keep_ref, cst_ref, px_ref, sum_ref, acc_ref, g_ref):
    px = px_ref[...]
    g_ref[...] = jnp.broadcast_to(px[:, 0:1], (PX, LANES))

    def first(side, ct, half):
        return keep_ref[pl.ds(64 * side + ct * T + half * 8, 8), :]

    def store(ct, at, x):
        acc_ref[ct, at, :] = sum_ref[ct, at, :] + x

    for kind in range(2):
        @pl.when(place_ref[0] % 2 == kind)
        def _():
            decay_rows(kind, first, cst_ref, g_ref, store)


def finish_kernel(place_ref, got_ref, cst_ref, px_ref, sum_ref, gate_ref, tok_ref, wo_ref,
                  out_ref, acc_ref, g_ref, enter_ref, gated_ref):
    groups = acc_ref.shape[0]
    px = px_ref[...]
    g_ref[...] = jnp.broadcast_to(px[:, 0:1], (PX, LANES))
    enter_ref[...] = got_ref[...].astype(F32)

    def first(side, ct, half):
        return enter_ref[pl.ds(64 * side + ct * T + half * 8, 8), :]

    def store(ct, at, x):
        acc_ref[ct, at, :] = sum_ref[ct, at, :] + x

    for kind in range(2):
        @pl.when(place_ref[0] % 2 != kind)
        def _():
            decay_rows(kind, first, cst_ref, g_ref, store)

    for ct in range(groups):
        lanes = slice(ct * LANES, (ct + 1) * LANES)
        gated_ref[:, lanes] = (acc_ref[ct] * gate_ref[:, lanes]).astype(BF16)
    mixed = jnp.dot(gated_ref[...], wo_ref[...], preferred_element_type=F32)
    out_ref[...] = (tok_ref[...].astype(F32) + mixed).astype(BF16)


def neighbours(x_first, x_last, axis):
    size = lax.axis_size(axis)
    up = [(i, i + 1) for i in range(size - 1)]
    down = [(i + 1, i) for i in range(size - 1)]
    return lax.ppermute(x_last, axis, up), lax.ppermute(x_first, axis, down)


def tail_block(product):
    high = product.astype(BF16)
    low = (product - high.astype(F32)).astype(BF16)
    lane = lax.broadcasted_iota(jnp.int32, (T, LANES), 1)
    return jnp.where(lane < 64, high[:, None], low[:, None])


def near_groups(rows, cols):
    return [[(2 * y + k) * cols + XS * z + x for k in range(2) for x in range(XS)]
            for y in range(rows // 2) for z in range(cols // XS)]


def far_groups(rows, cols):
    along_z = [[2 * y * cols + XS * z + x for z in range(cols // XS)]
               for y in range(rows // 2) for x in range(XS)]
    along_y = [[(2 * y + 1) * cols + c for y in range(rows // 2)] for c in range(cols)]
    return along_z + along_y


def swap(x, groups):
    return lax.all_to_all(x, ("row", "col"), 0, 0, axis_index_groups=groups, tiled=True)


def body(tokens, input_weight, kernel, direction_decay_table, pixel_extra_decay, output_weight):
    width = output_weight.shape[0]
    groups = width // LANES
    channels = tokens.shape[2]
    rows, cols = lax.axis_size("row"), lax.axis_size("col")
    table, extra = direction_decay_table, pixel_extra_decay
    above, below = neighbours(tokens[:3], tokens[T - 3:], "row")

    def strip(at):
        x = jnp.concatenate([above[:, at], tokens[:, at], below[:, at],
                             jnp.zeros((PW - T - 6, 3, channels), BF16)], axis=0)
        return x.transpose(1, 0, 2).reshape(3 * PW, channels)

    before, after = neighbours(strip(slice(0, 3)), strip(slice(T - 3, T)), "col")

    cst = jnp.concatenate([jnp.exp(-table), -jnp.expm1(-2.0 * table), jnp.exp(-2.0 * table)], axis=0)
    whole = jnp.exp(-float(T) * table).reshape(4, groups, 1, LANES)
    whole = jnp.broadcast_to(whole, (4, groups, T, LANES)).reshape(4, groups * T, LANES)
    px = jnp.stack([jnp.exp(-extra), -jnp.expm1(-2.0 * extra)], axis=-1).reshape(PX, 2)
    tails = jnp.stack([tail_block(jnp.exp(-jnp.sum(extra, axis=1))),
                       tail_block(jnp.exp(-jnp.sum(extra, axis=0)))])
    place = jnp.stack([lax.axis_index("row"), lax.axis_index("col")]).astype(jnp.int32)
    flat = tokens.reshape(PX, channels)
    gate = jax.nn.silu(jnp.dot(flat, input_weight[:, width:], preferred_element_type=F32))
    before, gate, whole, place = lax.optimization_barrier((before, gate, whole, place))
    values_weight, taps = input_weight[:, :width], kernel.reshape(49, width)

    spec = pl.BlockSpec(memory_space=VMEM)
    smem = pl.BlockSpec(memory_space=pltpu.SMEM)
    params = pltpu.CompilerParams(vmem_limit_bytes=16 * 2**20)
    tile = jax.ShapeDtypeStruct((groups, PX, LANES), F32)
    padded = jax.ShapeDtypeStruct((groups, PW * PW, LANES), F32)
    own, partial = pl.pallas_call(
        inner_kernel,
        out_shape=(padded, tile),
        in_specs=[spec] * 5,
        out_specs=(spec, spec),
        compiler_params=params,
        cost_estimate=pl.CostEstimate(flops=2 * 352 * channels * width, bytes_accessed=4 * 2**20, transcendentals=0),
        name="inner",
    )(above.reshape(3 * T, channels), flat, below.reshape(3 * T, channels), values_weight, taps)
    _, local, near = pl.pallas_call(
        conv_scan_kernel,
        out_shape=(padded, tile, jax.ShapeDtypeStruct((2 * XS, 144, LANES), BF16)),
        in_specs=[spec] * 9,
        out_specs=(spec, spec, spec),
        scratch_shapes=[VMEM((PX, LANES), F32), VMEM((PX, LANES), F32), VMEM((PX, LANES), F32),
                        VMEM((2, 128, LANES), F32)],
        input_output_aliases={7: 0},
        compiler_params=params,
        name="conv_scan",
    )(before, after, values_weight, taps, cst, px, tails, own, partial)
    near = swap(near, near_groups(rows, cols))

    far = pl.pallas_call(
        totals_kernel,
        out_shape=jax.ShapeDtypeStruct((FAR, 144, LANES), BF16),
        in_specs=[smem, spec, spec],
        out_specs=spec,
        compiler_params=params,
        name="totals",
    )(place, near, whole)
    far = swap(far, far_groups(rows, cols))

    keep, give = pl.pallas_call(
        enter_kernel,
        out_shape=(jax.ShapeDtypeStruct((128, LANES), F32), jax.ShapeDtypeStruct((128, LANES), BF16)),
        in_specs=[smem, spec, spec, spec],
        out_specs=(spec, spec),
        compiler_params=params,
        name="enter",
    )(place, near, far, whole)
    got = lax.ppermute(give, "row", [(i, i ^ 1) for i in range(rows)])

    acc = pl.pallas_call(
        own_axis_kernel,
        out_shape=tile,
        in_specs=[smem] + [spec] * 4,
        out_specs=spec,
        scratch_shapes=[VMEM((PX, LANES), F32)],
        compiler_params=params,
        cost_estimate=pl.CostEstimate(flops=6 * PX * width, bytes_accessed=2 * 2**20, transcendentals=0),
        name="own_axis",
    )(place, keep, cst, px, local)
    mixed = pl.pallas_call(
        finish_kernel,
        out_shape=jax.ShapeDtypeStruct((PX, channels), BF16),
        in_specs=[smem] + [spec] * 7,
        out_specs=spec,
        scratch_shapes=[VMEM((groups, PX, LANES), F32), VMEM((PX, LANES), F32),
                        VMEM((128, LANES), F32), VMEM((PX, width), BF16)],
        compiler_params=params,
        name="finish",
    )(place, got, cst, px, acc, gate, flat, output_weight)
    return mixed.reshape(T, T, channels)


def solution(mesh):
    return jax.shard_map(
        body,
        mesh=mesh,
        in_specs=(P("row", "col", None), P(), P(), P(), P("row", "col"), P()),
        out_specs=P("row", "col", None),
        check_vma=False,
    )
```

```python
import jax
import jax.numpy as jnp
from jax import lax
from jax.experimental import pallas as pl
from jax.experimental.pallas import tpu as pltpu
from jax.sharding import PartitionSpec as P

T = 16
PX = T * T
PW = 24
LANES = 128
XS = 4
FAR = 8
F32 = jnp.float32
BF16 = jnp.bfloat16
VMEM = pltpu.VMEM


def position():
    row, col = lax.axis_index("row"), lax.axis_index("col")
    return row % 2, row // 2, col % XS, col // XS


def project(x, wv_ref, store):
    for half in range(wv_ref.shape[1] // 512):
        p = jnp.dot(x, wv_ref[:, half * 256:(half + 1) * 256], preferred_element_type=F32)
        p = p.astype(BF16).astype(F32)
        store(2 * half, p[:, :LANES])
        store(2 * half + 1, p[:, LANES:])


def add_taps(acc, v_ref, taps_ref, ct, lanes, jt, shifts):
    for b in shifts:
        tap = [taps_ref[a, pl.ds(b, 1), lanes] for a in range(7)]
        tap = [jnp.broadcast_to(t, (8, LANES)) for t in tap]
        for r in range(T + 6):
            x = v_ref[ct, pl.ds(r * PW + jt * 8 + b, 8), :]
            for a in range(7):
                i = r - a
                if 0 <= i < T:
                    acc[i] = tap[a] * x if acc[i] is None else acc[i] + tap[a] * x
    return acc


def inner_kernel(above_ref, tok_ref, below_ref, wv_ref, taps_ref, px_ref, v_ref, acc_ref, g_ref, h_ref):
    groups = v_ref.shape[0]
    px = px_ref[...]
    g_ref[...] = jnp.broadcast_to(px[:, 0:1], (PX, LANES))
    h_ref[...] = jnp.broadcast_to(px[:, 1:2], (PX, LANES))
    for ref, first in ((above_ref, 0), (tok_ref, 3), (below_ref, T + 3)):
        count = ref.shape[0] // T

        def store(ct, p, first=first, count=count):
            for i in range(count):
                v_ref[ct, pl.ds((first + i) * PW + 3, T), :] = p[i * T:(i + 1) * T]

        project(ref[...], wv_ref, store)

    def group(ct, carry):
        lanes = pl.ds(pl.multiple_of(ct * LANES, LANES), LANES)
        for jt in range(2):
            acc = add_taps([None] * T, v_ref, taps_ref, ct, lanes, jt, range(3, 7) if jt == 0 else range(4))
            for i in range(T):
                acc_ref[ct, pl.ds(i * T + jt * 8, 8), :] = acc[i]
        return carry

    lax.fori_loop(0, groups, group, 0)


def conv_scan_kernel(before_ref, after_ref, wv_ref, taps_ref, cst_ref, g_ref, h_ref, tails_ref, own_ref, acc_ref,
                     v_ref, sum_ref, near_ref, side_ref, val_ref, end_ref):
    del own_ref
    groups = v_ref.shape[0]
    side_ref[0:3 * PW] = before_ref[...].astype(F32)
    side_ref[3 * PW:] = after_ref[...].astype(F32)

    def store(ct, p):
        for j in range(6):
            at = j if j < 3 else T + j
            v_ref[ct, pl.ds(at, PW, stride=PW), :] = p[j * PW:(j + 1) * PW]

    project(side_ref[...].astype(BF16), wv_ref, store)

    def group(ct, carry):
        lanes = pl.ds(pl.multiple_of(ct * LANES, LANES), LANES)
        cst = [cst_ref[pl.ds(k, 1), lanes] for k in range(12)]

        def flow(d, g, h, x):
            q = cst[4 + d] + cst[8 + d] * h
            return cst[d] * g, q * lax.rsqrt(q) * x

        for jt in range(2):
            acc = [acc_ref[ct, pl.ds(i * T + jt * 8, 8), :] for i in range(T)]
            acc = add_taps(acc, v_ref, taps_ref, ct, lanes, jt, range(3) if jt == 0 else range(4, 7))
            vals = [x / (1.0 + jnp.exp(-x)) for x in acc]
            for i in range(T):
                val_ref[pl.ds(i * T + jt * 8, 8), :] = vals[i]
            state = jnp.zeros((8, LANES), F32)
            downs = []
            for i in range(T):
                at = pl.ds(i * T + jt * 8, 8)
                d, f = flow(2, g_ref[at, :], h_ref[at, :], vals[i])
                state = d * state + f
                downs.append(state)
            end_ref[1, pl.ds(0 + ct * T + jt * 8, 8), :] = state
            state = jnp.zeros((8, LANES), F32)
            for i in reversed(range(T)):
                at = pl.ds(i * T + jt * 8, 8)
                d, f = flow(3, g_ref[at, :], h_ref[at, :], vals[i])
                state = d * state + f
                sum_ref[ct, at, :] = downs[i] + state
            end_ref[1, pl.ds(64 + ct * T + jt * 8, 8), :] = state
        for it in range(2):
            state = jnp.zeros((8, LANES), F32)
            lefts = []
            for j in range(T):
                at = pl.ds(it * 8 * T + j, 8, stride=T)
                d, f = flow(0, g_ref[at, :], h_ref[at, :], val_ref[at, :])
                state = d * state + f
                lefts.append(state)
            end_ref[0, pl.ds(0 + ct * T + it * 8, 8), :] = state
            state = jnp.zeros((8, LANES), F32)
            for j in reversed(range(T)):
                at = pl.ds(it * 8 * T + j, 8, stride=T)
                d, f = flow(1, g_ref[at, :], h_ref[at, :], val_ref[at, :])
                state = d * state + f
                sum_ref[ct, at, :] = sum_ref[ct, at, :] + (lefts[j] + state)
            end_ref[0, pl.ds(64 + ct * T + it * 8, 8), :] = state
        return carry

    lax.fori_loop(0, groups, group, 0)
    for peer in range(2 * XS):
        near_ref[peer, 0:128] = end_ref[peer // XS].astype(BF16)
        near_ref[peer, 128:144] = tails_ref[peer // XS]


def line_decay(block, at):
    decay = jnp.broadcast_to(block[128:144, at:at + 1], (T, LANES))
    return jnp.concatenate([decay] * 4, axis=0)


def pair_decay(block, at, gap):
    return line_decay(block, at) + line_decay(block, at + gap)


def totals_kernel(near_ref, whole_ref, far_ref):
    core, y, x, z = position()
    lane = lax.broadcasted_iota(jnp.int32, (T, LANES), 1)

    def spread(first, second):
        parts = []
        for d in (first, second):
            high = d[:T].astype(BF16).astype(F32)
            parts += [high, d[:T] - high]
        return jnp.where(lane < 32, parts[0], jnp.where(
            lane < 64, parts[1], jnp.where(lane < 96, parts[2], parts[3]))).astype(BF16)

    @pl.when(core == 0)
    def _():
        ahead, back = whole_ref[0], whole_ref[1]
        products = []
        for k in range(2):
            blocks = [near_ref[k * XS + i].astype(F32) for i in range(XS)]
            decays = [pair_decay(b, 0, 64) for b in blocks]
            former, product = blocks[0][:64], decays[0]
            for i in range(1, XS):
                former = ahead * decays[i] * former + blocks[i][:64]
                product = product * decays[i]
            latter = blocks[XS - 1][64:128]
            for i in reversed(range(XS - 1)):
                latter = back * decays[i] * latter + blocks[i][64:128]
            products.append(product)
            former, latter = former.astype(BF16), latter.astype(BF16)
            for peer in range(FAR):
                far_ref[peer, 64 * k:64 * k + 64] = jnp.where(peer > z, former, latter)
        tail = spread(products[0], products[1])
        for peer in range(FAR):
            far_ref[peer, 128:144] = tail

    @pl.when(core == 1)
    def _():
        first, second = near_ref[x].astype(F32), near_ref[XS + x].astype(F32)
        decays = [pair_decay(first, 0, 64), pair_decay(second, 0, 64)]
        former = (whole_ref[2] * decays[1] * first[:64] + second[:64]).astype(BF16)
        latter = (whole_ref[3] * decays[0] * second[64:128] + first[64:128]).astype(BF16)
        product = decays[0] * decays[1]
        tail = spread(product, product)
        for peer in range(FAR):
            far_ref[peer, 0:64] = jnp.where(peer > y, former, latter)
            far_ref[peer, 64:128] = jnp.zeros((64, LANES), BF16)
            far_ref[peer, 128:144] = tail


def enter_kernel(near_ref, far_ref, whole_ref, keep_ref, give_ref):
    core, y, x, z = position()

    def far_states(me, k, ahead, back):
        blocks = [far_ref[i].astype(F32) for i in range(FAR)]
        decays = [pair_decay(b, 64 * k, 32) for b in blocks]
        fore = jnp.zeros((64, LANES), F32)
        aft = jnp.zeros((64, LANES), F32)
        for i in range(FAR - 1):
            fore = jnp.where(i < me, ahead * decays[i] * fore + blocks[i][64 * k:64 * k + 64], fore)
        for i in reversed(range(1, FAR)):
            aft = jnp.where(i > me, back * decays[i] * aft + blocks[i][64 * k:64 * k + 64], aft)
        return fore, aft

    @pl.when(core == 0)
    def _():
        ahead, back = whole_ref[0], whole_ref[1]
        ahead_far, back_far = ahead, back
        for _ in range(2):
            ahead_far, back_far = ahead_far * ahead_far, back_far * back_far
        for k in range(2):
            fore, aft = far_states(z, k, ahead_far, back_far)
            blocks = [near_ref[k * XS + i].astype(F32) for i in range(XS)]
            decays = [pair_decay(b, 0, 64) for b in blocks]
            for i in range(XS - 1):
                fore = jnp.where(i < x, ahead * decays[i] * fore + blocks[i][:64], fore)
            for i in reversed(range(1, XS)):
                aft = jnp.where(i > x, back * decays[i] * aft + blocks[i][64:128], aft)
            if k == 0:
                keep_ref[0:64], keep_ref[64:128] = fore, aft
            else:
                give_ref[0:64], give_ref[64:128] = fore.astype(BF16), aft.astype(BF16)

    @pl.when(core == 1)
    def _():
        ahead, back = whole_ref[2], whole_ref[3]
        fore, aft = far_states(y, 0, ahead * ahead, back * back)
        first, second = near_ref[x].astype(F32), near_ref[XS + x].astype(F32)
        give_ref[0:64] = fore.astype(BF16)
        give_ref[64:128] = (back * pair_decay(second, 0, 64) * aft + second[64:128]).astype(BF16)
        keep_ref[0:64] = ahead * pair_decay(first, 0, 64) * fore + first[:64]
        keep_ref[64:128] = aft


def decay_rows(kind, first, cst_ref, g_ref, store):
    def group(ct, carry):
        lanes = pl.ds(pl.multiple_of(ct * LANES, LANES), LANES)
        ahead, back = cst_ref[pl.ds(2 * kind, 1), lanes], cst_ref[pl.ds(2 * kind + 1, 1), lanes]
        for half in range(2):
            fore = first(0, ct, half)
            aft = first(1, ct, half)

            def at(n):
                return pl.ds(half * 8 * T + n, 8, stride=T) if kind == 0 else pl.ds(n * T + half * 8, 8)

            fores = []
            for n in range(T):
                fore = fore * (ahead * g_ref[at(n), :])
                fores.append(fore)
            for n in reversed(range(T)):
                aft = aft * (back * g_ref[at(n), :])
                store(ct, at(n), fores[n] + aft)
        return carry

    lax.fori_loop(0, 4, group, 0)


def own_axis_kernel(keep_ref, cst_ref, g_ref, sum_ref, acc_ref):
    def first(side, ct, half):
        return keep_ref[pl.ds(64 * side + ct * T + half * 8, 8), :]

    def store(ct, at, x):
        acc_ref[ct, at, :] = sum_ref[ct, at, :] + x

    for kind in range(2):
        @pl.when(position()[0] == kind)
        def _():
            decay_rows(kind, first, cst_ref, g_ref, store)


def finish_kernel(got_ref, cst_ref, g_ref, sum_ref, gate_ref, tok_ref, wo_ref,
                  out_ref, acc_ref, enter_ref, gated_ref):
    groups = acc_ref.shape[0]
    enter_ref[...] = got_ref[...].astype(F32)

    def first(side, ct, half):
        return enter_ref[pl.ds(64 * side + ct * T + half * 8, 8), :]

    def store(ct, at, x):
        acc_ref[ct, at, :] = sum_ref[ct, at, :] + x

    for kind in range(2):
        @pl.when(position()[0] != kind)
        def _():
            decay_rows(kind, first, cst_ref, g_ref, store)

    for ct in range(groups):
        lanes = slice(ct * LANES, (ct + 1) * LANES)
        gated_ref[:, lanes] = (acc_ref[ct] * gate_ref[:, lanes]).astype(BF16)
    mixed = jnp.dot(gated_ref[...], wo_ref[...], preferred_element_type=F32)
    out_ref[...] = (tok_ref[...].astype(F32) + mixed).astype(BF16)


def neighbours(x_first, x_last, axis):
    size = lax.axis_size(axis)
    up = [(i, i + 1) for i in range(size - 1)]
    down = [(i + 1, i) for i in range(size - 1)]
    return lax.ppermute(x_last, axis, up), lax.ppermute(x_first, axis, down)


def tail_block(product):
    high = product.astype(BF16)
    low = (product - high.astype(F32)).astype(BF16)
    lane = lax.broadcasted_iota(jnp.int32, (T, LANES), 1)
    return jnp.where(lane < 64, high[:, None], low[:, None])


def near_groups(rows, cols):
    return [[(2 * y + k) * cols + XS * z + x for k in range(2) for x in range(XS)]
            for y in range(rows // 2) for z in range(cols // XS)]


def far_groups(rows, cols):
    along_z = [[2 * y * cols + XS * z + x for z in range(cols // XS)]
               for y in range(rows // 2) for x in range(XS)]
    along_y = [[(2 * y + 1) * cols + c for y in range(rows // 2)] for c in range(cols)]
    return along_z + along_y


def swap(x, groups):
    return lax.all_to_all(x, ("row", "col"), 0, 0, axis_index_groups=groups, tiled=True)


def body(tokens, input_weight, kernel, direction_decay_table, pixel_extra_decay, output_weight):
    width = output_weight.shape[0]
    groups = width // LANES
    channels = tokens.shape[2]
    rows, cols = lax.axis_size("row"), lax.axis_size("col")
    table, extra = direction_decay_table, pixel_extra_decay
    above, below = neighbours(tokens[:3], tokens[T - 3:], "row")

    def strip(at):
        x = jnp.concatenate([above[:, at], tokens[:, at], below[:, at],
                             jnp.zeros((PW - T - 6, 3, channels), BF16)], axis=0)
        return x.transpose(1, 0, 2).reshape(3 * PW, channels)

    first, last = strip(slice(0, 3)), strip(slice(T - 3, T))
    px = jnp.stack([jnp.exp(-extra), -jnp.expm1(-2.0 * extra)], axis=-1).reshape(PX, 2)
    tails = jnp.stack([tail_block(jnp.exp(-jnp.sum(extra, axis=1))),
                       tail_block(jnp.exp(-jnp.sum(extra, axis=0)))])
    first, last, table, later_weight, px, tails = lax.optimization_barrier(
        (first, last, table, input_weight, px, tails))
    before, after = neighbours(first, last, "col")

    cst = jnp.concatenate([jnp.exp(-table), -jnp.expm1(-2.0 * table), jnp.exp(-2.0 * table)], axis=0)
    whole = jnp.exp(-float(T) * table).reshape(4, groups, 1, LANES)
    whole = jnp.broadcast_to(whole, (4, groups, T, LANES)).reshape(4, groups * T, LANES)
    flat = tokens.reshape(PX, channels)
    gate = jax.nn.silu(jnp.dot(flat, later_weight[:, width:], preferred_element_type=F32))
    before, after, gate, whole, cst = lax.optimization_barrier((before, after, gate, whole, cst))

    spec = pl.BlockSpec(memory_space=VMEM)
    params = pltpu.CompilerParams(vmem_limit_bytes=16 * 2**20)
    tile = jax.ShapeDtypeStruct((groups, PX, LANES), F32)
    padded = jax.ShapeDtypeStruct((groups, PW * PW, LANES), F32)
    spread = jax.ShapeDtypeStruct((PX, LANES), F32)
    own, partial, g, h = pl.pallas_call(
        inner_kernel,
        out_shape=(padded, tile, spread, spread),
        in_specs=[spec] * 6,
        out_specs=(spec,) * 4,
        compiler_params=params,
        cost_estimate=pl.CostEstimate(flops=2 * 352 * channels * width, bytes_accessed=4 * 2**20, transcendentals=0),
        name="inner",
    )(above.reshape(3 * T, channels), flat, below.reshape(3 * T, channels), input_weight, kernel, px)
    _, local, near = pl.pallas_call(
        conv_scan_kernel,
        out_shape=(padded, tile, jax.ShapeDtypeStruct((2 * XS, 144, LANES), BF16)),
        in_specs=[spec] * 10,
        out_specs=(spec, spec, spec),
        scratch_shapes=[VMEM((6 * PW, channels), F32), VMEM((PX, LANES), F32), VMEM((2, 128, LANES), F32)],
        input_output_aliases={8: 0},
        compiler_params=params,
        name="conv_scan",
    )(before, after, input_weight, kernel, cst, g, h, tails, own, partial)
    near = swap(near, near_groups(rows, cols))

    far = pl.pallas_call(
        totals_kernel,
        out_shape=jax.ShapeDtypeStruct((FAR, 144, LANES), BF16),
        in_specs=[spec, spec],
        out_specs=spec,
        compiler_params=params,
        name="totals",
    )(near, whole)
    far = swap(far, far_groups(rows, cols))

    keep, give = pl.pallas_call(
        enter_kernel,
        out_shape=(jax.ShapeDtypeStruct((128, LANES), F32), jax.ShapeDtypeStruct((128, LANES), BF16)),
        in_specs=[spec, spec, spec],
        out_specs=(spec, spec),
        compiler_params=params,
        name="enter",
    )(near, far, whole)
    got = lax.ppermute(give, "row", [(i, i ^ 1) for i in range(rows)])

    acc = pl.pallas_call(
        own_axis_kernel,
        out_shape=tile,
        in_specs=[spec] * 4,
        out_specs=spec,
        compiler_params=params,
        cost_estimate=pl.CostEstimate(flops=6 * PX * width, bytes_accessed=2 * 2**20, transcendentals=0),
        name="own_axis",
    )(keep, cst, g, local)
    mixed = pl.pallas_call(
        finish_kernel,
        out_shape=jax.ShapeDtypeStruct((PX, channels), BF16),
        in_specs=[spec] * 7,
        out_specs=spec,
        scratch_shapes=[VMEM((groups, PX, LANES), F32), VMEM((128, LANES), F32), VMEM((PX, width), BF16)],
        compiler_params=params,
        name="finish",
    )(got, cst, g, acc, gate, flat, output_weight)
    return mixed.reshape(T, T, channels)


def solution(mesh):
    return jax.shard_map(
        body,
        mesh=mesh,
        in_specs=(P("row", "col", None), P(), P(), P(), P("row", "col"), P()),
        out_specs=P("row", "col", None),
        check_vma=False,
    )
```

```python
import jax
import jax.numpy as jnp
from jax import lax
from jax.experimental import pallas as pl
from jax.experimental.pallas import tpu as pltpu
from jax.sharding import PartitionSpec as P

T = 16
PX = T * T
PW = 24
LANES = 128
XS = 4
FAR = 8
F32 = jnp.float32
BF16 = jnp.bfloat16
VMEM = pltpu.VMEM


def position():
    row, col = lax.axis_index("row"), lax.axis_index("col")
    return row % 2, row // 2, col % XS, col // XS


def project(x, wv_ref, store):
    for half in range(wv_ref.shape[1] // 512):
        p = jnp.dot(x, wv_ref[:, half * 256:(half + 1) * 256], preferred_element_type=F32)
        p = p.astype(BF16).astype(F32)
        store(2 * half, p[:, :LANES])
        store(2 * half + 1, p[:, LANES:])


def add_taps(acc, v_ref, taps_ref, ct, lanes, jt, shifts):
    for b in shifts:
        tap = [taps_ref[a, pl.ds(b, 1), lanes] for a in range(7)]
        tap = [jnp.broadcast_to(t, (8, LANES)) for t in tap]
        for r in range(T + 6):
            x = v_ref[ct, pl.ds(r * PW + jt * 8 + b, 8), :]
            for a in range(7):
                i = r - a
                if 0 <= i < T:
                    acc[i] = tap[a] * x if acc[i] is None else acc[i] + tap[a] * x
    return acc


def fall(x):
    series = x * (1.0 - x / 2.0 * (1.0 - x / 3.0 * (1.0 - x / 4.0 * (1.0 - x / 5.0 * (1.0 - x / 6.0)))))
    return jnp.where(x < 0.1, series, 1.0 - jnp.exp(-x))


def spread_decays(table_ref, extra_ref, cst_ref, whole_ref, g_ref, h_ref, tails_ref):
    table = table_ref[...]
    cst_ref[0:4] = jnp.exp(-table)
    cst_ref[4:8] = fall(2.0 * table)
    cst_ref[8:12] = jnp.exp(-2.0 * table)
    cst_ref[12:16] = jnp.exp(-float(T) * table)
    for d in range(4):
        for ct in range(table.shape[1] // LANES):
            whole_ref[d, ct * T:(ct + 1) * T] = jnp.broadcast_to(
                cst_ref[12 + d:13 + d, ct * LANES:(ct + 1) * LANES], (T, LANES))
    extra = extra_ref[...]
    diagonal = lax.broadcasted_iota(jnp.int32, (T, T), 0) == lax.broadcasted_iota(jnp.int32, (T, T), 1)
    down = jnp.zeros((T, LANES), F32)
    for i in range(T):
        line = jnp.broadcast_to(extra[i:i + 1], (T, T))
        line = jnp.sum(jnp.where(diagonal, line, 0.0), axis=1, keepdims=True)
        line = jnp.broadcast_to(line, (T, LANES))
        g_ref[i * T:(i + 1) * T] = jnp.exp(-line)
        h_ref[i * T:(i + 1) * T] = fall(2.0 * line)
        down = down + line
    across = jnp.broadcast_to(jnp.sum(extra, axis=1, keepdims=True), (T, LANES))
    lane = lax.broadcasted_iota(jnp.int32, (T, LANES), 1)
    for k, total in enumerate((across, down)):
        decay = jnp.exp(-total)
        high = decay.astype(BF16).astype(F32)
        tails_ref[k] = jnp.where(lane < 64, high, decay - high).astype(BF16)


def inner_kernel(above_ref, tok_ref, below_ref, weight_ref, taps_ref, table_ref, extra_ref,
                 acc_ref, gate_ref, cst_ref, whole_ref, g_ref, h_ref, tails_ref, v_ref):
    groups = v_ref.shape[0]
    spread_decays(table_ref, extra_ref, cst_ref, whole_ref, g_ref, h_ref, tails_ref)
    for ct in range(groups):
        for j in (0, 1, 2, T + 3, T + 4, T + 5):
            v_ref[ct, pl.ds(j, PW, stride=PW), :] = jnp.zeros((PW, LANES), F32)
    for ref, first in ((above_ref, 0), (tok_ref, 3), (below_ref, T + 3)):
        count = ref.shape[0] // T

        def store(ct, p, first=first, count=count):
            for i in range(count):
                v_ref[ct, pl.ds((first + i) * PW + 3, T), :] = p[i * T:(i + 1) * T]

        project(ref[...], weight_ref, store)
    width = groups * LANES
    for half in range(width // 256):
        at = slice(width + half * 256, width + (half + 1) * 256)
        pre = jnp.dot(tok_ref[...], weight_ref[:, at], preferred_element_type=F32)
        gate_ref[:, half * 256:(half + 1) * 256] = pre / (1.0 + jnp.exp(-pre))

    def group(ct, carry):
        lanes = pl.ds(pl.multiple_of(ct * LANES, LANES), LANES)
        for jt in range(2):
            acc = add_taps([None] * T, v_ref, taps_ref, ct, lanes, jt, range(7))
            for i in range(T):
                acc_ref[ct, pl.ds(i * T + jt * 8, 8), :] = acc[i]
        return carry

    lax.fori_loop(0, groups, group, 0)


def conv_scan_kernel(before_ref, after_ref, wv_ref, taps_ref, cst_ref, g_ref, h_ref, tails_ref, own_ref,
                     acc_ref, sum_ref, near_ref, side_ref, line_ref, val_ref, end_ref):
    del own_ref
    groups = line_ref.shape[0]
    side_ref[0:3 * PW] = before_ref[...].astype(F32)
    side_ref[3 * PW:] = after_ref[...].astype(F32)

    def keep_line(ct, p):
        line_ref[ct] = p

    project(side_ref[...].astype(BF16), wv_ref, keep_line)

    def group(ct, carry):
        lanes = pl.ds(pl.multiple_of(ct * LANES, LANES), LANES)
        cst = [cst_ref[pl.ds(k, 1), lanes] for k in range(12)]

        def flow(d, g, h, x):
            q = cst[4 + d] + cst[8 + d] * h
            return cst[d] * g, q * lax.rsqrt(q) * x

        for side in range(2):
            outs = range(3) if side == 0 else range(T - 3, T)
            added = {}
            for a in range(7):
                for k in range(3):
                    column = k if side == 0 else T + 3 + k
                    reads = [line_ref[ct, pl.ds((3 * side + k) * PW + it * 8 + a, 8), :] for it in range(2)]
                    for j in outs:
                        if 0 <= column - j < 7:
                            tap = taps_ref[a, pl.ds(column - j, 1), lanes]
                            for it in range(2):
                                term = tap * reads[it]
                                added[j, it] = added[j, it] + term if (j, it) in added else term
            for (j, it), x in added.items():
                at = pl.ds(it * 8 * T + j, 8, stride=T)
                acc_ref[ct, at, :] = acc_ref[ct, at, :] + x
        for jt in range(2):
            acc = [acc_ref[ct, pl.ds(i * T + jt * 8, 8), :] for i in range(T)]
            vals = [x / (1.0 + jnp.exp(-x)) for x in acc]
            for i in range(T):
                val_ref[pl.ds(i * T + jt * 8, 8), :] = vals[i]
            state = jnp.zeros((8, LANES), F32)
            downs = []
            for i in range(T):
                at = pl.ds(i * T + jt * 8, 8)
                d, f = flow(2, g_ref[at, :], h_ref[at, :], vals[i])
                state = d * state + f
                downs.append(state)
            end_ref[1, pl.ds(0 + ct * T + jt * 8, 8), :] = state
            state = jnp.zeros((8, LANES), F32)
            for i in reversed(range(T)):
                at = pl.ds(i * T + jt * 8, 8)
                d, f = flow(3, g_ref[at, :], h_ref[at, :], vals[i])
                state = d * state + f
                sum_ref[ct, at, :] = downs[i] + state
            end_ref[1, pl.ds(64 + ct * T + jt * 8, 8), :] = state
        for it in range(2):
            state = jnp.zeros((8, LANES), F32)
            lefts = []
            for j in range(T):
                at = pl.ds(it * 8 * T + j, 8, stride=T)
                d, f = flow(0, g_ref[at, :], h_ref[at, :], val_ref[at, :])
                state = d * state + f
                lefts.append(state)
            end_ref[0, pl.ds(0 + ct * T + it * 8, 8), :] = state
            state = jnp.zeros((8, LANES), F32)
            for j in reversed(range(T)):
                at = pl.ds(it * 8 * T + j, 8, stride=T)
                d, f = flow(1, g_ref[at, :], h_ref[at, :], val_ref[at, :])
                state = d * state + f
                sum_ref[ct, at, :] = sum_ref[ct, at, :] + (lefts[j] + state)
            end_ref[0, pl.ds(64 + ct * T + it * 8, 8), :] = state
        return carry

    lax.fori_loop(0, groups, group, 0)
    for peer in range(2 * XS):
        near_ref[peer, 0:128] = end_ref[peer // XS].astype(BF16)
        near_ref[peer, 128:144] = tails_ref[peer // XS]


def line_decay(block, at):
    decay = jnp.broadcast_to(block[128:144, at:at + 1], (T, LANES))
    return jnp.concatenate([decay] * 4, axis=0)


def pair_decay(block, at, gap):
    return line_decay(block, at) + line_decay(block, at + gap)


def totals_kernel(near_ref, whole_ref, far_ref):
    core, y, x, z = position()
    lane = lax.broadcasted_iota(jnp.int32, (T, LANES), 1)

    def spread(first, second):
        parts = []
        for d in (first, second):
            high = d[:T].astype(BF16).astype(F32)
            parts += [high, d[:T] - high]
        return jnp.where(lane < 32, parts[0], jnp.where(
            lane < 64, parts[1], jnp.where(lane < 96, parts[2], parts[3]))).astype(BF16)

    @pl.when(core == 0)
    def _():
        ahead, back = whole_ref[0], whole_ref[1]
        products = []
        for k in range(2):
            blocks = [near_ref[k * XS + i].astype(F32) for i in range(XS)]
            decays = [pair_decay(b, 0, 64) for b in blocks]
            former, product = blocks[0][:64], decays[0]
            for i in range(1, XS):
                former = ahead * decays[i] * former + blocks[i][:64]
                product = product * decays[i]
            latter = blocks[XS - 1][64:128]
            for i in reversed(range(XS - 1)):
                latter = back * decays[i] * latter + blocks[i][64:128]
            products.append(product)
            former, latter = former.astype(BF16), latter.astype(BF16)
            for peer in range(FAR):
                far_ref[peer, 64 * k:64 * k + 64] = jnp.where(peer > z, former, latter)
        tail = spread(products[0], products[1])
        for peer in range(FAR):
            far_ref[peer, 128:144] = tail

    @pl.when(core == 1)
    def _():
        first, second = near_ref[x].astype(F32), near_ref[XS + x].astype(F32)
        decays = [pair_decay(first, 0, 64), pair_decay(second, 0, 64)]
        former = (whole_ref[2] * decays[1] * first[:64] + second[:64]).astype(BF16)
        latter = (whole_ref[3] * decays[0] * second[64:128] + first[64:128]).astype(BF16)
        product = decays[0] * decays[1]
        tail = spread(product, product)
        for peer in range(FAR):
            far_ref[peer, 0:64] = jnp.where(peer > y, former, latter)
            far_ref[peer, 64:128] = jnp.zeros((64, LANES), BF16)
            far_ref[peer, 128:144] = tail


def enter_kernel(near_ref, far_ref, whole_ref, keep_ref, give_ref):
    core, y, x, z = position()

    def far_states(me, k, ahead, back):
        blocks = [far_ref[i].astype(F32) for i in range(FAR)]
        decays = [pair_decay(b, 64 * k, 32) for b in blocks]
        fore = jnp.zeros((64, LANES), F32)
        aft = jnp.zeros((64, LANES), F32)
        for i in range(FAR - 1):
            fore = jnp.where(i < me, ahead * decays[i] * fore + blocks[i][64 * k:64 * k + 64], fore)
        for i in reversed(range(1, FAR)):
            aft = jnp.where(i > me, back * decays[i] * aft + blocks[i][64 * k:64 * k + 64], aft)
        return fore, aft

    @pl.when(core == 0)
    def _():
        ahead, back = whole_ref[0], whole_ref[1]
        ahead_far, back_far = ahead, back
        for _ in range(2):
            ahead_far, back_far = ahead_far * ahead_far, back_far * back_far
        for k in range(2):
            fore, aft = far_states(z, k, ahead_far, back_far)
            blocks = [near_ref[k * XS + i].astype(F32) for i in range(XS)]
            decays = [pair_decay(b, 0, 64) for b in blocks]
            for i in range(XS - 1):
                fore = jnp.where(i < x, ahead * decays[i] * fore + blocks[i][:64], fore)
            for i in reversed(range(1, XS)):
                aft = jnp.where(i > x, back * decays[i] * aft + blocks[i][64:128], aft)
            if k == 0:
                keep_ref[0:64], keep_ref[64:128] = fore, aft
            else:
                give_ref[0:64], give_ref[64:128] = fore.astype(BF16), aft.astype(BF16)

    @pl.when(core == 1)
    def _():
        ahead, back = whole_ref[2], whole_ref[3]
        fore, aft = far_states(y, 0, ahead * ahead, back * back)
        first, second = near_ref[x].astype(F32), near_ref[XS + x].astype(F32)
        give_ref[0:64] = fore.astype(BF16)
        give_ref[64:128] = (back * pair_decay(second, 0, 64) * aft + second[64:128]).astype(BF16)
        keep_ref[0:64] = ahead * pair_decay(first, 0, 64) * fore + first[:64]
        keep_ref[64:128] = aft


def decay_rows(kind, first, cst_ref, g_ref, store):
    def group(ct, carry):
        lanes = pl.ds(pl.multiple_of(ct * LANES, LANES), LANES)
        ahead, back = cst_ref[pl.ds(2 * kind, 1), lanes], cst_ref[pl.ds(2 * kind + 1, 1), lanes]
        for half in range(2):
            fore = first(0, ct, half)
            aft = first(1, ct, half)

            def at(n):
                return pl.ds(half * 8 * T + n, 8, stride=T) if kind == 0 else pl.ds(n * T + half * 8, 8)

            fores = []
            for n in range(T):
                fore = fore * (ahead * g_ref[at(n), :])
                fores.append(fore)
            for n in reversed(range(T)):
                aft = aft * (back * g_ref[at(n), :])
                store(ct, at(n), fores[n] + aft)
        return carry

    lax.fori_loop(0, 4, group, 0)


def own_axis_kernel(keep_ref, cst_ref, g_ref, sum_ref, acc_ref):
    def first(side, ct, half):
        return keep_ref[pl.ds(64 * side + ct * T + half * 8, 8), :]

    def store(ct, at, x):
        acc_ref[ct, at, :] = sum_ref[ct, at, :] + x

    for kind in range(2):
        @pl.when(position()[0] == kind)
        def _():
            decay_rows(kind, first, cst_ref, g_ref, store)


def finish_kernel(got_ref, cst_ref, g_ref, sum_ref, gate_ref, tok_ref, wo_ref,
                  out_ref, acc_ref, enter_ref, gated_ref):
    groups = acc_ref.shape[0]
    enter_ref[...] = got_ref[...].astype(F32)

    def first(side, ct, half):
        return enter_ref[pl.ds(64 * side + ct * T + half * 8, 8), :]

    def store(ct, at, x):
        acc_ref[ct, at, :] = sum_ref[ct, at, :] + x

    for kind in range(2):
        @pl.when(position()[0] != kind)
        def _():
            decay_rows(kind, first, cst_ref, g_ref, store)

    for ct in range(groups):
        lanes = slice(ct * LANES, (ct + 1) * LANES)
        gated_ref[:, lanes] = (acc_ref[ct] * gate_ref[:, lanes]).astype(BF16)
    mixed = jnp.dot(gated_ref[...], wo_ref[...], preferred_element_type=F32)
    out_ref[...] = (tok_ref[...].astype(F32) + mixed).astype(BF16)


def neighbours(x_first, x_last, axis):
    size = lax.axis_size(axis)
    up = [(i, i + 1) for i in range(size - 1)]
    down = [(i + 1, i) for i in range(size - 1)]
    return lax.ppermute(x_last, axis, up), lax.ppermute(x_first, axis, down)


def near_groups(rows, cols):
    return [[(2 * y + k) * cols + XS * z + x for k in range(2) for x in range(XS)]
            for y in range(rows // 2) for z in range(cols // XS)]


def far_groups(rows, cols):
    along_z = [[2 * y * cols + XS * z + x for z in range(cols // XS)]
               for y in range(rows // 2) for x in range(XS)]
    along_y = [[(2 * y + 1) * cols + c for y in range(rows // 2)] for c in range(cols)]
    return along_z + along_y


def swap(x, groups):
    return lax.all_to_all(x, ("row", "col"), 0, 0, axis_index_groups=groups, tiled=True)


def body(tokens, input_weight, kernel, direction_decay_table, pixel_extra_decay, output_weight):
    width = output_weight.shape[0]
    groups = width // LANES
    channels = tokens.shape[2]
    rows, cols = lax.axis_size("row"), lax.axis_size("col")
    table, extra = direction_decay_table, pixel_extra_decay
    flat = tokens.reshape(PX, channels)
    above, below = neighbours(tokens[:3], tokens[T - 3:], "row")

    def strip(at):
        x = jnp.concatenate([above[:, at], tokens[:, at], below[:, at],
                             jnp.zeros((PW - T - 6, 3, channels), BF16)], axis=0)
        return x.transpose(1, 0, 2).reshape(3 * PW, channels)

    before, after = neighbours(strip(slice(0, 3)), strip(slice(T - 3, T)), "col")

    spec = pl.BlockSpec(memory_space=VMEM)
    params = pltpu.CompilerParams(vmem_limit_bytes=16 * 2**20)
    tile = jax.ShapeDtypeStruct((groups, PX, LANES), F32)
    spread = jax.ShapeDtypeStruct((PX, LANES), F32)
    own, gate, cst, whole, g, h, tails = pl.pallas_call(
        inner_kernel,
        out_shape=(tile, jax.ShapeDtypeStruct((PX, width), F32), jax.ShapeDtypeStruct((16, width), F32),
                   jax.ShapeDtypeStruct((4, groups * T, LANES), F32), spread, spread,
                   jax.ShapeDtypeStruct((2, T, LANES), BF16)),
        in_specs=[spec] * 7,
        out_specs=(spec,) * 7,
        scratch_shapes=[VMEM((groups, PW * PW, LANES), F32)],
        compiler_params=params,
        cost_estimate=pl.CostEstimate(flops=2 * 608 * channels * width, bytes_accessed=4 * 2**20, transcendentals=0),
        name="inner",
    )(above.reshape(3 * T, channels), flat, below.reshape(3 * T, channels), input_weight, kernel, table, extra)
    _, local, near = pl.pallas_call(
        conv_scan_kernel,
        out_shape=(tile, tile, jax.ShapeDtypeStruct((2 * XS, 144, LANES), BF16)),
        in_specs=[spec] * 9,
        out_specs=(spec, spec, spec),
        scratch_shapes=[VMEM((6 * PW, channels), F32), VMEM((groups, 6 * PW, LANES), F32),
                        VMEM((PX, LANES), F32), VMEM((2, 128, LANES), F32)],
        input_output_aliases={8: 0},
        compiler_params=params,
        name="conv_scan",
    )(before, after, input_weight, kernel, cst, g, h, tails, own)
    near = swap(near, near_groups(rows, cols))

    far = pl.pallas_call(
        totals_kernel,
        out_shape=jax.ShapeDtypeStruct((FAR, 144, LANES), BF16),
        in_specs=[spec, spec],
        out_specs=spec,
        compiler_params=params,
        name="totals",
    )(near, whole)
    far = swap(far, far_groups(rows, cols))

    keep, give = pl.pallas_call(
        enter_kernel,
        out_shape=(jax.ShapeDtypeStruct((128, LANES), F32), jax.ShapeDtypeStruct((128, LANES), BF16)),
        in_specs=[spec, spec, spec],
        out_specs=(spec, spec),
        compiler_params=params,
        name="enter",
    )(near, far, whole)
    got = lax.ppermute(give, "row", [(i, i ^ 1) for i in range(rows)])

    acc = pl.pallas_call(
        own_axis_kernel,
        out_shape=tile,
        in_specs=[spec] * 4,
        out_specs=spec,
        compiler_params=params,
        cost_estimate=pl.CostEstimate(flops=6 * PX * width, bytes_accessed=2 * 2**20, transcendentals=0),
        name="own_axis",
    )(keep, cst, g, local)
    mixed = pl.pallas_call(
        finish_kernel,
        out_shape=jax.ShapeDtypeStruct((PX, channels), BF16),
        in_specs=[spec] * 7,
        out_specs=spec,
        scratch_shapes=[VMEM((groups, PX, LANES), F32), VMEM((128, LANES), F32), VMEM((PX, width), BF16)],
        compiler_params=params,
        name="finish",
    )(got, cst, g, acc, gate, flat, output_weight)
    return mixed.reshape(T, T, channels)


def solution(mesh):
    return jax.shard_map(
        body,
        mesh=mesh,
        in_specs=(P("row", "col", None), P(), P(), P(), P("row", "col"), P()),
        out_specs=P("row", "col", None),
        check_vma=False,
    )
```

```python
import jax
import jax.numpy as jnp
from jax import lax
from jax.experimental import pallas as pl
from jax.experimental.pallas import tpu as pltpu
from jax.sharding import PartitionSpec as P

T = 16
PX = T * T
PW = 24
LANES = 128
XS = 4
FAR = 8
F32 = jnp.float32
BF16 = jnp.bfloat16
VMEM = pltpu.VMEM


def position():
    row, col = lax.axis_index("row"), lax.axis_index("col")
    return row % 2, row // 2, col % XS, col // XS


def project(x, wv_ref, store):
    for half in range(wv_ref.shape[1] // 512):
        p = jnp.dot(x, wv_ref[:, half * 256:(half + 1) * 256], preferred_element_type=F32)
        p = p.astype(BF16).astype(F32)
        store(2 * half, p[:, :LANES])
        store(2 * half + 1, p[:, LANES:])


def add_taps(acc, v_ref, taps_ref, ct, lanes, jt, shifts):
    for b in shifts:
        tap = [taps_ref[a, pl.ds(b, 1), lanes] for a in range(7)]
        tap = [jnp.broadcast_to(t, (8, LANES)) for t in tap]
        for r in range(T + 6):
            x = v_ref[ct, pl.ds(r * PW + jt * 8 + b, 8), :]
            for a in range(7):
                i = r - a
                if 0 <= i < T:
                    acc[i] = tap[a] * x if acc[i] is None else acc[i] + tap[a] * x
    return acc


def fall(x):
    series = x * (1.0 - x / 2.0 * (1.0 - x / 3.0 * (1.0 - x / 4.0 * (1.0 - x / 5.0 * (1.0 - x / 6.0)))))
    return jnp.where(x < 0.1, series, 1.0 - jnp.exp(-x))


def spread_decays(table_ref, extra_ref, cst_ref, whole_ref, g_ref, tails_ref, flow_refs, h_ref):
    table = table_ref[...]
    cst_ref[0:4] = jnp.exp(-table)
    cst_ref[4:8] = fall(2.0 * table)
    cst_ref[8:12] = jnp.exp(-2.0 * table)
    cst_ref[12:16] = jnp.exp(-float(T) * table)
    for d in range(4):
        for ct in range(table.shape[1] // LANES):
            whole_ref[d, ct * T:(ct + 1) * T] = jnp.broadcast_to(
                cst_ref[12 + d:13 + d, ct * LANES:(ct + 1) * LANES], (T, LANES))
    extra = extra_ref[...]
    diagonal = lax.broadcasted_iota(jnp.int32, (T, T), 0) == lax.broadcasted_iota(jnp.int32, (T, T), 1)
    down = jnp.zeros((T, LANES), F32)
    for i in range(T):
        line = jnp.broadcast_to(extra[i:i + 1], (T, T))
        line = jnp.sum(jnp.where(diagonal, line, 0.0), axis=1, keepdims=True)
        line = jnp.broadcast_to(line, (T, LANES))
        g_ref[i * T:(i + 1) * T] = jnp.exp(-line)
        h_ref[i * T:(i + 1) * T] = fall(2.0 * line)
        down = down + line
    across = jnp.broadcast_to(jnp.sum(extra, axis=1, keepdims=True), (T, LANES))
    lane = lax.broadcasted_iota(jnp.int32, (T, LANES), 1)
    for k, total in enumerate((across, down)):
        decay = jnp.exp(-total)
        high = decay.astype(BF16).astype(F32)
        tails_ref[k] = jnp.where(lane < 64, high, decay - high).astype(BF16)

    def group(ct, carry):
        lanes = pl.ds(pl.multiple_of(ct * LANES, LANES), LANES)
        for d in range(4):
            base, slope = cst_ref[pl.ds(4 + d, 1), lanes], cst_ref[pl.ds(8 + d, 1), lanes]
            q = base + slope * h_ref[...]
            flow_refs[d // 2][d % 2, ct] = q * lax.rsqrt(q)
        return carry

    lax.fori_loop(0, flow_refs[0].shape[1], group, 0)


def inner_kernel(above_ref, tok_ref, below_ref, weight_ref, taps_ref, table_ref, extra_ref,
                 acc_ref, gate_ref, cst_ref, whole_ref, g_ref, tails_ref, along_ref, down_ref, v_ref, h_ref):
    groups = v_ref.shape[0]
    spread_decays(table_ref, extra_ref, cst_ref, whole_ref, g_ref, tails_ref, (along_ref, down_ref), h_ref)
    for ct in range(groups):
        for j in (0, 1, 2, T + 3, T + 4, T + 5):
            v_ref[ct, pl.ds(j, PW, stride=PW), :] = jnp.zeros((PW, LANES), F32)
    for ref, first in ((above_ref, 0), (tok_ref, 3), (below_ref, T + 3)):
        count = ref.shape[0] // T

        def store(ct, p, first=first, count=count):
            for i in range(count):
                v_ref[ct, pl.ds((first + i) * PW + 3, T), :] = p[i * T:(i + 1) * T]

        project(ref[...], weight_ref, store)
    width = groups * LANES
    for half in range(width // 256):
        at = slice(width + half * 256, width + (half + 1) * 256)
        pre = jnp.dot(tok_ref[...], weight_ref[:, at], preferred_element_type=F32)
        gate_ref[:, half * 256:(half + 1) * 256] = pre / (1.0 + jnp.exp(-pre))

    def group(ct, carry):
        lanes = pl.ds(pl.multiple_of(ct * LANES, LANES), LANES)
        for jt in range(2):
            acc = add_taps([None] * T, v_ref, taps_ref, ct, lanes, jt, range(7))
            for i in range(T):
                acc_ref[ct, pl.ds(i * T + jt * 8, 8), :] = acc[i]
        return carry

    lax.fori_loop(0, groups, group, 0)


def conv_scan_kernel(before_ref, after_ref, wv_ref, taps_ref, cst_ref, g_ref, along_ref, down_ref, tails_ref,
                     own_ref, acc_ref, sum_ref, near_ref, side_ref, line_ref, val_ref, end_ref):
    del own_ref
    groups = line_ref.shape[0]
    side_ref[0:3 * PW] = before_ref[...].astype(F32)
    side_ref[3 * PW:] = after_ref[...].astype(F32)

    def keep_line(ct, p):
        line_ref[ct] = p

    project(side_ref[...].astype(BF16), wv_ref, keep_line)

    def group(ct, carry):
        lanes = pl.ds(pl.multiple_of(ct * LANES, LANES), LANES)
        cst = [cst_ref[pl.ds(k, 1), lanes] for k in range(4)]

        def flow(d, at, x):
            return cst[d] * g_ref[at, :], (along_ref, down_ref)[d // 2][d % 2, ct, at, :] * x

        for side in range(2):
            outs = range(3) if side == 0 else range(T - 3, T)
            added = {}
            for a in range(7):
                for k in range(3):
                    column = k if side == 0 else T + 3 + k
                    reads = [line_ref[ct, pl.ds((3 * side + k) * PW + it * 8 + a, 8), :] for it in range(2)]
                    for j in outs:
                        if 0 <= column - j < 7:
                            tap = taps_ref[a, pl.ds(column - j, 1), lanes]
                            for it in range(2):
                                term = tap * reads[it]
                                added[j, it] = added[j, it] + term if (j, it) in added else term
            for (j, it), x in added.items():
                at = pl.ds(it * 8 * T + j, 8, stride=T)
                acc_ref[ct, at, :] = acc_ref[ct, at, :] + x
        for jt in range(2):
            acc = [acc_ref[ct, pl.ds(i * T + jt * 8, 8), :] for i in range(T)]
            vals = [x / (1.0 + jnp.exp(-x)) for x in acc]
            for i in range(T):
                val_ref[pl.ds(i * T + jt * 8, 8), :] = vals[i]
            state = jnp.zeros((8, LANES), F32)
            downs = []
            for i in range(T):
                at = pl.ds(i * T + jt * 8, 8)
                d, f = flow(2, at, vals[i])
                state = d * state + f
                downs.append(state)
            end_ref[1, pl.ds(0 + ct * T + jt * 8, 8), :] = state
            state = jnp.zeros((8, LANES), F32)
            for i in reversed(range(T)):
                at = pl.ds(i * T + jt * 8, 8)
                d, f = flow(3, at, vals[i])
                state = d * state + f
                sum_ref[ct, at, :] = downs[i] + state
            end_ref[1, pl.ds(64 + ct * T + jt * 8, 8), :] = state
        for it in range(2):
            state = jnp.zeros((8, LANES), F32)
            lefts = []
            for j in range(T):
                at = pl.ds(it * 8 * T + j, 8, stride=T)
                d, f = flow(0, at, val_ref[at, :])
                state = d * state + f
                lefts.append(state)
            end_ref[0, pl.ds(0 + ct * T + it * 8, 8), :] = state
            state = jnp.zeros((8, LANES), F32)
            for j in reversed(range(T)):
                at = pl.ds(it * 8 * T + j, 8, stride=T)
                d, f = flow(1, at, val_ref[at, :])
                state = d * state + f
                sum_ref[ct, at, :] = sum_ref[ct, at, :] + (lefts[j] + state)
            end_ref[0, pl.ds(64 + ct * T + it * 8, 8), :] = state
        return carry

    lax.fori_loop(0, groups, group, 0)
    for peer in range(2 * XS):
        near_ref[peer, 0:128] = end_ref[peer // XS].astype(BF16)
        near_ref[peer, 128:144] = tails_ref[peer // XS]


def line_decay(block, at):
    decay = jnp.broadcast_to(block[128:144, at:at + 1], (T, LANES))
    return jnp.concatenate([decay] * 4, axis=0)


def pair_decay(block, at, gap):
    return line_decay(block, at) + line_decay(block, at + gap)


def totals_kernel(near_ref, whole_ref, far_ref):
    core, y, x, z = position()
    lane = lax.broadcasted_iota(jnp.int32, (T, LANES), 1)

    def spread(first, second):
        parts = []
        for d in (first, second):
            high = d[:T].astype(BF16).astype(F32)
            parts += [high, d[:T] - high]
        return jnp.where(lane < 32, parts[0], jnp.where(
            lane < 64, parts[1], jnp.where(lane < 96, parts[2], parts[3]))).astype(BF16)

    @pl.when(core == 0)
    def _():
        ahead, back = whole_ref[0], whole_ref[1]
        products = []
        for k in range(2):
            blocks = [near_ref[k * XS + i].astype(F32) for i in range(XS)]
            decays = [pair_decay(b, 0, 64) for b in blocks]
            former, product = blocks[0][:64], decays[0]
            for i in range(1, XS):
                former = ahead * decays[i] * former + blocks[i][:64]
                product = product * decays[i]
            latter = blocks[XS - 1][64:128]
            for i in reversed(range(XS - 1)):
                latter = back * decays[i] * latter + blocks[i][64:128]
            products.append(product)
            former, latter = former.astype(BF16), latter.astype(BF16)
            for peer in range(FAR):
                far_ref[peer, 64 * k:64 * k + 64] = jnp.where(peer > z, former, latter)
        tail = spread(products[0], products[1])
        for peer in range(FAR):
            far_ref[peer, 128:144] = tail

    @pl.when(core == 1)
    def _():
        first, second = near_ref[x].astype(F32), near_ref[XS + x].astype(F32)
        decays = [pair_decay(first, 0, 64), pair_decay(second, 0, 64)]
        former = (whole_ref[2] * decays[1] * first[:64] + second[:64]).astype(BF16)
        latter = (whole_ref[3] * decays[0] * second[64:128] + first[64:128]).astype(BF16)
        product = decays[0] * decays[1]
        tail = spread(product, product)
        for peer in range(FAR):
            far_ref[peer, 0:64] = jnp.where(peer > y, former, latter)
            far_ref[peer, 64:128] = jnp.zeros((64, LANES), BF16)
            far_ref[peer, 128:144] = tail


def enter_kernel(near_ref, far_ref, whole_ref, keep_ref, give_ref):
    core, y, x, z = position()

    def far_states(me, k, ahead, back):
        blocks = [far_ref[i].astype(F32) for i in range(FAR)]
        decays = [pair_decay(b, 64 * k, 32) for b in blocks]
        fore = jnp.zeros((64, LANES), F32)
        aft = jnp.zeros((64, LANES), F32)
        for i in range(FAR - 1):
            fore = jnp.where(i < me, ahead * decays[i] * fore + blocks[i][64 * k:64 * k + 64], fore)
        for i in reversed(range(1, FAR)):
            aft = jnp.where(i > me, back * decays[i] * aft + blocks[i][64 * k:64 * k + 64], aft)
        return fore, aft

    @pl.when(core == 0)
    def _():
        ahead, back = whole_ref[0], whole_ref[1]
        ahead_far, back_far = ahead, back
        for _ in range(2):
            ahead_far, back_far = ahead_far * ahead_far, back_far * back_far
        for k in range(2):
            fore, aft = far_states(z, k, ahead_far, back_far)
            blocks = [near_ref[k * XS + i].astype(F32) for i in range(XS)]
            decays = [pair_decay(b, 0, 64) for b in blocks]
            for i in range(XS - 1):
                fore = jnp.where(i < x, ahead * decays[i] * fore + blocks[i][:64], fore)
            for i in reversed(range(1, XS)):
                aft = jnp.where(i > x, back * decays[i] * aft + blocks[i][64:128], aft)
            if k == 0:
                keep_ref[0:64], keep_ref[64:128] = fore, aft
            else:
                give_ref[0:64], give_ref[64:128] = fore.astype(BF16), aft.astype(BF16)

    @pl.when(core == 1)
    def _():
        ahead, back = whole_ref[2], whole_ref[3]
        fore, aft = far_states(y, 0, ahead * ahead, back * back)
        first, second = near_ref[x].astype(F32), near_ref[XS + x].astype(F32)
        give_ref[0:64] = fore.astype(BF16)
        give_ref[64:128] = (back * pair_decay(second, 0, 64) * aft + second[64:128]).astype(BF16)
        keep_ref[0:64] = ahead * pair_decay(first, 0, 64) * fore + first[:64]
        keep_ref[64:128] = aft


def decay_rows(kind, first, cst_ref, g_ref, store):
    def group(ct, carry):
        lanes = pl.ds(pl.multiple_of(ct * LANES, LANES), LANES)
        ahead, back = cst_ref[pl.ds(2 * kind, 1), lanes], cst_ref[pl.ds(2 * kind + 1, 1), lanes]
        for half in range(2):
            fore = first(0, ct, half)
            aft = first(1, ct, half)

            def at(n):
                return pl.ds(half * 8 * T + n, 8, stride=T) if kind == 0 else pl.ds(n * T + half * 8, 8)

            fores = []
            for n in range(T):
                fore = fore * (ahead * g_ref[at(n), :])
                fores.append(fore)
            for n in reversed(range(T)):
                aft = aft * (back * g_ref[at(n), :])
                store(ct, at(n), fores[n] + aft)
        return carry

    lax.fori_loop(0, 4, group, 0)


def own_axis_kernel(keep_ref, cst_ref, g_ref, sum_ref, acc_ref):
    def first(side, ct, half):
        return keep_ref[pl.ds(64 * side + ct * T + half * 8, 8), :]

    def store(ct, at, x):
        acc_ref[ct, at, :] = sum_ref[ct, at, :] + x

    for kind in range(2):
        @pl.when(position()[0] == kind)
        def _():
            decay_rows(kind, first, cst_ref, g_ref, store)


def finish_kernel(got_ref, cst_ref, g_ref, sum_ref, gate_ref, tok_ref, wo_ref,
                  out_ref, acc_ref, enter_ref, gated_ref):
    groups = acc_ref.shape[0]
    enter_ref[...] = got_ref[...].astype(F32)

    def first(side, ct, half):
        return enter_ref[pl.ds(64 * side + ct * T + half * 8, 8), :]

    def store(ct, at, x):
        acc_ref[ct, at, :] = sum_ref[ct, at, :] + x

    for kind in range(2):
        @pl.when(position()[0] != kind)
        def _():
            decay_rows(kind, first, cst_ref, g_ref, store)

    for ct in range(groups):
        lanes = slice(ct * LANES, (ct + 1) * LANES)
        gated_ref[:, lanes] = (acc_ref[ct] * gate_ref[:, lanes]).astype(BF16)
    mixed = jnp.dot(gated_ref[...], wo_ref[...], preferred_element_type=F32)
    out_ref[...] = (tok_ref[...].astype(F32) + mixed).astype(BF16)


def neighbours(x_first, x_last, axis):
    size = lax.axis_size(axis)
    up = [(i, i + 1) for i in range(size - 1)]
    down = [(i + 1, i) for i in range(size - 1)]
    return lax.ppermute(x_last, axis, up), lax.ppermute(x_first, axis, down)


def near_groups(rows, cols):
    return [[(2 * y + k) * cols + XS * z + x for k in range(2) for x in range(XS)]
            for y in range(rows // 2) for z in range(cols // XS)]


def far_groups(rows, cols):
    along_z = [[2 * y * cols + XS * z + x for z in range(cols // XS)]
               for y in range(rows // 2) for x in range(XS)]
    along_y = [[(2 * y + 1) * cols + c for y in range(rows // 2)] for c in range(cols)]
    return along_z + along_y


def swap(x, groups):
    return lax.all_to_all(x, ("row", "col"), 0, 0, axis_index_groups=groups, tiled=True)


def body(tokens, input_weight, kernel, direction_decay_table, pixel_extra_decay, output_weight):
    width = output_weight.shape[0]
    groups = width // LANES
    channels = tokens.shape[2]
    rows, cols = lax.axis_size("row"), lax.axis_size("col")
    table, extra = direction_decay_table, pixel_extra_decay
    flat = tokens.reshape(PX, channels)
    above, below = neighbours(tokens[:3], tokens[T - 3:], "row")

    def strip(at):
        x = jnp.concatenate([above[:, at], tokens[:, at], below[:, at],
                             jnp.zeros((PW - T - 6, 3, channels), BF16)], axis=0)
        return x.transpose(1, 0, 2).reshape(3 * PW, channels)

    before, after = neighbours(strip(slice(0, 3)), strip(slice(T - 3, T)), "col")

    spec = pl.BlockSpec(memory_space=VMEM)
    params = pltpu.CompilerParams(vmem_limit_bytes=16 * 2**20)
    tile = jax.ShapeDtypeStruct((groups, PX, LANES), F32)
    factor = jax.ShapeDtypeStruct((2, groups, PX, LANES), F32)
    own, gate, cst, whole, g, tails, along, downward = pl.pallas_call(
        inner_kernel,
        out_shape=(tile, jax.ShapeDtypeStruct((PX, width), F32), jax.ShapeDtypeStruct((16, width), F32),
                   jax.ShapeDtypeStruct((4, groups * T, LANES), F32),
                   jax.ShapeDtypeStruct((PX, LANES), F32), jax.ShapeDtypeStruct((2, T, LANES), BF16),
                   factor, factor),
        in_specs=[spec] * 7,
        out_specs=(spec,) * 8,
        scratch_shapes=[VMEM((groups, PW * PW, LANES), F32), VMEM((PX, LANES), F32)],
        compiler_params=params,
        cost_estimate=pl.CostEstimate(flops=2 * 608 * channels * width, bytes_accessed=4 * 2**20, transcendentals=0),
        name="inner",
    )(above.reshape(3 * T, channels), flat, below.reshape(3 * T, channels), input_weight, kernel, table, extra)
    _, local, near = pl.pallas_call(
        conv_scan_kernel,
        out_shape=(tile, tile, jax.ShapeDtypeStruct((2 * XS, 144, LANES), BF16)),
        in_specs=[spec] * 10,
        out_specs=(spec, spec, spec),
        scratch_shapes=[VMEM((6 * PW, channels), F32), VMEM((groups, 6 * PW, LANES), F32),
                        VMEM((PX, LANES), F32), VMEM((2, 128, LANES), F32)],
        input_output_aliases={9: 0},
        compiler_params=params,
        name="conv_scan",
    )(before, after, input_weight, kernel, cst, g, along, downward, tails, own)
    near = swap(near, near_groups(rows, cols))

    far = pl.pallas_call(
        totals_kernel,
        out_shape=jax.ShapeDtypeStruct((FAR, 144, LANES), BF16),
        in_specs=[spec, spec],
        out_specs=spec,
        compiler_params=params,
        name="totals",
    )(near, whole)
    far = swap(far, far_groups(rows, cols))

    keep, give = pl.pallas_call(
        enter_kernel,
        out_shape=(jax.ShapeDtypeStruct((128, LANES), F32), jax.ShapeDtypeStruct((128, LANES), BF16)),
        in_specs=[spec, spec, spec],
        out_specs=(spec, spec),
        compiler_params=params,
        name="enter",
    )(near, far, whole)
    got = lax.ppermute(give, "row", [(i, i ^ 1) for i in range(rows)])

    acc = pl.pallas_call(
        own_axis_kernel,
        out_shape=tile,
        in_specs=[spec] * 4,
        out_specs=spec,
        compiler_params=params,
        cost_estimate=pl.CostEstimate(flops=6 * PX * width, bytes_accessed=2 * 2**20, transcendentals=0),
        name="own_axis",
    )(keep, cst, g, local)
    mixed = pl.pallas_call(
        finish_kernel,
        out_shape=jax.ShapeDtypeStruct((PX, channels), BF16),
        in_specs=[spec] * 7,
        out_specs=spec,
        scratch_shapes=[VMEM((groups, PX, LANES), F32), VMEM((128, LANES), F32), VMEM((PX, width), BF16)],
        compiler_params=params,
        name="finish",
    )(got, cst, g, acc, gate, flat, output_weight)
    return mixed.reshape(T, T, channels)


def solution(mesh):
    return jax.shard_map(
        body,
        mesh=mesh,
        in_specs=(P("row", "col", None), P(), P(), P(), P("row", "col"), P()),
        out_specs=P("row", "col", None),
        check_vma=False,
    )
```

```python
import jax
import jax.numpy as jnp
from jax import lax
from jax.experimental import pallas as pl
from jax.experimental.pallas import tpu as pltpu
from jax.sharding import PartitionSpec as P

T = 16
PX = T * T
PW = 24
LANES = 128
XS = 4
FAR = 8
F32 = jnp.float32
BF16 = jnp.bfloat16
VMEM = pltpu.VMEM


def position():
    row, col = lax.axis_index("row"), lax.axis_index("col")
    return row % 2, row // 2, col % XS, col // XS


def project(x, wv_ref, store):
    for half in range(wv_ref.shape[1] // 512):
        p = jnp.dot(x, wv_ref[:, half * 256:(half + 1) * 256], preferred_element_type=F32)
        p = p.astype(BF16).astype(F32)
        store(2 * half, p[:, :LANES])
        store(2 * half + 1, p[:, LANES:])


def add_taps(acc, v_ref, taps_ref, ct, lanes, jt, shifts):
    for b in shifts:
        tap = [taps_ref[a, pl.ds(b, 1), lanes] for a in range(7)]
        tap = [jnp.broadcast_to(t, (8, LANES)) for t in tap]
        for r in range(3, T + 3):
            x = v_ref[ct, pl.ds(r * PW + jt * 8 + b, 8), :]
            for a in range(7):
                i = r - a
                if 0 <= i < T:
                    acc[i] = tap[a] * x if acc[i] is None else acc[i] + tap[a] * x
    return acc


def fall(x):
    series = x * (1.0 - x / 2.0 * (1.0 - x / 3.0 * (1.0 - x / 4.0 * (1.0 - x / 5.0 * (1.0 - x / 6.0)))))
    return jnp.where(x < 0.1, series, 1.0 - jnp.exp(-x))


def spread_decays(table_ref, extra_ref, cst_ref, whole_ref, g_ref, h_ref, tails_ref):
    table = table_ref[...]
    cst_ref[0:4] = jnp.exp(-table)
    cst_ref[4:8] = fall(2.0 * table)
    cst_ref[8:12] = jnp.exp(-2.0 * table)
    cst_ref[12:16] = jnp.exp(-float(T) * table)
    for d in range(4):
        for ct in range(table.shape[1] // LANES):
            whole_ref[d, ct * T:(ct + 1) * T] = jnp.broadcast_to(
                cst_ref[12 + d:13 + d, ct * LANES:(ct + 1) * LANES], (T, LANES))
    extra = extra_ref[...]
    diagonal = lax.broadcasted_iota(jnp.int32, (T, T), 0) == lax.broadcasted_iota(jnp.int32, (T, T), 1)
    down = jnp.zeros((T, LANES), F32)
    for i in range(T):
        line = jnp.broadcast_to(extra[i:i + 1], (T, T))
        line = jnp.sum(jnp.where(diagonal, line, 0.0), axis=1, keepdims=True)
        line = jnp.broadcast_to(line, (T, LANES))
        g_ref[i * T:(i + 1) * T] = jnp.exp(-line)
        h_ref[i * T:(i + 1) * T] = fall(2.0 * line)
        down = down + line
    across = jnp.broadcast_to(jnp.sum(extra, axis=1, keepdims=True), (T, LANES))
    lane = lax.broadcasted_iota(jnp.int32, (T, LANES), 1)
    for k, total in enumerate((across, down)):
        decay = jnp.exp(-total)
        high = decay.astype(BF16).astype(F32)
        tails_ref[k] = jnp.where(lane < 64, high, decay - high).astype(BF16)


def own_kernel(tok_ref, weight_ref, taps_ref, acc_ref, v_ref):
    groups = v_ref.shape[0]
    for ct in range(groups):
        for j in (0, 1, 2, T + 3, T + 4, T + 5):
            v_ref[ct, pl.ds(j, PW, stride=PW), :] = jnp.zeros((PW, LANES), F32)

    def store(ct, p):
        for i in range(T):
            v_ref[ct, pl.ds((3 + i) * PW + 3, T), :] = p[i * T:(i + 1) * T]

    project(tok_ref[...], weight_ref, store)

    def group(ct, carry):
        lanes = pl.ds(pl.multiple_of(ct * LANES, LANES), LANES)
        for jt in range(2):
            acc = add_taps([None] * T, v_ref, taps_ref, ct, lanes, jt, range(7))
            for i in range(T):
                acc_ref[ct, pl.ds(i * T + jt * 8, 8), :] = acc[i]
        return carry

    lax.fori_loop(0, groups, group, 0)


def rows_kernel(above_ref, below_ref, tok_ref, weight_ref, taps_ref, table_ref, extra_ref, own_ref,
                acc_ref, gate_ref, cst_ref, whole_ref, g_ref, h_ref, tails_ref, v_ref):
    del own_ref
    groups = v_ref.shape[0]
    spread_decays(table_ref, extra_ref, cst_ref, whole_ref, g_ref, h_ref, tails_ref)
    for ct in range(groups):
        for j in (0, 1, 2, T + 3, T + 4, T + 5):
            v_ref[ct, pl.ds(j, 8, stride=PW), :] = jnp.zeros((8, LANES), F32)
    for ref, first in ((above_ref, 0), (below_ref, 3)):

        def store(ct, p, first=first):
            for k in range(3):
                v_ref[ct, pl.ds((first + k) * PW + 3, T), :] = p[k * T:(k + 1) * T]

        project(ref[...], weight_ref, store)
    width = groups * LANES
    for half in range(width // 256):
        at = slice(width + half * 256, width + (half + 1) * 256)
        pre = jnp.dot(tok_ref[...], weight_ref[:, at], preferred_element_type=F32)
        gate_ref[:, half * 256:(half + 1) * 256] = pre / (1.0 + jnp.exp(-pre))

    def group(ct, carry):
        lanes = pl.ds(pl.multiple_of(ct * LANES, LANES), LANES)
        for jt in range(2):
            outs = (0, 1, 2, T - 3, T - 2, T - 1)
            acc = {i: acc_ref[ct, pl.ds(i * T + jt * 8, 8), :] for i in outs}
            for b in range(7):
                for k in range(6):
                    row = k if k < 3 else T + k
                    x = v_ref[ct, pl.ds(k * PW + jt * 8 + b, 8), :]
                    for i in outs:
                        if 0 <= row - i < 7:
                            acc[i] = acc[i] + taps_ref[row - i, pl.ds(b, 1), lanes] * x
            for i in outs:
                acc_ref[ct, pl.ds(i * T + jt * 8, 8), :] = acc[i]
        return carry

    lax.fori_loop(0, groups, group, 0)


def conv_scan_kernel(before_ref, after_ref, wv_ref, taps_ref, cst_ref, g_ref, h_ref, tails_ref, own_ref,
                     acc_ref, sum_ref, near_ref, side_ref, line_ref, val_ref, end_ref):
    del own_ref
    groups = line_ref.shape[0]
    side_ref[0:3 * PW] = before_ref[...].astype(F32)
    side_ref[3 * PW:] = after_ref[...].astype(F32)

    def keep_line(ct, p):
        line_ref[ct] = p

    project(side_ref[...].astype(BF16), wv_ref, keep_line)

    def group(ct, carry):
        lanes = pl.ds(pl.multiple_of(ct * LANES, LANES), LANES)
        cst = [cst_ref[pl.ds(k, 1), lanes] for k in range(12)]

        def flow(d, g, h, x):
            q = cst[4 + d] + cst[8 + d] * h
            return cst[d] * g, q * lax.rsqrt(q) * x

        for side in range(2):
            outs = range(3) if side == 0 else range(T - 3, T)
            added = {}
            for a in range(7):
                for k in range(3):
                    column = k if side == 0 else T + 3 + k
                    reads = [line_ref[ct, pl.ds((3 * side + k) * PW + it * 8 + a, 8), :] for it in range(2)]
                    for j in outs:
                        if 0 <= column - j < 7:
                            tap = taps_ref[a, pl.ds(column - j, 1), lanes]
                            for it in range(2):
                                term = tap * reads[it]
                                added[j, it] = added[j, it] + term if (j, it) in added else term
            for (j, it), x in added.items():
                at = pl.ds(it * 8 * T + j, 8, stride=T)
                acc_ref[ct, at, :] = acc_ref[ct, at, :] + x
        for jt in range(2):
            acc = [acc_ref[ct, pl.ds(i * T + jt * 8, 8), :] for i in range(T)]
            vals = [x / (1.0 + jnp.exp(-x)) for x in acc]
            for i in range(T):
                val_ref[pl.ds(i * T + jt * 8, 8), :] = vals[i]
            state = jnp.zeros((8, LANES), F32)
            downs = []
            for i in range(T):
                at = pl.ds(i * T + jt * 8, 8)
                d, f = flow(2, g_ref[at, :], h_ref[at, :], vals[i])
                state = d * state + f
                downs.append(state)
            end_ref[1, pl.ds(0 + ct * T + jt * 8, 8), :] = state
            state = jnp.zeros((8, LANES), F32)
            for i in reversed(range(T)):
                at = pl.ds(i * T + jt * 8, 8)
                d, f = flow(3, g_ref[at, :], h_ref[at, :], vals[i])
                state = d * state + f
                sum_ref[ct, at, :] = downs[i] + state
            end_ref[1, pl.ds(64 + ct * T + jt * 8, 8), :] = state
        for it in range(2):
            state = jnp.zeros((8, LANES), F32)
            lefts = []
            for j in range(T):
                at = pl.ds(it * 8 * T + j, 8, stride=T)
                d, f = flow(0, g_ref[at, :], h_ref[at, :], val_ref[at, :])
                state = d * state + f
                lefts.append(state)
            end_ref[0, pl.ds(0 + ct * T + it * 8, 8), :] = state
            state = jnp.zeros((8, LANES), F32)
            for j in reversed(range(T)):
                at = pl.ds(it * 8 * T + j, 8, stride=T)
                d, f = flow(1, g_ref[at, :], h_ref[at, :], val_ref[at, :])
                state = d * state + f
                sum_ref[ct, at, :] = sum_ref[ct, at, :] + (lefts[j] + state)
            end_ref[0, pl.ds(64 + ct * T + it * 8, 8), :] = state
        return carry

    lax.fori_loop(0, groups, group, 0)
    for peer in range(2 * XS):
        near_ref[peer, 0:128] = end_ref[peer // XS].astype(BF16)
        near_ref[peer, 128:144] = tails_ref[peer // XS]


def line_decay(block, at):
    decay = jnp.broadcast_to(block[128:144, at:at + 1], (T, LANES))
    return jnp.concatenate([decay] * 4, axis=0)


def pair_decay(block, at, gap):
    return line_decay(block, at) + line_decay(block, at + gap)


def totals_kernel(near_ref, whole_ref, far_ref):
    core, y, x, z = position()
    lane = lax.broadcasted_iota(jnp.int32, (T, LANES), 1)

    def spread(first, second):
        parts = []
        for d in (first, second):
            high = d[:T].astype(BF16).astype(F32)
            parts += [high, d[:T] - high]
        return jnp.where(lane < 32, parts[0], jnp.where(
            lane < 64, parts[1], jnp.where(lane < 96, parts[2], parts[3]))).astype(BF16)

    @pl.when(core == 0)
    def _():
        ahead, back = whole_ref[0], whole_ref[1]
        products = []
        for k in range(2):
            blocks = [near_ref[k * XS + i].astype(F32) for i in range(XS)]
            decays = [pair_decay(b, 0, 64) for b in blocks]
            former, product = blocks[0][:64], decays[0]
            for i in range(1, XS):
                former = ahead * decays[i] * former + blocks[i][:64]
                product = product * decays[i]
            latter = blocks[XS - 1][64:128]
            for i in reversed(range(XS - 1)):
                latter = back * decays[i] * latter + blocks[i][64:128]
            products.append(product)
            former, latter = former.astype(BF16), latter.astype(BF16)
            for peer in range(FAR):
                far_ref[peer, 64 * k:64 * k + 64] = jnp.where(peer > z, former, latter)
        tail = spread(products[0], products[1])
        for peer in range(FAR):
            far_ref[peer, 128:144] = tail

    @pl.when(core == 1)
    def _():
        first, second = near_ref[x].astype(F32), near_ref[XS + x].astype(F32)
        decays = [pair_decay(first, 0, 64), pair_decay(second, 0, 64)]
        former = (whole_ref[2] * decays[1] * first[:64] + second[:64]).astype(BF16)
        latter = (whole_ref[3] * decays[0] * second[64:128] + first[64:128]).astype(BF16)
        product = decays[0] * decays[1]
        tail = spread(product, product)
        for peer in range(FAR):
            far_ref[peer, 0:64] = jnp.where(peer > y, former, latter)
            far_ref[peer, 64:128] = jnp.zeros((64, LANES), BF16)
            far_ref[peer, 128:144] = tail


def enter_kernel(near_ref, far_ref, whole_ref, keep_ref, give_ref):
    core, y, x, z = position()

    def far_states(me, k, ahead, back):
        blocks = [far_ref[i].astype(F32) for i in range(FAR)]
        decays = [pair_decay(b, 64 * k, 32) for b in blocks]
        fore = jnp.zeros((64, LANES), F32)
        aft = jnp.zeros((64, LANES), F32)
        for i in range(FAR - 1):
            fore = jnp.where(i < me, ahead * decays[i] * fore + blocks[i][64 * k:64 * k + 64], fore)
        for i in reversed(range(1, FAR)):
            aft = jnp.where(i > me, back * decays[i] * aft + blocks[i][64 * k:64 * k + 64], aft)
        return fore, aft

    @pl.when(core == 0)
    def _():
        ahead, back = whole_ref[0], whole_ref[1]
        ahead_far, back_far = ahead, back
        for _ in range(2):
            ahead_far, back_far = ahead_far * ahead_far, back_far * back_far
        for k in range(2):
            fore, aft = far_states(z, k, ahead_far, back_far)
            blocks = [near_ref[k * XS + i].astype(F32) for i in range(XS)]
            decays = [pair_decay(b, 0, 64) for b in blocks]
            for i in range(XS - 1):
                fore = jnp.where(i < x, ahead * decays[i] * fore + blocks[i][:64], fore)
            for i in reversed(range(1, XS)):
                aft = jnp.where(i > x, back * decays[i] * aft + blocks[i][64:128], aft)
            if k == 0:
                keep_ref[0:64], keep_ref[64:128] = fore, aft
            else:
                give_ref[0:64], give_ref[64:128] = fore.astype(BF16), aft.astype(BF16)

    @pl.when(core == 1)
    def _():
        ahead, back = whole_ref[2], whole_ref[3]
        fore, aft = far_states(y, 0, ahead * ahead, back * back)
        first, second = near_ref[x].astype(F32), near_ref[XS + x].astype(F32)
        give_ref[0:64] = fore.astype(BF16)
        give_ref[64:128] = (back * pair_decay(second, 0, 64) * aft + second[64:128]).astype(BF16)
        keep_ref[0:64] = ahead * pair_decay(first, 0, 64) * fore + first[:64]
        keep_ref[64:128] = aft


def decay_rows(kind, first, cst_ref, g_ref, store):
    def group(ct, carry):
        lanes = pl.ds(pl.multiple_of(ct * LANES, LANES), LANES)
        ahead, back = cst_ref[pl.ds(2 * kind, 1), lanes], cst_ref[pl.ds(2 * kind + 1, 1), lanes]
        for half in range(2):
            fore = first(0, ct, half)
            aft = first(1, ct, half)

            def at(n):
                return pl.ds(half * 8 * T + n, 8, stride=T) if kind == 0 else pl.ds(n * T + half * 8, 8)

            fores = []
            for n in range(T):
                fore = fore * (ahead * g_ref[at(n), :])
                fores.append(fore)
            for n in reversed(range(T)):
                aft = aft * (back * g_ref[at(n), :])
                store(ct, at(n), fores[n] + aft)
        return carry

    lax.fori_loop(0, 4, group, 0)


def own_axis_kernel(keep_ref, cst_ref, g_ref, sum_ref, acc_ref):
    def first(side, ct, half):
        return keep_ref[pl.ds(64 * side + ct * T + half * 8, 8), :]

    def store(ct, at, x):
        acc_ref[ct, at, :] = sum_ref[ct, at, :] + x

    for kind in range(2):
        @pl.when(position()[0] == kind)
        def _():
            decay_rows(kind, first, cst_ref, g_ref, store)


def finish_kernel(got_ref, cst_ref, g_ref, sum_ref, gate_ref, tok_ref, wo_ref,
                  out_ref, acc_ref, enter_ref, gated_ref):
    groups = acc_ref.shape[0]
    enter_ref[...] = got_ref[...].astype(F32)

    def first(side, ct, half):
        return enter_ref[pl.ds(64 * side + ct * T + half * 8, 8), :]

    def store(ct, at, x):
        acc_ref[ct, at, :] = sum_ref[ct, at, :] + x

    for kind in range(2):
        @pl.when(position()[0] != kind)
        def _():
            decay_rows(kind, first, cst_ref, g_ref, store)

    for ct in range(groups):
        lanes = slice(ct * LANES, (ct + 1) * LANES)
        gated_ref[:, lanes] = (acc_ref[ct] * gate_ref[:, lanes]).astype(BF16)
    mixed = jnp.dot(gated_ref[...], wo_ref[...], preferred_element_type=F32)
    out_ref[...] = (tok_ref[...].astype(F32) + mixed).astype(BF16)


def neighbours(x_first, x_last, axis):
    size = lax.axis_size(axis)
    up = [(i, i + 1) for i in range(size - 1)]
    down = [(i + 1, i) for i in range(size - 1)]
    return lax.ppermute(x_last, axis, up), lax.ppermute(x_first, axis, down)


def near_groups(rows, cols):
    return [[(2 * y + k) * cols + XS * z + x for k in range(2) for x in range(XS)]
            for y in range(rows // 2) for z in range(cols // XS)]


def far_groups(rows, cols):
    along_z = [[2 * y * cols + XS * z + x for z in range(cols // XS)]
               for y in range(rows // 2) for x in range(XS)]
    along_y = [[(2 * y + 1) * cols + c for y in range(rows // 2)] for c in range(cols)]
    return along_z + along_y


def swap(x, groups):
    return lax.all_to_all(x, ("row", "col"), 0, 0, axis_index_groups=groups, tiled=True)


def body(tokens, input_weight, kernel, direction_decay_table, pixel_extra_decay, output_weight):
    width = output_weight.shape[0]
    groups = width // LANES
    channels = tokens.shape[2]
    rows, cols = lax.axis_size("row"), lax.axis_size("col")
    table, extra = direction_decay_table, pixel_extra_decay
    flat = tokens.reshape(PX, channels)
    above, below = neighbours(tokens[:3], tokens[T - 3:], "row")

    def strip(at):
        x = jnp.concatenate([above[:, at], tokens[:, at], below[:, at],
                             jnp.zeros((PW - T - 6, 3, channels), BF16)], axis=0)
        return x.transpose(1, 0, 2).reshape(3 * PW, channels)

    spec = pl.BlockSpec(memory_space=VMEM)
    params = pltpu.CompilerParams(vmem_limit_bytes=16 * 2**20)
    tile = jax.ShapeDtypeStruct((groups, PX, LANES), F32)
    spread = jax.ShapeDtypeStruct((PX, LANES), F32)
    own = pl.pallas_call(
        own_kernel,
        out_shape=tile,
        in_specs=[spec] * 3,
        out_specs=spec,
        scratch_shapes=[VMEM((groups, PW * PW, LANES), F32)],
        compiler_params=params,
        cost_estimate=pl.CostEstimate(flops=2 * PX * channels * width, bytes_accessed=3 * 2**20, transcendentals=0),
        name="own",
    )(flat, input_weight, kernel)
    first, last, own = lax.optimization_barrier((strip(slice(0, 3)), strip(slice(T - 3, T)), own))
    before, after = neighbours(first, last, "col")

    own, gate, cst, whole, g, h, tails = pl.pallas_call(
        rows_kernel,
        out_shape=(tile, jax.ShapeDtypeStruct((PX, width), F32), jax.ShapeDtypeStruct((16, width), F32),
                   jax.ShapeDtypeStruct((4, groups * T, LANES), F32), spread, spread,
                   jax.ShapeDtypeStruct((2, T, LANES), BF16)),
        in_specs=[spec] * 8,
        out_specs=(spec,) * 7,
        scratch_shapes=[VMEM((groups, 8 * PW, LANES), F32)],
        input_output_aliases={7: 0},
        compiler_params=params,
        cost_estimate=pl.CostEstimate(flops=2 * PX * channels * width, bytes_accessed=2**20, transcendentals=0),
        name="rows",
    )(above.reshape(3 * T, channels), below.reshape(3 * T, channels), flat, input_weight, kernel, table, extra, own)
    _, local, near = pl.pallas_call(
        conv_scan_kernel,
        out_shape=(tile, tile, jax.ShapeDtypeStruct((2 * XS, 144, LANES), BF16)),
        in_specs=[spec] * 9,
        out_specs=(spec, spec, spec),
        scratch_shapes=[VMEM((6 * PW, channels), F32), VMEM((groups, 6 * PW, LANES), F32),
                        VMEM((PX, LANES), F32), VMEM((2, 128, LANES), F32)],
        input_output_aliases={8: 0},
        compiler_params=params,
        name="conv_scan",
    )(before, after, input_weight, kernel, cst, g, h, tails, own)
    near = swap(near, near_groups(rows, cols))

    far = pl.pallas_call(
        totals_kernel,
        out_shape=jax.ShapeDtypeStruct((FAR, 144, LANES), BF16),
        in_specs=[spec, spec],
        out_specs=spec,
        compiler_params=params,
        name="totals",
    )(near, whole)
    far = swap(far, far_groups(rows, cols))

    keep, give = pl.pallas_call(
        enter_kernel,
        out_shape=(jax.ShapeDtypeStruct((128, LANES), F32), jax.ShapeDtypeStruct((128, LANES), BF16)),
        in_specs=[spec, spec, spec],
        out_specs=(spec, spec),
        compiler_params=params,
        name="enter",
    )(near, far, whole)
    got = lax.ppermute(give, "row", [(i, i ^ 1) for i in range(rows)])

    acc = pl.pallas_call(
        own_axis_kernel,
        out_shape=tile,
        in_specs=[spec] * 4,
        out_specs=spec,
        compiler_params=params,
        cost_estimate=pl.CostEstimate(flops=6 * PX * width, bytes_accessed=2 * 2**20, transcendentals=0),
        name="own_axis",
    )(keep, cst, g, local)
    mixed = pl.pallas_call(
        finish_kernel,
        out_shape=jax.ShapeDtypeStruct((PX, channels), BF16),
        in_specs=[spec] * 7,
        out_specs=spec,
        scratch_shapes=[VMEM((groups, PX, LANES), F32), VMEM((128, LANES), F32), VMEM((PX, width), BF16)],
        compiler_params=params,
        name="finish",
    )(got, cst, g, acc, gate, flat, output_weight)
    return mixed.reshape(T, T, channels)


def solution(mesh):
    return jax.shard_map(
        body,
        mesh=mesh,
        in_specs=(P("row", "col", None), P(), P(), P(), P("row", "col"), P()),
        out_specs=P("row", "col", None),
        check_vma=False,
    )
```

```python
import jax
import jax.numpy as jnp
from jax import lax
from jax.experimental import pallas as pl
from jax.experimental.pallas import tpu as pltpu
from jax.sharding import PartitionSpec as P

T = 16
PX = T * T
PW = 24
LANES = 128
XS = 4
FAR = 8
F32 = jnp.float32
BF16 = jnp.bfloat16
VMEM = pltpu.VMEM


def position():
    row, col = lax.axis_index("row"), lax.axis_index("col")
    return row % 2, row // 2, col % XS, col // XS


def project(x, wv_ref, store):
    for half in range(wv_ref.shape[1] // 512):
        p = jnp.dot(x, wv_ref[:, half * 256:(half + 1) * 256], preferred_element_type=F32)
        p = p.astype(BF16).astype(F32)
        store(2 * half, p[:, :LANES])
        store(2 * half + 1, p[:, LANES:])


def add_taps(acc, v_ref, taps_ref, ct, lanes, jt, shifts):
    for b in shifts:
        tap = [taps_ref[a, pl.ds(b, 1), lanes] for a in range(7)]
        tap = [jnp.broadcast_to(t, (8, LANES)) for t in tap]
        for r in range(T + 6):
            x = v_ref[ct, pl.ds(r * PW + jt * 8 + b, 8), :]
            for a in range(7):
                i = r - a
                if 0 <= i < T:
                    acc[i] = tap[a] * x if acc[i] is None else acc[i] + tap[a] * x
    return acc


def fall(x):
    series = x * (1.0 - x / 2.0 * (1.0 - x / 3.0 * (1.0 - x / 4.0 * (1.0 - x / 5.0 * (1.0 - x / 6.0)))))
    return jnp.where(x < 0.1, series, 1.0 - jnp.exp(-x))


def spread_decays(table_ref, extra_ref, cst_ref, whole_ref, g_ref, tails_ref, flow_refs, h_ref):
    table = table_ref[...]
    cst_ref[0:4] = jnp.exp(-table)
    cst_ref[4:8] = fall(2.0 * table)
    cst_ref[8:12] = jnp.exp(-2.0 * table)
    cst_ref[12:16] = jnp.exp(-float(T) * table)
    for d in range(4):
        for ct in range(table.shape[1] // LANES):
            whole_ref[d, ct * T:(ct + 1) * T] = jnp.broadcast_to(
                cst_ref[12 + d:13 + d, ct * LANES:(ct + 1) * LANES], (T, LANES))
    extra = extra_ref[...]
    diagonal = lax.broadcasted_iota(jnp.int32, (T, T), 0) == lax.broadcasted_iota(jnp.int32, (T, T), 1)
    down = jnp.zeros((T, LANES), F32)
    for i in range(T):
        line = jnp.broadcast_to(extra[i:i + 1], (T, T))
        line = jnp.sum(jnp.where(diagonal, line, 0.0), axis=1, keepdims=True)
        line = jnp.broadcast_to(line, (T, LANES))
        g_ref[i * T:(i + 1) * T] = jnp.exp(-line)
        h_ref[i * T:(i + 1) * T] = fall(2.0 * line)
        down = down + line
    across = jnp.broadcast_to(jnp.sum(extra, axis=1, keepdims=True), (T, LANES))
    lane = lax.broadcasted_iota(jnp.int32, (T, LANES), 1)
    for k, total in enumerate((across, down)):
        decay = jnp.exp(-total)
        high = decay.astype(BF16).astype(F32)
        tails_ref[k] = jnp.where(lane < 64, high, decay - high).astype(BF16)

    def group(ct, carry):
        lanes = pl.ds(pl.multiple_of(ct * LANES, LANES), LANES)
        for d in range(4):
            base, slope = cst_ref[pl.ds(4 + d, 1), lanes], cst_ref[pl.ds(8 + d, 1), lanes]
            q = base + slope * h_ref[...]
            flow_refs[d // 2][d % 2, ct] = q * lax.rsqrt(q)
        return carry

    lax.fori_loop(0, flow_refs[0].shape[1], group, 0)


def inner_kernel(above_ref, tok_ref, below_ref, weight_ref, taps_ref, table_ref, extra_ref,
                 acc_ref, gate_ref, cst_ref, whole_ref, g_ref, tails_ref, along_ref, down_ref, v_ref, h_ref):
    groups = v_ref.shape[0]
    spread_decays(table_ref, extra_ref, cst_ref, whole_ref, g_ref, tails_ref, (along_ref, down_ref), h_ref)
    for ct in range(groups):
        for j in (0, 1, 2, T + 3, T + 4, T + 5):
            v_ref[ct, pl.ds(j, PW, stride=PW), :] = jnp.zeros((PW, LANES), F32)
    for ref, first in ((above_ref, 0), (tok_ref, 3), (below_ref, T + 3)):
        count = ref.shape[0] // T

        def store(ct, p, first=first, count=count):
            for i in range(count):
                v_ref[ct, pl.ds((first + i) * PW + 3, T), :] = p[i * T:(i + 1) * T]

        project(ref[...], weight_ref, store)
    width = groups * LANES
    for half in range(width // 256):
        at = slice(width + half * 256, width + (half + 1) * 256)
        pre = jnp.dot(tok_ref[...], weight_ref[:, at], preferred_element_type=F32)
        gate_ref[:, half * 256:(half + 1) * 256] = pre / (1.0 + jnp.exp(-pre))

    def group(ct, carry):
        lanes = pl.ds(pl.multiple_of(ct * LANES, LANES), LANES)
        for jt in range(2):
            acc = add_taps([None] * T, v_ref, taps_ref, ct, lanes, jt, range(7))
            for i in range(T):
                acc_ref[ct, pl.ds(i * T + jt * 8, 8), :] = acc[i]
        return carry

    lax.fori_loop(0, groups, group, 0)


def conv_scan_kernel(before_ref, after_ref, wv_ref, taps_ref, cst_ref, g_ref, along_ref, down_ref, tails_ref,
                     own_ref, acc_ref, sum_ref, near_ref, side_ref, line_ref, val_ref, end_ref):
    del own_ref
    groups = line_ref.shape[0]
    side_ref[0:3 * PW] = before_ref[...].astype(F32)
    side_ref[3 * PW:] = after_ref[...].astype(F32)

    def keep_line(ct, p):
        line_ref[ct] = p

    project(side_ref[...].astype(BF16), wv_ref, keep_line)

    def group(ct, carry):
        lanes = pl.ds(pl.multiple_of(ct * LANES, LANES), LANES)
        cst = [cst_ref[pl.ds(k, 1), lanes] for k in range(4)]

        def flow(d, at, x):
            return cst[d] * g_ref[at, :], (along_ref, down_ref)[d // 2][d % 2, ct, at, :] * x

        for side in range(2):
            outs = range(3) if side == 0 else range(T - 3, T)
            added = {}
            for a in range(7):
                for k in range(3):
                    column = k if side == 0 else T + 3 + k
                    reads = [line_ref[ct, pl.ds((3 * side + k) * PW + it * 8 + a, 8), :] for it in range(2)]
                    for j in outs:
                        if 0 <= column - j < 7:
                            tap = taps_ref[a, pl.ds(column - j, 1), lanes]
                            for it in range(2):
                                term = tap * reads[it]
                                added[j, it] = added[j, it] + term if (j, it) in added else term
            for (j, it), x in added.items():
                at = pl.ds(it * 8 * T + j, 8, stride=T)
                acc_ref[ct, at, :] = acc_ref[ct, at, :] + x
        for jt in range(2):
            acc = [acc_ref[ct, pl.ds(i * T + jt * 8, 8), :] for i in range(T)]
            vals = [x / (1.0 + jnp.exp(-x)) for x in acc]
            for i in range(T):
                val_ref[pl.ds(i * T + jt * 8, 8), :] = vals[i]
            state = jnp.zeros((8, LANES), F32)
            downs = []
            for i in range(T):
                at = pl.ds(i * T + jt * 8, 8)
                d, f = flow(2, at, vals[i])
                state = d * state + f
                downs.append(state)
            end_ref[1, pl.ds(0 + ct * T + jt * 8, 8), :] = state
            state = jnp.zeros((8, LANES), F32)
            for i in reversed(range(T)):
                at = pl.ds(i * T + jt * 8, 8)
                d, f = flow(3, at, vals[i])
                state = d * state + f
                sum_ref[ct, at, :] = downs[i] + state
            end_ref[1, pl.ds(64 + ct * T + jt * 8, 8), :] = state
        for it in range(2):
            state = jnp.zeros((8, LANES), F32)
            lefts = []
            for j in range(T):
                at = pl.ds(it * 8 * T + j, 8, stride=T)
                d, f = flow(0, at, val_ref[at, :])
                state = d * state + f
                lefts.append(state)
            end_ref[0, pl.ds(0 + ct * T + it * 8, 8), :] = state
            state = jnp.zeros((8, LANES), F32)
            for j in reversed(range(T)):
                at = pl.ds(it * 8 * T + j, 8, stride=T)
                d, f = flow(1, at, val_ref[at, :])
                state = d * state + f
                sum_ref[ct, at, :] = sum_ref[ct, at, :] + (lefts[j] + state)
            end_ref[0, pl.ds(64 + ct * T + it * 8, 8), :] = state
        return carry

    lax.fori_loop(0, groups, group, 0)
    for peer in range(2 * XS):
        near_ref[peer, 0:128] = end_ref[peer // XS].astype(BF16)
        near_ref[peer, 128:144] = tails_ref[peer // XS]


def line_decay(block, at):
    decay = jnp.broadcast_to(block[128:144, at:at + 1], (T, LANES))
    return jnp.concatenate([decay] * 4, axis=0)


def pair_decay(block, at, gap):
    return line_decay(block, at) + line_decay(block, at + gap)


def totals_kernel(near_ref, whole_ref, far_ref):
    core, y, x, z = position()
    lane = lax.broadcasted_iota(jnp.int32, (T, LANES), 1)

    def spread(first, second):
        parts = []
        for d in (first, second):
            high = d[:T].astype(BF16).astype(F32)
            parts += [high, d[:T] - high]
        return jnp.where(lane < 32, parts[0], jnp.where(
            lane < 64, parts[1], jnp.where(lane < 96, parts[2], parts[3]))).astype(BF16)

    @pl.when(core == 0)
    def _():
        ahead, back = whole_ref[0], whole_ref[1]
        products = []
        for k in range(2):
            blocks = [near_ref[k * XS + i].astype(F32) for i in range(XS)]
            decays = [pair_decay(b, 0, 64) for b in blocks]
            former, product = blocks[0][:64], decays[0]
            for i in range(1, XS):
                former = ahead * decays[i] * former + blocks[i][:64]
                product = product * decays[i]
            latter = blocks[XS - 1][64:128]
            for i in reversed(range(XS - 1)):
                latter = back * decays[i] * latter + blocks[i][64:128]
            products.append(product)
            former, latter = former.astype(BF16), latter.astype(BF16)
            for peer in range(FAR):
                far_ref[peer, 64 * k:64 * k + 64] = jnp.where(peer > z, former, latter)
        tail = spread(products[0], products[1])
        for peer in range(FAR):
            far_ref[peer, 128:144] = tail

    @pl.when(core == 1)
    def _():
        first, second = near_ref[x].astype(F32), near_ref[XS + x].astype(F32)
        decays = [pair_decay(first, 0, 64), pair_decay(second, 0, 64)]
        former = (whole_ref[2] * decays[1] * first[:64] + second[:64]).astype(BF16)
        latter = (whole_ref[3] * decays[0] * second[64:128] + first[64:128]).astype(BF16)
        product = decays[0] * decays[1]
        tail = spread(product, product)
        for peer in range(FAR):
            far_ref[peer, 0:64] = jnp.where(peer > y, former, latter)
            far_ref[peer, 64:128] = jnp.zeros((64, LANES), BF16)
            far_ref[peer, 128:144] = tail


def enter_kernel(near_ref, far_ref, whole_ref, keep_ref, give_ref):
    core, y, x, z = position()

    def far_states(me, k, ahead, back):
        blocks = [far_ref[i].astype(F32) for i in range(FAR)]
        decays = [pair_decay(b, 64 * k, 32) for b in blocks]
        fore = jnp.zeros((64, LANES), F32)
        aft = jnp.zeros((64, LANES), F32)
        for i in range(FAR - 1):
            fore = jnp.where(i < me, ahead * decays[i] * fore + blocks[i][64 * k:64 * k + 64], fore)
        for i in reversed(range(1, FAR)):
            aft = jnp.where(i > me, back * decays[i] * aft + blocks[i][64 * k:64 * k + 64], aft)
        return fore, aft

    @pl.when(core == 0)
    def _():
        ahead, back = whole_ref[0], whole_ref[1]
        ahead_far, back_far = ahead, back
        for _ in range(2):
            ahead_far, back_far = ahead_far * ahead_far, back_far * back_far
        for k in range(2):
            fore, aft = far_states(z, k, ahead_far, back_far)
            blocks = [near_ref[k * XS + i].astype(F32) for i in range(XS)]
            decays = [pair_decay(b, 0, 64) for b in blocks]
            for i in range(XS - 1):
                fore = jnp.where(i < x, ahead * decays[i] * fore + blocks[i][:64], fore)
            for i in reversed(range(1, XS)):
                aft = jnp.where(i > x, back * decays[i] * aft + blocks[i][64:128], aft)
            if k == 0:
                keep_ref[0:64], keep_ref[64:128] = fore, aft
            else:
                give_ref[0:64], give_ref[64:128] = fore.astype(BF16), aft.astype(BF16)

    @pl.when(core == 1)
    def _():
        ahead, back = whole_ref[2], whole_ref[3]
        fore, aft = far_states(y, 0, ahead * ahead, back * back)
        first, second = near_ref[x].astype(F32), near_ref[XS + x].astype(F32)
        give_ref[0:64] = fore.astype(BF16)
        give_ref[64:128] = (back * pair_decay(second, 0, 64) * aft + second[64:128]).astype(BF16)
        keep_ref[0:64] = ahead * pair_decay(first, 0, 64) * fore + first[:64]
        keep_ref[64:128] = aft


def decay_rows(kind, first, cst_ref, g_ref, store):
    def group(ct, carry):
        lanes = pl.ds(pl.multiple_of(ct * LANES, LANES), LANES)
        ahead, back = cst_ref[pl.ds(2 * kind, 1), lanes], cst_ref[pl.ds(2 * kind + 1, 1), lanes]
        for half in range(2):
            fore = first(0, ct, half)
            aft = first(1, ct, half)

            def at(n):
                return pl.ds(half * 8 * T + n, 8, stride=T) if kind == 0 else pl.ds(n * T + half * 8, 8)

            fores = []
            for n in range(T):
                fore = fore * (ahead * g_ref[at(n), :])
                fores.append(fore)
            for n in reversed(range(T)):
                aft = aft * (back * g_ref[at(n), :])
                store(ct, at(n), fores[n] + aft)
        return carry

    lax.fori_loop(0, 4, group, 0)


def own_axis_kernel(keep_ref, cst_ref, g_ref, sum_ref, acc_ref, ahead_ref, back_ref):
    def first(side, ct, half):
        return keep_ref[pl.ds(64 * side + ct * T + half * 8, 8), :]

    def store(ct, at, x):
        acc_ref[ct, at, :] = sum_ref[ct, at, :] + x

    @pl.when(position()[0] == 0)
    def _():
        decay_rows(0, first, cst_ref, g_ref, store)

    @pl.when(position()[0] == 1)
    def _():
        decay_rows(1, first, cst_ref, g_ref, store)

        def group(ct, carry):
            lanes = pl.ds(pl.multiple_of(ct * LANES, LANES), LANES)
            for side, ref, order in ((0, ahead_ref, range(T)), (1, back_ref, reversed(range(T)))):
                base = cst_ref[pl.ds(side, 1), lanes]
                states = [jnp.ones((8, LANES), F32)] * 2
                for j in order:
                    for half in range(2):
                        at = pl.ds(half * 8 * T + j, 8, stride=T)
                        states[half] = states[half] * (base * g_ref[at, :])
                        ref[ct, at, :] = states[half]
            return carry

        lax.fori_loop(0, 4, group, 0)


def finish_kernel(got_ref, cst_ref, g_ref, sum_ref, ahead_ref, back_ref, gate_ref, tok_ref, wo_ref,
                  out_ref, acc_ref, enter_ref, gated_ref):
    groups = acc_ref.shape[0]
    enter_ref[...] = got_ref[...].astype(F32)

    def first(side, ct, half):
        return enter_ref[pl.ds(64 * side + ct * T + half * 8, 8), :]

    def store(ct, at, x):
        acc_ref[ct, at, :] = sum_ref[ct, at, :] + x

    @pl.when(position()[0] == 0)
    def _():
        decay_rows(1, first, cst_ref, g_ref, store)

    @pl.when(position()[0] == 1)
    def _():
        def group(ct, carry):
            for i in range(T):
                fore, aft = enter_ref[pl.ds(ct * T + i, 1), :], enter_ref[pl.ds(64 + ct * T + i, 1), :]
                for half in range(2):
                    at = pl.ds(i * T + half * 8, 8)
                    acc_ref[ct, at, :] = sum_ref[ct, at, :] + (fore * ahead_ref[ct, at, :] + aft * back_ref[ct, at, :])
            return carry

        lax.fori_loop(0, groups, group, 0)

    for ct in range(groups):
        lanes = slice(ct * LANES, (ct + 1) * LANES)
        gated_ref[:, lanes] = (acc_ref[ct] * gate_ref[:, lanes]).astype(BF16)
    mixed = jnp.dot(gated_ref[...], wo_ref[...], preferred_element_type=F32)
    out_ref[...] = (tok_ref[...].astype(F32) + mixed).astype(BF16)


def neighbours(x_first, x_last, axis):
    size = lax.axis_size(axis)
    up = [(i, i + 1) for i in range(size - 1)]
    down = [(i + 1, i) for i in range(size - 1)]
    return lax.ppermute(x_last, axis, up), lax.ppermute(x_first, axis, down)


def near_groups(rows, cols):
    return [[(2 * y + k) * cols + XS * z + x for k in range(2) for x in range(XS)]
            for y in range(rows // 2) for z in range(cols // XS)]


def far_groups(rows, cols):
    along_z = [[2 * y * cols + XS * z + x for z in range(cols // XS)]
               for y in range(rows // 2) for x in range(XS)]
    along_y = [[(2 * y + 1) * cols + c for y in range(rows // 2)] for c in range(cols)]
    return along_z + along_y


def swap(x, groups):
    return lax.all_to_all(x, ("row", "col"), 0, 0, axis_index_groups=groups, tiled=True)


def body(tokens, input_weight, kernel, direction_decay_table, pixel_extra_decay, output_weight):
    width = output_weight.shape[0]
    groups = width // LANES
    channels = tokens.shape[2]
    rows, cols = lax.axis_size("row"), lax.axis_size("col")
    table, extra = direction_decay_table, pixel_extra_decay
    flat = tokens.reshape(PX, channels)
    above, below = neighbours(tokens[:3], tokens[T - 3:], "row")

    def strip(at):
        x = jnp.concatenate([above[:, at], tokens[:, at], below[:, at],
                             jnp.zeros((PW - T - 6, 3, channels), BF16)], axis=0)
        return x.transpose(1, 0, 2).reshape(3 * PW, channels)

    before, after = neighbours(strip(slice(0, 3)), strip(slice(T - 3, T)), "col")

    spec = pl.BlockSpec(memory_space=VMEM)
    params = pltpu.CompilerParams(vmem_limit_bytes=16 * 2**20)
    tile = jax.ShapeDtypeStruct((groups, PX, LANES), F32)
    factor = jax.ShapeDtypeStruct((2, groups, PX, LANES), F32)
    own, gate, cst, whole, g, tails, along, downward = pl.pallas_call(
        inner_kernel,
        out_shape=(tile, jax.ShapeDtypeStruct((PX, width), F32), jax.ShapeDtypeStruct((16, width), F32),
                   jax.ShapeDtypeStruct((4, groups * T, LANES), F32),
                   jax.ShapeDtypeStruct((PX, LANES), F32), jax.ShapeDtypeStruct((2, T, LANES), BF16),
                   factor, factor),
        in_specs=[spec] * 7,
        out_specs=(spec,) * 8,
        scratch_shapes=[VMEM((groups, PW * PW, LANES), F32), VMEM((PX, LANES), F32)],
        compiler_params=params,
        cost_estimate=pl.CostEstimate(flops=2 * 608 * channels * width, bytes_accessed=4 * 2**20, transcendentals=0),
        name="inner",
    )(above.reshape(3 * T, channels), flat, below.reshape(3 * T, channels), input_weight, kernel, table, extra)
    _, local, near = pl.pallas_call(
        conv_scan_kernel,
        out_shape=(tile, tile, jax.ShapeDtypeStruct((2 * XS, 144, LANES), BF16)),
        in_specs=[spec] * 10,
        out_specs=(spec, spec, spec),
        scratch_shapes=[VMEM((6 * PW, channels), F32), VMEM((groups, 6 * PW, LANES), F32),
                        VMEM((PX, LANES), F32), VMEM((2, 128, LANES), F32)],
        input_output_aliases={9: 0},
        compiler_params=params,
        name="conv_scan",
    )(before, after, input_weight, kernel, cst, g, along, downward, tails, own)
    near = swap(near, near_groups(rows, cols))

    far = pl.pallas_call(
        totals_kernel,
        out_shape=jax.ShapeDtypeStruct((FAR, 144, LANES), BF16),
        in_specs=[spec, spec],
        out_specs=spec,
        compiler_params=params,
        name="totals",
    )(near, whole)
    far = swap(far, far_groups(rows, cols))

    keep, give = pl.pallas_call(
        enter_kernel,
        out_shape=(jax.ShapeDtypeStruct((128, LANES), F32), jax.ShapeDtypeStruct((128, LANES), BF16)),
        in_specs=[spec, spec, spec],
        out_specs=(spec, spec),
        compiler_params=params,
        name="enter",
    )(near, far, whole)
    got = lax.ppermute(give, "row", [(i, i ^ 1) for i in range(rows)])

    acc, ahead, back = pl.pallas_call(
        own_axis_kernel,
        out_shape=(tile,) * 3,
        in_specs=[spec] * 4,
        out_specs=(spec,) * 3,
        compiler_params=params,
        cost_estimate=pl.CostEstimate(flops=6 * PX * width, bytes_accessed=2 * 2**20, transcendentals=0),
        name="own_axis",
    )(keep, cst, g, local)
    mixed = pl.pallas_call(
        finish_kernel,
        out_shape=jax.ShapeDtypeStruct((PX, channels), BF16),
        in_specs=[spec] * 9,
        out_specs=spec,
        scratch_shapes=[VMEM((groups, PX, LANES), F32), VMEM((128, LANES), F32), VMEM((PX, width), BF16)],
        compiler_params=params,
        name="finish",
    )(got, cst, g, acc, ahead, back, gate, flat, output_weight)
    return mixed.reshape(T, T, channels)


def solution(mesh):
    return jax.shard_map(
        body,
        mesh=mesh,
        in_specs=(P("row", "col", None), P(), P(), P(), P("row", "col"), P()),
        out_specs=P("row", "col", None),
        check_vma=False,
    )
```

```python
import jax
import jax.numpy as jnp
from jax import lax
from jax.experimental import pallas as pl
from jax.experimental.pallas import tpu as pltpu
from jax.sharding import PartitionSpec as P

T = 16
PX = T * T
PW = 24
LANES = 128
XS = 4
FAR = 8
F32 = jnp.float32
BF16 = jnp.bfloat16
VMEM = pltpu.VMEM


def position():
    row, col = lax.axis_index("row"), lax.axis_index("col")
    return row % 2, row // 2, col % XS, col // XS


def project(x, wv_ref, store):
    for half in range(wv_ref.shape[1] // 512):
        p = jnp.dot(x, wv_ref[:, half * 256:(half + 1) * 256], preferred_element_type=F32)
        p = p.astype(BF16).astype(F32)
        store(2 * half, p[:, :LANES])
        store(2 * half + 1, p[:, LANES:])


def add_taps(acc, v_ref, taps_ref, ct, lanes, jt, shifts):
    for b in shifts:
        tap = [taps_ref[a, pl.ds(b, 1), lanes] for a in range(7)]
        tap = [jnp.broadcast_to(t, (8, LANES)) for t in tap]
        for r in range(T + 6):
            x = v_ref[ct, pl.ds(r * PW + jt * 8 + b, 8), :]
            for a in range(7):
                i = r - a
                if 0 <= i < T:
                    acc[i] = tap[a] * x if acc[i] is None else acc[i] + tap[a] * x
    return acc


def fall(x):
    series = x * (1.0 - x / 2.0 * (1.0 - x / 3.0 * (1.0 - x / 4.0 * (1.0 - x / 5.0 * (1.0 - x / 6.0)))))
    return jnp.where(x < 0.1, series, 1.0 - jnp.exp(-x))


def spread_decays(table_ref, extra_ref, cst_ref, whole_ref, g_ref, across_ref, tails_ref, flow_refs, h_refs):
    table = table_ref[...]
    cst_ref[0:4] = jnp.exp(-table)
    cst_ref[4:8] = fall(2.0 * table)
    cst_ref[8:12] = jnp.exp(-2.0 * table)
    cst_ref[12:16] = jnp.exp(-float(T) * table)
    for d in range(4):
        for ct in range(table.shape[1] // LANES):
            whole_ref[d, ct * T:(ct + 1) * T] = jnp.broadcast_to(
                cst_ref[12 + d:13 + d, ct * LANES:(ct + 1) * LANES], (T, LANES))
    extra = extra_ref[...]
    diagonal = lax.broadcasted_iota(jnp.int32, (T, T), 0) == lax.broadcasted_iota(jnp.int32, (T, T), 1)
    down = jnp.zeros((T, LANES), F32)
    for i in range(T):
        line = jnp.broadcast_to(extra[i:i + 1], (T, T))
        line = jnp.sum(jnp.where(diagonal, line, 0.0), axis=1, keepdims=True)
        line = jnp.broadcast_to(line, (T, LANES))
        g_ref[i * T:(i + 1) * T] = jnp.exp(-line)
        h_refs[1][i * T:(i + 1) * T] = fall(2.0 * line)
        down = down + line
        line = jnp.broadcast_to(extra[:, i:i + 1], (T, LANES))
        across_ref[i * T:(i + 1) * T] = jnp.exp(-line)
        h_refs[0][i * T:(i + 1) * T] = fall(2.0 * line)
    across = jnp.broadcast_to(jnp.sum(extra, axis=1, keepdims=True), (T, LANES))
    lane = lax.broadcasted_iota(jnp.int32, (T, LANES), 1)
    for k, total in enumerate((across, down)):
        decay = jnp.exp(-total)
        high = decay.astype(BF16).astype(F32)
        tails_ref[k] = jnp.where(lane < 64, high, decay - high).astype(BF16)

    def group(ct, carry):
        lanes = pl.ds(pl.multiple_of(ct * LANES, LANES), LANES)
        for d in range(4):
            base, slope = cst_ref[pl.ds(4 + d, 1), lanes], cst_ref[pl.ds(8 + d, 1), lanes]
            q = base + slope * h_refs[d // 2][...]
            flow_refs[d // 2][d % 2, ct] = q * lax.rsqrt(q)
        return carry

    lax.fori_loop(0, flow_refs[0].shape[1], group, 0)


def inner_kernel(above_ref, tok_ref, below_ref, weight_ref, taps_ref, table_ref, extra_ref,
                 acc_ref, gate_ref, cst_ref, whole_ref, g_ref, across_ref, tails_ref, along_ref, down_ref,
                 v_ref, ha_ref, hd_ref):
    groups = v_ref.shape[0]
    spread_decays(table_ref, extra_ref, cst_ref, whole_ref, g_ref, across_ref, tails_ref,
                  (along_ref, down_ref), (ha_ref, hd_ref))
    for ct in range(groups):
        for j in (0, 1, 2, T + 3, T + 4, T + 5):
            v_ref[ct, pl.ds(j, PW, stride=PW), :] = jnp.zeros((PW, LANES), F32)
    for ref, first in ((above_ref, 0), (tok_ref, 3), (below_ref, T + 3)):
        count = ref.shape[0] // T

        def store(ct, p, first=first, count=count):
            for i in range(count):
                v_ref[ct, pl.ds((first + i) * PW + 3, T), :] = p[i * T:(i + 1) * T]

        project(ref[...], weight_ref, store)
    width = groups * LANES
    for half in range(width // 256):
        at = slice(width + half * 256, width + (half + 1) * 256)
        pre = jnp.dot(tok_ref[...], weight_ref[:, at], preferred_element_type=F32)
        gate_ref[:, half * 256:(half + 1) * 256] = pre / (1.0 + jnp.exp(-pre))

    def group(ct, carry):
        lanes = pl.ds(pl.multiple_of(ct * LANES, LANES), LANES)
        for jt in range(2):
            acc = add_taps([None] * T, v_ref, taps_ref, ct, lanes, jt, range(7))
            for i in range(T):
                acc_ref[ct, pl.ds(i * T + jt * 8, 8), :] = acc[i]
        return carry

    lax.fori_loop(0, groups, group, 0)


def conv_scan_kernel(before_ref, after_ref, wv_ref, taps_ref, cst_ref, g_ref, across_ref, along_ref, down_ref,
                     tails_ref, own_ref, acc_ref, sum_ref, near_ref, side_ref, line_ref, val_ref, end_ref):
    del own_ref
    groups = line_ref.shape[0]
    side_ref[0:3 * PW] = before_ref[...].astype(F32)
    side_ref[3 * PW:] = after_ref[...].astype(F32)

    def keep_line(ct, p):
        line_ref[ct] = p

    project(side_ref[...].astype(BF16), wv_ref, keep_line)

    def group(ct, carry):
        lanes = pl.ds(pl.multiple_of(ct * LANES, LANES), LANES)
        cst = [cst_ref[pl.ds(k, 1), lanes] for k in range(4)]

        def flow(d, at, x):
            g, factor = ((across_ref, along_ref), (g_ref, down_ref))[d // 2]
            return cst[d] * g[at, :], factor[d % 2, ct, at, :] * x

        for side in range(2):
            outs = range(3) if side == 0 else range(T - 3, T)
            added = {}
            for a in range(7):
                for k in range(3):
                    column = k if side == 0 else T + 3 + k
                    reads = [line_ref[ct, pl.ds((3 * side + k) * PW + it * 8 + a, 8), :] for it in range(2)]
                    for j in outs:
                        if 0 <= column - j < 7:
                            tap = taps_ref[a, pl.ds(column - j, 1), lanes]
                            for it in range(2):
                                term = tap * reads[it]
                                added[j, it] = added[j, it] + term if (j, it) in added else term
            for (j, it), x in added.items():
                at = pl.ds(it * 8 * T + j, 8, stride=T)
                acc_ref[ct, at, :] = acc_ref[ct, at, :] + x
        for jt in range(2):
            acc = [acc_ref[ct, pl.ds(i * T + jt * 8, 8), :] for i in range(T)]
            vals = [x / (1.0 + jnp.exp(-x)) for x in acc]
            for i in range(T):
                val_ref[pl.ds(i * T + jt * 8, 8), :] = vals[i]
            state = jnp.zeros((8, LANES), F32)
            downs = []
            for i in range(T):
                at = pl.ds(i * T + jt * 8, 8)
                d, f = flow(2, at, vals[i])
                state = d * state + f
                downs.append(state)
            end_ref[1, pl.ds(0 + ct * T + jt * 8, 8), :] = state
            state = jnp.zeros((8, LANES), F32)
            for i in reversed(range(T)):
                at = pl.ds(i * T + jt * 8, 8)
                d, f = flow(3, at, vals[i])
                state = d * state + f
                sum_ref[ct, at, :] = downs[i] + state
            end_ref[1, pl.ds(64 + ct * T + jt * 8, 8), :] = state
        for it in range(2):
            values = [val_ref[pl.ds(it * 8 * T + j, 8, stride=T), :] for j in range(T)]
            state = jnp.zeros((8, LANES), F32)
            lefts = []
            for j in range(T):
                d, f = flow(0, pl.ds(j * T + it * 8, 8), values[j])
                state = d * state + f
                lefts.append(state)
            end_ref[0, pl.ds(0 + ct * T + it * 8, 8), :] = state
            state = jnp.zeros((8, LANES), F32)
            for j in reversed(range(T)):
                at = pl.ds(it * 8 * T + j, 8, stride=T)
                d, f = flow(1, pl.ds(j * T + it * 8, 8), values[j])
                state = d * state + f
                sum_ref[ct, at, :] = sum_ref[ct, at, :] + (lefts[j] + state)
            end_ref[0, pl.ds(64 + ct * T + it * 8, 8), :] = state
        return carry

    lax.fori_loop(0, groups, group, 0)
    for peer in range(2 * XS):
        near_ref[peer, 0:128] = end_ref[peer // XS].astype(BF16)
        near_ref[peer, 128:144] = tails_ref[peer // XS]


def line_decay(block, at):
    decay = jnp.broadcast_to(block[128:144, at:at + 1], (T, LANES))
    return jnp.concatenate([decay] * 4, axis=0)


def pair_decay(block, at, gap):
    return line_decay(block, at) + line_decay(block, at + gap)


def totals_kernel(near_ref, whole_ref, far_ref):
    core, y, x, z = position()
    lane = lax.broadcasted_iota(jnp.int32, (T, LANES), 1)

    def spread(first, second):
        parts = []
        for d in (first, second):
            high = d[:T].astype(BF16).astype(F32)
            parts += [high, d[:T] - high]
        return jnp.where(lane < 32, parts[0], jnp.where(
            lane < 64, parts[1], jnp.where(lane < 96, parts[2], parts[3]))).astype(BF16)

    @pl.when(core == 0)
    def _():
        ahead, back = whole_ref[0], whole_ref[1]
        products = []
        for k in range(2):
            blocks = [near_ref[k * XS + i].astype(F32) for i in range(XS)]
            decays = [pair_decay(b, 0, 64) for b in blocks]
            former, product = blocks[0][:64], decays[0]
            for i in range(1, XS):
                former = ahead * decays[i] * former + blocks[i][:64]
                product = product * decays[i]
            latter = blocks[XS - 1][64:128]
            for i in reversed(range(XS - 1)):
                latter = back * decays[i] * latter + blocks[i][64:128]
            products.append(product)
            former, latter = former.astype(BF16), latter.astype(BF16)
            for peer in range(FAR):
                far_ref[peer, 64 * k:64 * k + 64] = jnp.where(peer > z, former, latter)
        tail = spread(products[0], products[1])
        for peer in range(FAR):
            far_ref[peer, 128:144] = tail

    @pl.when(core == 1)
    def _():
        first, second = near_ref[x].astype(F32), near_ref[XS + x].astype(F32)
        decays = [pair_decay(first, 0, 64), pair_decay(second, 0, 64)]
        former = (whole_ref[2] * decays[1] * first[:64] + second[:64]).astype(BF16)
        latter = (whole_ref[3] * decays[0] * second[64:128] + first[64:128]).astype(BF16)
        product = decays[0] * decays[1]
        tail = spread(product, product)
        for peer in range(FAR):
            far_ref[peer, 0:64] = jnp.where(peer > y, former, latter)
            far_ref[peer, 64:128] = jnp.zeros((64, LANES), BF16)
            far_ref[peer, 128:144] = tail


def enter_kernel(near_ref, far_ref, whole_ref, keep_ref, give_ref):
    core, y, x, z = position()

    def far_states(me, k, ahead, back):
        blocks = [far_ref[i].astype(F32) for i in range(FAR)]
        decays = [pair_decay(b, 64 * k, 32) for b in blocks]
        fore = jnp.zeros((64, LANES), F32)
        aft = jnp.zeros((64, LANES), F32)
        for i in range(FAR - 1):
            fore = jnp.where(i < me, ahead * decays[i] * fore + blocks[i][64 * k:64 * k + 64], fore)
        for i in reversed(range(1, FAR)):
            aft = jnp.where(i > me, back * decays[i] * aft + blocks[i][64 * k:64 * k + 64], aft)
        return fore, aft

    @pl.when(core == 0)
    def _():
        ahead, back = whole_ref[0], whole_ref[1]
        ahead_far, back_far = ahead, back
        for _ in range(2):
            ahead_far, back_far = ahead_far * ahead_far, back_far * back_far
        for k in range(2):
            fore, aft = far_states(z, k, ahead_far, back_far)
            blocks = [near_ref[k * XS + i].astype(F32) for i in range(XS)]
            decays = [pair_decay(b, 0, 64) for b in blocks]
            for i in range(XS - 1):
                fore = jnp.where(i < x, ahead * decays[i] * fore + blocks[i][:64], fore)
            for i in reversed(range(1, XS)):
                aft = jnp.where(i > x, back * decays[i] * aft + blocks[i][64:128], aft)
            if k == 0:
                keep_ref[0:64], keep_ref[64:128] = fore, aft
            else:
                give_ref[0:64], give_ref[64:128] = fore.astype(BF16), aft.astype(BF16)

    @pl.when(core == 1)
    def _():
        ahead, back = whole_ref[2], whole_ref[3]
        fore, aft = far_states(y, 0, ahead * ahead, back * back)
        first, second = near_ref[x].astype(F32), near_ref[XS + x].astype(F32)
        give_ref[0:64] = fore.astype(BF16)
        give_ref[64:128] = (back * pair_decay(second, 0, 64) * aft + second[64:128]).astype(BF16)
        keep_ref[0:64] = ahead * pair_decay(first, 0, 64) * fore + first[:64]
        keep_ref[64:128] = aft


def decay_rows(kind, first, cst_ref, g_ref, store):
    def group(ct, carry):
        lanes = pl.ds(pl.multiple_of(ct * LANES, LANES), LANES)
        ahead, back = cst_ref[pl.ds(2 * kind, 1), lanes], cst_ref[pl.ds(2 * kind + 1, 1), lanes]
        for half in range(2):
            fore = first(0, ct, half)
            aft = first(1, ct, half)

            def at(n):
                return pl.ds(half * 8 * T + n, 8, stride=T) if kind == 0 else pl.ds(n * T + half * 8, 8)

            fores = []
            for n in range(T):
                fore = fore * (ahead * g_ref[at(n), :])
                fores.append(fore)
            for n in reversed(range(T)):
                aft = aft * (back * g_ref[at(n), :])
                store(ct, at(n), fores[n] + aft)
        return carry

    lax.fori_loop(0, 4, group, 0)


def own_axis_kernel(keep_ref, cst_ref, g_ref, sum_ref, acc_ref, ahead_ref, back_ref):
    def first(side, ct, half):
        return keep_ref[pl.ds(64 * side + ct * T + half * 8, 8), :]

    def store(ct, at, x):
        acc_ref[ct, at, :] = sum_ref[ct, at, :] + x

    @pl.when(position()[0] == 0)
    def _():
        decay_rows(0, first, cst_ref, g_ref, store)

    @pl.when(position()[0] == 1)
    def _():
        decay_rows(1, first, cst_ref, g_ref, store)

        def group(ct, carry):
            lanes = pl.ds(pl.multiple_of(ct * LANES, LANES), LANES)
            for side, ref, order in ((0, ahead_ref, range(T)), (1, back_ref, reversed(range(T)))):
                base = cst_ref[pl.ds(side, 1), lanes]
                states = [jnp.ones((8, LANES), F32)] * 2
                for j in order:
                    for half in range(2):
                        at = pl.ds(half * 8 * T + j, 8, stride=T)
                        states[half] = states[half] * (base * g_ref[at, :])
                        ref[ct, at, :] = states[half]
            return carry

        lax.fori_loop(0, 4, group, 0)


def finish_kernel(got_ref, cst_ref, g_ref, sum_ref, ahead_ref, back_ref, gate_ref, tok_ref, wo_ref,
                  out_ref, acc_ref, enter_ref, gated_ref):
    groups = acc_ref.shape[0]
    enter_ref[...] = got_ref[...].astype(F32)

    def first(side, ct, half):
        return enter_ref[pl.ds(64 * side + ct * T + half * 8, 8), :]

    def store(ct, at, x):
        acc_ref[ct, at, :] = sum_ref[ct, at, :] + x

    @pl.when(position()[0] == 0)
    def _():
        decay_rows(1, first, cst_ref, g_ref, store)

    @pl.when(position()[0] == 1)
    def _():
        def group(ct, carry):
            for i in range(T):
                fore, aft = enter_ref[pl.ds(ct * T + i, 1), :], enter_ref[pl.ds(64 + ct * T + i, 1), :]
                for half in range(2):
                    at = pl.ds(i * T + half * 8, 8)
                    acc_ref[ct, at, :] = sum_ref[ct, at, :] + (fore * ahead_ref[ct, at, :] + aft * back_ref[ct, at, :])
            return carry

        lax.fori_loop(0, groups, group, 0)

    for ct in range(groups):
        lanes = slice(ct * LANES, (ct + 1) * LANES)
        gated_ref[:, lanes] = (acc_ref[ct] * gate_ref[:, lanes]).astype(BF16)
    mixed = jnp.dot(gated_ref[...], wo_ref[...], preferred_element_type=F32)
    out_ref[...] = (tok_ref[...].astype(F32) + mixed).astype(BF16)


def neighbours(x_first, x_last, axis):
    size = lax.axis_size(axis)
    up = [(i, i + 1) for i in range(size - 1)]
    down = [(i + 1, i) for i in range(size - 1)]
    return lax.ppermute(x_last, axis, up), lax.ppermute(x_first, axis, down)


def near_groups(rows, cols):
    return [[(2 * y + k) * cols + XS * z + x for k in range(2) for x in range(XS)]
            for y in range(rows // 2) for z in range(cols // XS)]


def far_groups(rows, cols):
    along_z = [[2 * y * cols + XS * z + x for z in range(cols // XS)]
               for y in range(rows // 2) for x in range(XS)]
    along_y = [[(2 * y + 1) * cols + c for y in range(rows // 2)] for c in range(cols)]
    return along_z + along_y


def swap(x, groups):
    return lax.all_to_all(x, ("row", "col"), 0, 0, axis_index_groups=groups, tiled=True)


def body(tokens, input_weight, kernel, direction_decay_table, pixel_extra_decay, output_weight):
    width = output_weight.shape[0]
    groups = width // LANES
    channels = tokens.shape[2]
    rows, cols = lax.axis_size("row"), lax.axis_size("col")
    table, extra = direction_decay_table, pixel_extra_decay
    flat = tokens.reshape(PX, channels)
    above, below = neighbours(tokens[:3], tokens[T - 3:], "row")

    def strip(at):
        x = jnp.concatenate([above[:, at], tokens[:, at], below[:, at],
                             jnp.zeros((PW - T - 6, 3, channels), BF16)], axis=0)
        return x.transpose(1, 0, 2).reshape(3 * PW, channels)

    before, after = neighbours(strip(slice(0, 3)), strip(slice(T - 3, T)), "col")

    spec = pl.BlockSpec(memory_space=VMEM)
    params = pltpu.CompilerParams(vmem_limit_bytes=16 * 2**20)
    tile = jax.ShapeDtypeStruct((groups, PX, LANES), F32)
    spread = jax.ShapeDtypeStruct((PX, LANES), F32)
    factor = jax.ShapeDtypeStruct((2, groups, PX, LANES), F32)
    own, gate, cst, whole, g, across, tails, along, downward = pl.pallas_call(
        inner_kernel,
        out_shape=(tile, jax.ShapeDtypeStruct((PX, width), F32), jax.ShapeDtypeStruct((16, width), F32),
                   jax.ShapeDtypeStruct((4, groups * T, LANES), F32),
                   spread, spread, jax.ShapeDtypeStruct((2, T, LANES), BF16),
                   factor, factor),
        in_specs=[spec] * 7,
        out_specs=(spec,) * 9,
        scratch_shapes=[VMEM((groups, PW * PW, LANES), F32), VMEM((PX, LANES), F32), VMEM((PX, LANES), F32)],
        compiler_params=params,
        cost_estimate=pl.CostEstimate(flops=2 * 608 * channels * width, bytes_accessed=4 * 2**20, transcendentals=0),
        name="inner",
    )(above.reshape(3 * T, channels), flat, below.reshape(3 * T, channels), input_weight, kernel, table, extra)
    _, local, near = pl.pallas_call(
        conv_scan_kernel,
        out_shape=(tile, tile, jax.ShapeDtypeStruct((2 * XS, 144, LANES), BF16)),
        in_specs=[spec] * 11,
        out_specs=(spec, spec, spec),
        scratch_shapes=[VMEM((6 * PW, channels), F32), VMEM((groups, 6 * PW, LANES), F32),
                        VMEM((PX, LANES), F32), VMEM((2, 128, LANES), F32)],
        input_output_aliases={10: 0},
        compiler_params=params,
        name="conv_scan",
    )(before, after, input_weight, kernel, cst, g, across, along, downward, tails, own)
    near = swap(near, near_groups(rows, cols))

    far = pl.pallas_call(
        totals_kernel,
        out_shape=jax.ShapeDtypeStruct((FAR, 144, LANES), BF16),
        in_specs=[spec, spec],
        out_specs=spec,
        compiler_params=params,
        name="totals",
    )(near, whole)
    far = swap(far, far_groups(rows, cols))

    keep, give = pl.pallas_call(
        enter_kernel,
        out_shape=(jax.ShapeDtypeStruct((128, LANES), F32), jax.ShapeDtypeStruct((128, LANES), BF16)),
        in_specs=[spec, spec, spec],
        out_specs=(spec, spec),
        compiler_params=params,
        name="enter",
    )(near, far, whole)
    got = lax.ppermute(give, "row", [(i, i ^ 1) for i in range(rows)])

    acc, ahead, back = pl.pallas_call(
        own_axis_kernel,
        out_shape=(tile,) * 3,
        in_specs=[spec] * 4,
        out_specs=(spec,) * 3,
        compiler_params=params,
        cost_estimate=pl.CostEstimate(flops=6 * PX * width, bytes_accessed=2 * 2**20, transcendentals=0),
        name="own_axis",
    )(keep, cst, g, local)
    mixed = pl.pallas_call(
        finish_kernel,
        out_shape=jax.ShapeDtypeStruct((PX, channels), BF16),
        in_specs=[spec] * 9,
        out_specs=spec,
        scratch_shapes=[VMEM((groups, PX, LANES), F32), VMEM((128, LANES), F32), VMEM((PX, width), BF16)],
        compiler_params=params,
        name="finish",
    )(got, cst, g, acc, ahead, back, gate, flat, output_weight)
    return mixed.reshape(T, T, channels)


def solution(mesh):
    return jax.shard_map(
        body,
        mesh=mesh,
        in_specs=(P("row", "col", None), P(), P(), P(), P("row", "col"), P()),
        out_specs=P("row", "col", None),
        check_vma=False,
    )
```

```python
import jax
import jax.numpy as jnp
from jax import lax
from jax.experimental import pallas as pl
from jax.experimental.pallas import tpu as pltpu
from jax.sharding import PartitionSpec as P

T = 16
PX = T * T
PW = 24
LANES = 128
XS = 4
FAR = 8
F32 = jnp.float32
BF16 = jnp.bfloat16
VMEM = pltpu.VMEM


def position():
    row, col = lax.axis_index("row"), lax.axis_index("col")
    return row % 2, row // 2, col % XS, col // XS


def project(x, wv_ref, store):
    for half in range(wv_ref.shape[1] // 512):
        p = jnp.dot(x, wv_ref[:, half * 256:(half + 1) * 256], preferred_element_type=F32)
        p = p.astype(BF16).astype(F32)
        store(2 * half, p[:, :LANES])
        store(2 * half + 1, p[:, LANES:])


def add_taps(acc, v_ref, taps_ref, ct, lanes, jt, shifts):
    for b in shifts:
        tap = [taps_ref[a, pl.ds(b, 1), lanes] for a in range(7)]
        tap = [jnp.broadcast_to(t, (8, LANES)) for t in tap]
        for r in range(T + 6):
            x = v_ref[ct, pl.ds(r * PW + jt * 8 + b, 8), :]
            for a in range(7):
                i = r - a
                if 0 <= i < T:
                    acc[i] = tap[a] * x if acc[i] is None else acc[i] + tap[a] * x
    return acc


def fall(x):
    series = x * (1.0 - x / 2.0 * (1.0 - x / 3.0 * (1.0 - x / 4.0 * (1.0 - x / 5.0 * (1.0 - x / 6.0)))))
    return jnp.where(x < 0.1, series, 1.0 - jnp.exp(-x))


def spread_decays(table_ref, extra_ref, cst_ref, whole_ref, g_ref, across_ref, tails_ref, flow_refs, h_refs):
    table = table_ref[...]
    cst_ref[0:4] = jnp.exp(-table)
    cst_ref[4:8] = fall(2.0 * table)
    cst_ref[8:12] = jnp.exp(-2.0 * table)
    cst_ref[12:16] = jnp.exp(-float(T) * table)
    for d in range(4):
        for ct in range(table.shape[1] // LANES):
            whole_ref[d, ct * T:(ct + 1) * T] = jnp.broadcast_to(
                cst_ref[12 + d:13 + d, ct * LANES:(ct + 1) * LANES], (T, LANES))
    extra = extra_ref[...]
    diagonal = lax.broadcasted_iota(jnp.int32, (T, T), 0) == lax.broadcasted_iota(jnp.int32, (T, T), 1)
    down = jnp.zeros((T, LANES), F32)
    for i in range(T):
        line = jnp.broadcast_to(extra[i:i + 1], (T, T))
        line = jnp.sum(jnp.where(diagonal, line, 0.0), axis=1, keepdims=True)
        line = jnp.broadcast_to(line, (T, LANES))
        g_ref[i * T:(i + 1) * T] = jnp.exp(-line)
        h_refs[1][i * T:(i + 1) * T] = fall(2.0 * line)
        down = down + line
        line = jnp.broadcast_to(extra[:, i:i + 1], (T, LANES))
        across_ref[i * T:(i + 1) * T] = jnp.exp(-line)
        h_refs[0][i * T:(i + 1) * T] = fall(2.0 * line)
    across = jnp.broadcast_to(jnp.sum(extra, axis=1, keepdims=True), (T, LANES))
    lane = lax.broadcasted_iota(jnp.int32, (T, LANES), 1)
    for k, total in enumerate((across, down)):
        decay = jnp.exp(-total)
        high = decay.astype(BF16).astype(F32)
        tails_ref[k] = jnp.where(lane < 64, high, decay - high).astype(BF16)

    def group(ct, carry):
        lanes = pl.ds(pl.multiple_of(ct * LANES, LANES), LANES)
        for d in range(4):
            base, slope = cst_ref[pl.ds(4 + d, 1), lanes], cst_ref[pl.ds(8 + d, 1), lanes]
            q = base + slope * h_refs[d // 2][...]
            flow_refs[d // 2][d % 2, ct] = q * lax.rsqrt(q)
        return carry

    lax.fori_loop(0, flow_refs[0].shape[1], group, 0)


def inner_kernel(above_ref, tok_ref, below_ref, weight_ref, taps_ref, table_ref, extra_ref,
                 acc_ref, gate_ref, cst_ref, whole_ref, g_ref, across_ref, tails_ref, along_ref, down_ref,
                 v_ref, ha_ref, hd_ref):
    groups = v_ref.shape[0]
    spread_decays(table_ref, extra_ref, cst_ref, whole_ref, g_ref, across_ref, tails_ref,
                  (along_ref, down_ref), (ha_ref, hd_ref))
    for ct in range(groups):
        for r in range(T + 6):
            for j in (0, 2 * 8):
                v_ref[ct, pl.ds(r * PW + j, 8), :] = jnp.zeros((8, LANES), F32)
    for ref, first in ((above_ref, 0), (tok_ref, 3), (below_ref, T + 3)):
        count = ref.shape[0] // T

        def store(ct, p, first=first, count=count):
            for i in range(count):
                v_ref[ct, pl.ds((first + i) * PW + 3, T), :] = p[i * T:(i + 1) * T]

        project(ref[...], weight_ref, store)
    width = groups * LANES
    for half in range(width // 256):
        at = slice(width + half * 256, width + (half + 1) * 256)
        pre = jnp.dot(tok_ref[...], weight_ref[:, at], preferred_element_type=F32)
        gate_ref[:, half * 256:(half + 1) * 256] = pre / (1.0 + jnp.exp(-pre))

    def group(ct, carry):
        lanes = pl.ds(pl.multiple_of(ct * LANES, LANES), LANES)
        for jt in range(2):
            acc = add_taps([None] * T, v_ref, taps_ref, ct, lanes, jt, range(7))
            for i in range(T):
                acc_ref[ct, pl.ds(i * T + jt * 8, 8), :] = acc[i]
        return carry

    lax.fori_loop(0, groups, group, 0)


def conv_scan_kernel(before_ref, after_ref, wv_ref, taps_ref, cst_ref, g_ref, across_ref, along_ref, down_ref,
                     tails_ref, own_ref, acc_ref, sum_ref, near_ref, side_ref, line_ref, val_ref, end_ref):
    del own_ref
    groups = line_ref.shape[0]
    side_ref[0:3 * PW] = before_ref[...].astype(F32)
    side_ref[3 * PW:] = after_ref[...].astype(F32)

    def keep_line(ct, p):
        line_ref[ct] = p

    project(side_ref[...].astype(BF16), wv_ref, keep_line)

    def group(ct, carry):
        lanes = pl.ds(pl.multiple_of(ct * LANES, LANES), LANES)
        cst = [cst_ref[pl.ds(k, 1), lanes] for k in range(4)]

        def flow(d, at, x):
            g, factor = ((across_ref, along_ref), (g_ref, down_ref))[d // 2]
            return cst[d] * g[at, :], factor[d % 2, ct, at, :] * x

        for side in range(2):
            outs = range(3) if side == 0 else range(T - 3, T)
            added = {}
            for a in range(7):
                for k in range(3):
                    column = k if side == 0 else T + 3 + k
                    reads = [line_ref[ct, pl.ds((3 * side + k) * PW + it * 8 + a, 8), :] for it in range(2)]
                    for j in outs:
                        if 0 <= column - j < 7:
                            tap = taps_ref[a, pl.ds(column - j, 1), lanes]
                            for it in range(2):
                                term = tap * reads[it]
                                added[j, it] = added[j, it] + term if (j, it) in added else term
            for (j, it), x in added.items():
                at = pl.ds(it * 8 * T + j, 8, stride=T)
                acc_ref[ct, at, :] = acc_ref[ct, at, :] + x
        for jt in range(2):
            acc = [acc_ref[ct, pl.ds(i * T + jt * 8, 8), :] for i in range(T)]
            vals = [x / (1.0 + jnp.exp(-x)) for x in acc]
            for i in range(T):
                val_ref[pl.ds(i * T + jt * 8, 8), :] = vals[i]
        for it in range(2):
            values = [val_ref[pl.ds(it * 8 * T + j, 8, stride=T), :] for j in range(T)]
            state = jnp.zeros((8, LANES), F32)
            lefts = []
            for j in range(T):
                d, f = flow(0, pl.ds(j * T + it * 8, 8), values[j])
                state = d * state + f
                lefts.append(state)
            end_ref[0, pl.ds(0 + ct * T + it * 8, 8), :] = state
            state = jnp.zeros((8, LANES), F32)
            for j in reversed(range(T)):
                at = pl.ds(it * 8 * T + j, 8, stride=T)
                d, f = flow(1, pl.ds(j * T + it * 8, 8), values[j])
                state = d * state + f
                sum_ref[ct, at, :] = lefts[j] + state
            end_ref[0, pl.ds(64 + ct * T + it * 8, 8), :] = state
        for jt in range(2):
            state = jnp.zeros((8, LANES), F32)
            downs = []
            for i in range(T):
                at = pl.ds(i * T + jt * 8, 8)
                d, f = flow(2, at, val_ref[at, :])
                state = d * state + f
                downs.append(state)
            end_ref[1, pl.ds(0 + ct * T + jt * 8, 8), :] = state
            state = jnp.zeros((8, LANES), F32)
            for i in reversed(range(T)):
                at = pl.ds(i * T + jt * 8, 8)
                d, f = flow(3, at, val_ref[at, :])
                state = d * state + f
                sum_ref[ct, at, :] = sum_ref[ct, at, :] + (downs[i] + state)
            end_ref[1, pl.ds(64 + ct * T + jt * 8, 8), :] = state
        return carry

    lax.fori_loop(0, groups, group, 0)
    for peer in range(2 * XS):
        near_ref[peer, 0:128] = end_ref[peer // XS].astype(BF16)
        near_ref[peer, 128:144] = tails_ref[peer // XS]


def line_decay(block, at):
    decay = jnp.broadcast_to(block[128:144, at:at + 1], (T, LANES))
    return jnp.concatenate([decay] * 4, axis=0)


def pair_decay(block, at, gap):
    return line_decay(block, at) + line_decay(block, at + gap)


def totals_kernel(near_ref, whole_ref, far_ref):
    core, y, x, z = position()
    lane = lax.broadcasted_iota(jnp.int32, (T, LANES), 1)

    def spread(first, second):
        parts = []
        for d in (first, second):
            high = d[:T].astype(BF16).astype(F32)
            parts += [high, d[:T] - high]
        return jnp.where(lane < 32, parts[0], jnp.where(
            lane < 64, parts[1], jnp.where(lane < 96, parts[2], parts[3]))).astype(BF16)

    @pl.when(core == 0)
    def _():
        ahead, back = whole_ref[0], whole_ref[1]
        products = []
        for k in range(2):
            blocks = [near_ref[k * XS + i].astype(F32) for i in range(XS)]
            decays = [pair_decay(b, 0, 64) for b in blocks]
            former, product = blocks[0][:64], decays[0]
            for i in range(1, XS):
                former = ahead * decays[i] * former + blocks[i][:64]
                product = product * decays[i]
            latter = blocks[XS - 1][64:128]
            for i in reversed(range(XS - 1)):
                latter = back * decays[i] * latter + blocks[i][64:128]
            products.append(product)
            former, latter = former.astype(BF16), latter.astype(BF16)
            for peer in range(FAR):
                far_ref[peer, 64 * k:64 * k + 64] = jnp.where(peer > z, former, latter)
        tail = spread(products[0], products[1])
        for peer in range(FAR):
            far_ref[peer, 128:144] = tail

    @pl.when(core == 1)
    def _():
        first, second = near_ref[x].astype(F32), near_ref[XS + x].astype(F32)
        decays = [pair_decay(first, 0, 64), pair_decay(second, 0, 64)]
        former = (whole_ref[2] * decays[1] * first[:64] + second[:64]).astype(BF16)
        latter = (whole_ref[3] * decays[0] * second[64:128] + first[64:128]).astype(BF16)
        product = decays[0] * decays[1]
        tail = spread(product, product)
        for peer in range(FAR):
            far_ref[peer, 0:64] = jnp.where(peer > y, former, latter)
            far_ref[peer, 64:128] = jnp.zeros((64, LANES), BF16)
            far_ref[peer, 128:144] = tail


def enter_kernel(near_ref, far_ref, whole_ref, keep_ref, give_ref):
    core, y, x, z = position()

    def far_states(me, k, ahead, back):
        blocks = [far_ref[i].astype(F32) for i in range(FAR)]
        decays = [pair_decay(b, 64 * k, 32) for b in blocks]
        fore = jnp.zeros((64, LANES), F32)
        aft = jnp.zeros((64, LANES), F32)
        for i in range(FAR - 1):
            fore = jnp.where(i < me, ahead * decays[i] * fore + blocks[i][64 * k:64 * k + 64], fore)
        for i in reversed(range(1, FAR)):
            aft = jnp.where(i > me, back * decays[i] * aft + blocks[i][64 * k:64 * k + 64], aft)
        return fore, aft

    @pl.when(core == 0)
    def _():
        ahead, back = whole_ref[0], whole_ref[1]
        ahead_far, back_far = ahead, back
        for _ in range(2):
            ahead_far, back_far = ahead_far * ahead_far, back_far * back_far
        for k in range(2):
            fore, aft = far_states(z, k, ahead_far, back_far)
            blocks = [near_ref[k * XS + i].astype(F32) for i in range(XS)]
            decays = [pair_decay(b, 0, 64) for b in blocks]
            for i in range(XS - 1):
                fore = jnp.where(i < x, ahead * decays[i] * fore + blocks[i][:64], fore)
            for i in reversed(range(1, XS)):
                aft = jnp.where(i > x, back * decays[i] * aft + blocks[i][64:128], aft)
            if k == 0:
                keep_ref[0:64], keep_ref[64:128] = fore, aft
            else:
                give_ref[0:64], give_ref[64:128] = fore.astype(BF16), aft.astype(BF16)

    @pl.when(core == 1)
    def _():
        ahead, back = whole_ref[2], whole_ref[3]
        fore, aft = far_states(y, 0, ahead * ahead, back * back)
        first, second = near_ref[x].astype(F32), near_ref[XS + x].astype(F32)
        give_ref[0:64] = fore.astype(BF16)
        give_ref[64:128] = (back * pair_decay(second, 0, 64) * aft + second[64:128]).astype(BF16)
        keep_ref[0:64] = ahead * pair_decay(first, 0, 64) * fore + first[:64]
        keep_ref[64:128] = aft


def decay_rows(kind, first, cst_ref, g_ref, store):
    def group(ct, carry):
        lanes = pl.ds(pl.multiple_of(ct * LANES, LANES), LANES)
        ahead, back = cst_ref[pl.ds(2 * kind, 1), lanes], cst_ref[pl.ds(2 * kind + 1, 1), lanes]
        for half in range(2):
            fore = first(0, ct, half)
            aft = first(1, ct, half)

            def at(n):
                return pl.ds(half * 8 * T + n, 8, stride=T) if kind == 0 else pl.ds(n * T + half * 8, 8)

            fores = []
            for n in range(T):
                fore = fore * (ahead * g_ref[at(n), :])
                fores.append(fore)
            for n in reversed(range(T)):
                aft = aft * (back * g_ref[at(n), :])
                store(ct, at(n), fores[n] + aft)
        return carry

    lax.fori_loop(0, 4, group, 0)


def own_axis_kernel(keep_ref, cst_ref, g_ref, sum_ref, acc_ref, ahead_ref, back_ref):
    def first(side, ct, half):
        return keep_ref[pl.ds(64 * side + ct * T + half * 8, 8), :]

    def store(ct, at, x):
        acc_ref[ct, at, :] = sum_ref[ct, at, :] + x

    @pl.when(position()[0] == 0)
    def _():
        decay_rows(0, first, cst_ref, g_ref, store)

    @pl.when(position()[0] == 1)
    def _():
        decay_rows(1, first, cst_ref, g_ref, store)

        def group(ct, carry):
            lanes = pl.ds(pl.multiple_of(ct * LANES, LANES), LANES)
            for side, ref, order in ((0, ahead_ref, range(T)), (1, back_ref, reversed(range(T)))):
                base = cst_ref[pl.ds(side, 1), lanes]
                states = [jnp.ones((8, LANES), F32)] * 2
                for j in order:
                    for half in range(2):
                        at = pl.ds(half * 8 * T + j, 8, stride=T)
                        states[half] = states[half] * (base * g_ref[at, :])
                        ref[ct, at, :] = states[half]
            return carry

        lax.fori_loop(0, 4, group, 0)


def finish_kernel(got_ref, cst_ref, g_ref, sum_ref, ahead_ref, back_ref, gate_ref, tok_ref, wo_ref,
                  out_ref, acc_ref, enter_ref, gated_ref):
    groups = acc_ref.shape[0]
    enter_ref[...] = got_ref[...].astype(F32)

    def first(side, ct, half):
        return enter_ref[pl.ds(64 * side + ct * T + half * 8, 8), :]

    def store(ct, at, x):
        acc_ref[ct, at, :] = sum_ref[ct, at, :] + x

    @pl.when(position()[0] == 0)
    def _():
        decay_rows(1, first, cst_ref, g_ref, store)

    @pl.when(position()[0] == 1)
    def _():
        def group(ct, carry):
            for i in range(T):
                fore, aft = enter_ref[pl.ds(ct * T + i, 1), :], enter_ref[pl.ds(64 + ct * T + i, 1), :]
                for half in range(2):
                    at = pl.ds(i * T + half * 8, 8)
                    acc_ref[ct, at, :] = sum_ref[ct, at, :] + (fore * ahead_ref[ct, at, :] + aft * back_ref[ct, at, :])
            return carry

        lax.fori_loop(0, groups, group, 0)

    for ct in range(groups):
        lanes = slice(ct * LANES, (ct + 1) * LANES)
        gated_ref[:, lanes] = (acc_ref[ct] * gate_ref[:, lanes]).astype(BF16)
    mixed = jnp.dot(gated_ref[...], wo_ref[...], preferred_element_type=F32)
    out_ref[...] = (tok_ref[...].astype(F32) + mixed).astype(BF16)


def neighbours(x_first, x_last, axis):
    size = lax.axis_size(axis)
    up = [(i, i + 1) for i in range(size - 1)]
    down = [(i + 1, i) for i in range(size - 1)]
    return lax.ppermute(x_last, axis, up), lax.ppermute(x_first, axis, down)


def near_groups(rows, cols):
    return [[(2 * y + k) * cols + XS * z + x for k in range(2) for x in range(XS)]
            for y in range(rows // 2) for z in range(cols // XS)]


def far_groups(rows, cols):
    along_z = [[2 * y * cols + XS * z + x for z in range(cols // XS)]
               for y in range(rows // 2) for x in range(XS)]
    along_y = [[(2 * y + 1) * cols + c for y in range(rows // 2)] for c in range(cols)]
    return along_z + along_y


def swap(x, groups):
    return lax.all_to_all(x, ("row", "col"), 0, 0, axis_index_groups=groups, tiled=True)


def body(tokens, input_weight, kernel, direction_decay_table, pixel_extra_decay, output_weight):
    width = output_weight.shape[0]
    groups = width // LANES
    channels = tokens.shape[2]
    rows, cols = lax.axis_size("row"), lax.axis_size("col")
    table, extra = direction_decay_table, pixel_extra_decay
    flat = tokens.reshape(PX, channels)
    above, below = neighbours(tokens[:3], tokens[T - 3:], "row")

    def strip(at):
        x = jnp.concatenate([above[:, at], tokens[:, at], below[:, at],
                             jnp.zeros((PW - T - 6, 3, channels), BF16)], axis=0)
        return x.transpose(1, 0, 2).reshape(3 * PW, channels)

    before, after = neighbours(strip(slice(0, 3)), strip(slice(T - 3, T)), "col")

    spec = pl.BlockSpec(memory_space=VMEM)
    params = pltpu.CompilerParams(vmem_limit_bytes=16 * 2**20)
    tile = jax.ShapeDtypeStruct((groups, PX, LANES), F32)
    spread = jax.ShapeDtypeStruct((PX, LANES), F32)
    factor = jax.ShapeDtypeStruct((2, groups, PX, LANES), F32)
    own, gate, cst, whole, g, across, tails, along, downward = pl.pallas_call(
        inner_kernel,
        out_shape=(tile, jax.ShapeDtypeStruct((PX, width), F32), jax.ShapeDtypeStruct((16, width), F32),
                   jax.ShapeDtypeStruct((4, groups * T, LANES), F32),
                   spread, spread, jax.ShapeDtypeStruct((2, T, LANES), BF16),
                   factor, factor),
        in_specs=[spec] * 7,
        out_specs=(spec,) * 9,
        scratch_shapes=[VMEM((groups, PW * PW, LANES), F32), VMEM((PX, LANES), F32), VMEM((PX, LANES), F32)],
        compiler_params=params,
        cost_estimate=pl.CostEstimate(flops=2 * 608 * channels * width, bytes_accessed=4 * 2**20, transcendentals=0),
        name="inner",
    )(above.reshape(3 * T, channels), flat, below.reshape(3 * T, channels), input_weight, kernel, table, extra)
    _, local, near = pl.pallas_call(
        conv_scan_kernel,
        out_shape=(tile, tile, jax.ShapeDtypeStruct((2 * XS, 144, LANES), BF16)),
        in_specs=[spec] * 11,
        out_specs=(spec, spec, spec),
        scratch_shapes=[VMEM((6 * PW, channels), F32), VMEM((groups, 6 * PW, LANES), F32),
                        VMEM((PX, LANES), F32), VMEM((2, 128, LANES), F32)],
        input_output_aliases={10: 0},
        compiler_params=params,
        name="conv_scan",
    )(before, after, input_weight, kernel, cst, g, across, along, downward, tails, own)
    near = swap(near, near_groups(rows, cols))

    far = pl.pallas_call(
        totals_kernel,
        out_shape=jax.ShapeDtypeStruct((FAR, 144, LANES), BF16),
        in_specs=[spec, spec],
        out_specs=spec,
        compiler_params=params,
        name="totals",
    )(near, whole)
    far = swap(far, far_groups(rows, cols))

    keep, give = pl.pallas_call(
        enter_kernel,
        out_shape=(jax.ShapeDtypeStruct((128, LANES), F32), jax.ShapeDtypeStruct((128, LANES), BF16)),
        in_specs=[spec, spec, spec],
        out_specs=(spec, spec),
        compiler_params=params,
        name="enter",
    )(near, far, whole)
    got = lax.ppermute(give, "row", [(i, i ^ 1) for i in range(rows)])

    acc, ahead, back = pl.pallas_call(
        own_axis_kernel,
        out_shape=(tile,) * 3,
        in_specs=[spec] * 4,
        out_specs=(spec,) * 3,
        compiler_params=params,
        cost_estimate=pl.CostEstimate(flops=6 * PX * width, bytes_accessed=2 * 2**20, transcendentals=0),
        name="own_axis",
    )(keep, cst, g, local)
    mixed = pl.pallas_call(
        finish_kernel,
        out_shape=jax.ShapeDtypeStruct((PX, channels), BF16),
        in_specs=[spec] * 9,
        out_specs=spec,
        scratch_shapes=[VMEM((groups, PX, LANES), F32), VMEM((128, LANES), F32), VMEM((PX, width), BF16)],
        compiler_params=params,
        name="finish",
    )(got, cst, g, acc, ahead, back, gate, flat, output_weight)
    return mixed.reshape(T, T, channels)


def solution(mesh):
    return jax.shard_map(
        body,
        mesh=mesh,
        in_specs=(P("row", "col", None), P(), P(), P(), P("row", "col"), P()),
        out_specs=P("row", "col", None),
        check_vma=False,
    )
```

```python
import jax
import jax.numpy as jnp
from jax import lax
from jax.experimental import pallas as pl
from jax.experimental.pallas import tpu as pltpu
from jax.sharding import PartitionSpec as P

T = 16
PX = T * T
PW = 24
LANES = 128
XS = 4
FAR = 8
F32 = jnp.float32
BF16 = jnp.bfloat16
VMEM = pltpu.VMEM


def position():
    row, col = lax.axis_index("row"), lax.axis_index("col")
    return row % 2, row // 2, col % XS, col // XS


def project(x, wv_ref, store):
    for half in range(wv_ref.shape[1] // 512):
        p = jnp.dot(x, wv_ref[:, half * 256:(half + 1) * 256], preferred_element_type=F32)
        p = p.astype(BF16).astype(F32)
        store(2 * half, p[:, :LANES])
        store(2 * half + 1, p[:, LANES:])


def add_taps(acc, v_ref, taps_ref, ct, lanes, jt, shifts):
    for b in shifts:
        tap = [taps_ref[a, pl.ds(b, 1), lanes] for a in range(7)]
        tap = [jnp.broadcast_to(t, (8, LANES)) for t in tap]
        for r in range(T + 6):
            x = v_ref[ct, pl.ds(r * PW + jt * 8 + b, 8), :]
            for a in range(7):
                i = r - a
                if 0 <= i < T:
                    acc[i] = tap[a] * x if acc[i] is None else acc[i] + tap[a] * x
    return acc


def fall(x):
    series = x * (1.0 - x / 2.0 * (1.0 - x / 3.0 * (1.0 - x / 4.0 * (1.0 - x / 5.0 * (1.0 - x / 6.0)))))
    return jnp.where(x < 0.1, series, 1.0 - jnp.exp(-x))


def spread_decays(table_ref, extra_ref, cst_ref, whole_ref, g_ref, across_ref, tails_ref, h_refs):
    table = table_ref[...]
    cst_ref[0:4] = jnp.exp(-table)
    cst_ref[4:8] = fall(2.0 * table)
    cst_ref[8:12] = jnp.exp(-2.0 * table)
    cst_ref[12:16] = jnp.exp(-float(T) * table)
    for d in range(4):
        for ct in range(table.shape[1] // LANES):
            whole_ref[d, ct * T:(ct + 1) * T] = jnp.broadcast_to(
                cst_ref[12 + d:13 + d, ct * LANES:(ct + 1) * LANES], (T, LANES))
    extra = extra_ref[...]
    diagonal = lax.broadcasted_iota(jnp.int32, (T, T), 0) == lax.broadcasted_iota(jnp.int32, (T, T), 1)
    down = jnp.zeros((T, LANES), F32)
    for i in range(T):
        line = jnp.broadcast_to(extra[i:i + 1], (T, T))
        line = jnp.sum(jnp.where(diagonal, line, 0.0), axis=1, keepdims=True)
        line = jnp.broadcast_to(line, (T, LANES))
        g_ref[i * T:(i + 1) * T] = jnp.exp(-line)
        h_refs[1][i * T:(i + 1) * T] = fall(2.0 * line)
        down = down + line
        line = jnp.broadcast_to(extra[:, i:i + 1], (T, LANES))
        across_ref[i * T:(i + 1) * T] = jnp.exp(-line)
        h_refs[0][i * T:(i + 1) * T] = fall(2.0 * line)
    across = jnp.broadcast_to(jnp.sum(extra, axis=1, keepdims=True), (T, LANES))
    lane = lax.broadcasted_iota(jnp.int32, (T, LANES), 1)
    for k, total in enumerate((across, down)):
        decay = jnp.exp(-total)
        high = decay.astype(BF16).astype(F32)
        tails_ref[k] = jnp.where(lane < 64, high, decay - high).astype(BF16)


def inner_kernel(above_ref, tok_ref, below_ref, weight_ref, taps_ref, table_ref, extra_ref,
                 acc_ref, gate_ref, cst_ref, whole_ref, g_ref, across_ref, tails_ref, ha_ref, hd_ref, v_ref):
    groups = v_ref.shape[0]
    spread_decays(table_ref, extra_ref, cst_ref, whole_ref, g_ref, across_ref, tails_ref, (ha_ref, hd_ref))
    for ct in range(groups):
        for r in range(T + 6):
            for j in (0, 2 * 8):
                v_ref[ct, pl.ds(r * PW + j, 8), :] = jnp.zeros((8, LANES), F32)
    for ref, first in ((above_ref, 0), (tok_ref, 3), (below_ref, T + 3)):
        count = ref.shape[0] // T

        def store(ct, p, first=first, count=count):
            for i in range(count):
                v_ref[ct, pl.ds((first + i) * PW + 3, T), :] = p[i * T:(i + 1) * T]

        project(ref[...], weight_ref, store)
    width = groups * LANES
    for half in range(width // 256):
        at = slice(width + half * 256, width + (half + 1) * 256)
        pre = jnp.dot(tok_ref[...], weight_ref[:, at], preferred_element_type=F32)
        gate_ref[:, half * 256:(half + 1) * 256] = pre / (1.0 + jnp.exp(-pre))

    def group(ct, carry):
        lanes = pl.ds(pl.multiple_of(ct * LANES, LANES), LANES)
        for jt in range(2):
            acc = add_taps([None] * T, v_ref, taps_ref, ct, lanes, jt, range(7))
            for i in range(T):
                acc_ref[ct, pl.ds(i * T + jt * 8, 8), :] = acc[i]
        return carry

    lax.fori_loop(0, groups, group, 0)


def conv_scan_kernel(before_ref, after_ref, wv_ref, taps_ref, cst_ref, g_ref, across_ref, ha_ref, hd_ref,
                     tails_ref, own_ref, acc_ref, sum_ref, near_ref, side_ref, line_ref, val_ref, end_ref):
    del own_ref
    groups = line_ref.shape[0]
    side_ref[0:3 * PW] = before_ref[...].astype(F32)
    side_ref[3 * PW:] = after_ref[...].astype(F32)

    def keep_line(ct, p):
        line_ref[ct] = p

    project(side_ref[...].astype(BF16), wv_ref, keep_line)

    def group(ct, carry):
        lanes = pl.ds(pl.multiple_of(ct * LANES, LANES), LANES)
        cst = [cst_ref[pl.ds(k, 1), lanes] for k in range(12)]

        def flow(d, at, x):
            g, h = ((across_ref, ha_ref), (g_ref, hd_ref))[d // 2]
            q = cst[4 + d] + cst[8 + d] * h[at, :]
            return cst[d] * g[at, :], q * lax.rsqrt(q) * x

        for side in range(2):
            outs = range(3) if side == 0 else range(T - 3, T)
            added = {}
            for a in range(7):
                for k in range(3):
                    column = k if side == 0 else T + 3 + k
                    reads = [line_ref[ct, pl.ds((3 * side + k) * PW + it * 8 + a, 8), :] for it in range(2)]
                    for j in outs:
                        if 0 <= column - j < 7:
                            tap = taps_ref[a, pl.ds(column - j, 1), lanes]
                            for it in range(2):
                                term = tap * reads[it]
                                added[j, it] = added[j, it] + term if (j, it) in added else term
            for (j, it), x in added.items():
                at = pl.ds(it * 8 * T + j, 8, stride=T)
                acc_ref[ct, at, :] = acc_ref[ct, at, :] + x
        for jt in range(2):
            acc = [acc_ref[ct, pl.ds(i * T + jt * 8, 8), :] for i in range(T)]
            vals = [x / (1.0 + jnp.exp(-x)) for x in acc]
            for i in range(T):
                val_ref[pl.ds(i * T + jt * 8, 8), :] = vals[i]
        for it in range(2):
            values = [val_ref[pl.ds(it * 8 * T + j, 8, stride=T), :] for j in range(T)]
            state = jnp.zeros((8, LANES), F32)
            lefts = []
            for j in range(T):
                d, f = flow(0, pl.ds(j * T + it * 8, 8), values[j])
                state = d * state + f
                lefts.append(state)
            end_ref[0, pl.ds(0 + ct * T + it * 8, 8), :] = state
            state = jnp.zeros((8, LANES), F32)
            for j in reversed(range(T)):
                at = pl.ds(it * 8 * T + j, 8, stride=T)
                d, f = flow(1, pl.ds(j * T + it * 8, 8), values[j])
                state = d * state + f
                sum_ref[ct, at, :] = lefts[j] + state
            end_ref[0, pl.ds(64 + ct * T + it * 8, 8), :] = state
        for jt in range(2):
            state = jnp.zeros((8, LANES), F32)
            downs = []
            for i in range(T):
                at = pl.ds(i * T + jt * 8, 8)
                d, f = flow(2, at, val_ref[at, :])
                state = d * state + f
                downs.append(state)
            end_ref[1, pl.ds(0 + ct * T + jt * 8, 8), :] = state
            state = jnp.zeros((8, LANES), F32)
            for i in reversed(range(T)):
                at = pl.ds(i * T + jt * 8, 8)
                d, f = flow(3, at, val_ref[at, :])
                state = d * state + f
                sum_ref[ct, at, :] = sum_ref[ct, at, :] + (downs[i] + state)
            end_ref[1, pl.ds(64 + ct * T + jt * 8, 8), :] = state
        return carry

    lax.fori_loop(0, groups, group, 0)
    for peer in range(2 * XS):
        near_ref[peer, 0:128] = end_ref[peer // XS].astype(BF16)
        near_ref[peer, 128:144] = tails_ref[peer // XS]


def line_decay(block, at):
    decay = jnp.broadcast_to(block[128:144, at:at + 1], (T, LANES))
    return jnp.concatenate([decay] * 4, axis=0)


def pair_decay(block, at, gap):
    return line_decay(block, at) + line_decay(block, at + gap)


def totals_kernel(near_ref, whole_ref, far_ref):
    core, y, x, z = position()
    lane = lax.broadcasted_iota(jnp.int32, (T, LANES), 1)

    def spread(first, second):
        parts = []
        for d in (first, second):
            high = d[:T].astype(BF16).astype(F32)
            parts += [high, d[:T] - high]
        return jnp.where(lane < 32, parts[0], jnp.where(
            lane < 64, parts[1], jnp.where(lane < 96, parts[2], parts[3]))).astype(BF16)

    @pl.when(core == 0)
    def _():
        ahead, back = whole_ref[0], whole_ref[1]
        products = []
        for k in range(2):
            blocks = [near_ref[k * XS + i].astype(F32) for i in range(XS)]
            decays = [pair_decay(b, 0, 64) for b in blocks]
            former, product = blocks[0][:64], decays[0]
            for i in range(1, XS):
                former = ahead * decays[i] * former + blocks[i][:64]
                product = product * decays[i]
            latter = blocks[XS - 1][64:128]
            for i in reversed(range(XS - 1)):
                latter = back * decays[i] * latter + blocks[i][64:128]
            products.append(product)
            former, latter = former.astype(BF16), latter.astype(BF16)
            for peer in range(FAR):
                far_ref[peer, 64 * k:64 * k + 64] = jnp.where(peer > z, former, latter)
        tail = spread(products[0], products[1])
        for peer in range(FAR):
            far_ref[peer, 128:144] = tail

    @pl.when(core == 1)
    def _():
        first, second = near_ref[x].astype(F32), near_ref[XS + x].astype(F32)
        decays = [pair_decay(first, 0, 64), pair_decay(second, 0, 64)]
        former = (whole_ref[2] * decays[1] * first[:64] + second[:64]).astype(BF16)
        latter = (whole_ref[3] * decays[0] * second[64:128] + first[64:128]).astype(BF16)
        product = decays[0] * decays[1]
        tail = spread(product, product)
        for peer in range(FAR):
            far_ref[peer, 0:64] = jnp.where(peer > y, former, latter)
            far_ref[peer, 64:128] = jnp.zeros((64, LANES), BF16)
            far_ref[peer, 128:144] = tail


def enter_kernel(near_ref, far_ref, whole_ref, keep_ref, give_ref):
    core, y, x, z = position()

    def far_states(me, k, ahead, back):
        blocks = [far_ref[i].astype(F32) for i in range(FAR)]
        decays = [pair_decay(b, 64 * k, 32) for b in blocks]
        fore = jnp.zeros((64, LANES), F32)
        aft = jnp.zeros((64, LANES), F32)
        for i in range(FAR - 1):
            fore = jnp.where(i < me, ahead * decays[i] * fore + blocks[i][64 * k:64 * k + 64], fore)
        for i in reversed(range(1, FAR)):
            aft = jnp.where(i > me, back * decays[i] * aft + blocks[i][64 * k:64 * k + 64], aft)
        return fore, aft

    @pl.when(core == 0)
    def _():
        ahead, back = whole_ref[0], whole_ref[1]
        ahead_far, back_far = ahead, back
        for _ in range(2):
            ahead_far, back_far = ahead_far * ahead_far, back_far * back_far
        for k in range(2):
            fore, aft = far_states(z, k, ahead_far, back_far)
            blocks = [near_ref[k * XS + i].astype(F32) for i in range(XS)]
            decays = [pair_decay(b, 0, 64) for b in blocks]
            for i in range(XS - 1):
                fore = jnp.where(i < x, ahead * decays[i] * fore + blocks[i][:64], fore)
            for i in reversed(range(1, XS)):
                aft = jnp.where(i > x, back * decays[i] * aft + blocks[i][64:128], aft)
            if k == 0:
                keep_ref[0:64], keep_ref[64:128] = fore, aft
            else:
                give_ref[0:64], give_ref[64:128] = fore.astype(BF16), aft.astype(BF16)

    @pl.when(core == 1)
    def _():
        ahead, back = whole_ref[2], whole_ref[3]
        fore, aft = far_states(y, 0, ahead * ahead, back * back)
        first, second = near_ref[x].astype(F32), near_ref[XS + x].astype(F32)
        give_ref[0:64] = fore.astype(BF16)
        give_ref[64:128] = (back * pair_decay(second, 0, 64) * aft + second[64:128]).astype(BF16)
        keep_ref[0:64] = ahead * pair_decay(first, 0, 64) * fore + first[:64]
        keep_ref[64:128] = aft


def decay_rows(kind, first, cst_ref, g_ref, store):
    def group(ct, carry):
        lanes = pl.ds(pl.multiple_of(ct * LANES, LANES), LANES)
        ahead, back = cst_ref[pl.ds(2 * kind, 1), lanes], cst_ref[pl.ds(2 * kind + 1, 1), lanes]
        for half in range(2):
            fore = first(0, ct, half)
            aft = first(1, ct, half)

            def at(n):
                return pl.ds(half * 8 * T + n, 8, stride=T) if kind == 0 else pl.ds(n * T + half * 8, 8)

            fores = []
            for n in range(T):
                fore = fore * (ahead * g_ref[at(n), :])
                fores.append(fore)
            for n in reversed(range(T)):
                aft = aft * (back * g_ref[at(n), :])
                store(ct, at(n), fores[n] + aft)
        return carry

    lax.fori_loop(0, 4, group, 0)


def own_axis_kernel(keep_ref, cst_ref, g_ref, sum_ref, acc_ref, ahead_ref, back_ref):
    def first(side, ct, half):
        return keep_ref[pl.ds(64 * side + ct * T + half * 8, 8), :]

    def store(ct, at, x):
        acc_ref[ct, at, :] = sum_ref[ct, at, :] + x

    @pl.when(position()[0] == 0)
    def _():
        decay_rows(0, first, cst_ref, g_ref, store)

    @pl.when(position()[0] == 1)
    def _():
        decay_rows(1, first, cst_ref, g_ref, store)

        def group(ct, carry):
            lanes = pl.ds(pl.multiple_of(ct * LANES, LANES), LANES)
            for side, ref, order in ((0, ahead_ref, range(T)), (1, back_ref, reversed(range(T)))):
                base = cst_ref[pl.ds(side, 1), lanes]
                states = [jnp.ones((8, LANES), F32)] * 2
                for j in order:
                    for half in range(2):
                        at = pl.ds(half * 8 * T + j, 8, stride=T)
                        states[half] = states[half] * (base * g_ref[at, :])
                        ref[ct, at, :] = states[half]
            return carry

        lax.fori_loop(0, 4, group, 0)


def finish_kernel(got_ref, cst_ref, g_ref, sum_ref, ahead_ref, back_ref, gate_ref, tok_ref, wo_ref,
                  out_ref, acc_ref, enter_ref, gated_ref):
    groups = acc_ref.shape[0]
    enter_ref[...] = got_ref[...].astype(F32)

    def first(side, ct, half):
        return enter_ref[pl.ds(64 * side + ct * T + half * 8, 8), :]

    def store(ct, at, x):
        acc_ref[ct, at, :] = sum_ref[ct, at, :] + x

    @pl.when(position()[0] == 0)
    def _():
        decay_rows(1, first, cst_ref, g_ref, store)

    @pl.when(position()[0] == 1)
    def _():
        def group(ct, carry):
            for i in range(T):
                fore, aft = enter_ref[pl.ds(ct * T + i, 1), :], enter_ref[pl.ds(64 + ct * T + i, 1), :]
                for half in range(2):
                    at = pl.ds(i * T + half * 8, 8)
                    acc_ref[ct, at, :] = sum_ref[ct, at, :] + (fore * ahead_ref[ct, at, :] + aft * back_ref[ct, at, :])
            return carry

        lax.fori_loop(0, groups, group, 0)

    for ct in range(groups):
        lanes = slice(ct * LANES, (ct + 1) * LANES)
        gated_ref[:, lanes] = (acc_ref[ct] * gate_ref[:, lanes]).astype(BF16)
    mixed = jnp.dot(gated_ref[...], wo_ref[...], preferred_element_type=F32)
    out_ref[...] = (tok_ref[...].astype(F32) + mixed).astype(BF16)


def neighbours(x_first, x_last, axis):
    size = lax.axis_size(axis)
    up = [(i, i + 1) for i in range(size - 1)]
    down = [(i + 1, i) for i in range(size - 1)]
    return lax.ppermute(x_last, axis, up), lax.ppermute(x_first, axis, down)


def near_groups(rows, cols):
    return [[(2 * y + k) * cols + XS * z + x for k in range(2) for x in range(XS)]
            for y in range(rows // 2) for z in range(cols // XS)]


def far_groups(rows, cols):
    along_z = [[2 * y * cols + XS * z + x for z in range(cols // XS)]
               for y in range(rows // 2) for x in range(XS)]
    along_y = [[(2 * y + 1) * cols + c for y in range(rows // 2)] for c in range(cols)]
    return along_z + along_y


def swap(x, groups):
    return lax.all_to_all(x, ("row", "col"), 0, 0, axis_index_groups=groups, tiled=True)


def body(tokens, input_weight, kernel, direction_decay_table, pixel_extra_decay, output_weight):
    width = output_weight.shape[0]
    groups = width // LANES
    channels = tokens.shape[2]
    rows, cols = lax.axis_size("row"), lax.axis_size("col")
    table, extra = direction_decay_table, pixel_extra_decay
    flat = tokens.reshape(PX, channels)
    above, below = neighbours(tokens[:3], tokens[T - 3:], "row")

    def strip(at):
        x = jnp.concatenate([above[:, at], tokens[:, at], below[:, at],
                             jnp.zeros((PW - T - 6, 3, channels), BF16)], axis=0)
        return x.transpose(1, 0, 2).reshape(3 * PW, channels)

    before, after = neighbours(strip(slice(0, 3)), strip(slice(T - 3, T)), "col")

    spec = pl.BlockSpec(memory_space=VMEM)
    params = pltpu.CompilerParams(vmem_limit_bytes=16 * 2**20)
    tile = jax.ShapeDtypeStruct((groups, PX, LANES), F32)
    spread = jax.ShapeDtypeStruct((PX, LANES), F32)
    own, gate, cst, whole, g, across, tails, ha, hd = pl.pallas_call(
        inner_kernel,
        out_shape=(tile, jax.ShapeDtypeStruct((PX, width), F32), jax.ShapeDtypeStruct((16, width), F32),
                   jax.ShapeDtypeStruct((4, groups * T, LANES), F32),
                   spread, spread, jax.ShapeDtypeStruct((2, T, LANES), BF16),
                   spread, spread),
        in_specs=[spec] * 7,
        out_specs=(spec,) * 9,
        scratch_shapes=[VMEM((groups, PW * PW, LANES), F32)],
        compiler_params=params,
        cost_estimate=pl.CostEstimate(flops=2 * 608 * channels * width, bytes_accessed=4 * 2**20, transcendentals=0),
        name="inner",
    )(above.reshape(3 * T, channels), flat, below.reshape(3 * T, channels), input_weight, kernel, table, extra)
    _, local, near = pl.pallas_call(
        conv_scan_kernel,
        out_shape=(tile, tile, jax.ShapeDtypeStruct((2 * XS, 144, LANES), BF16)),
        in_specs=[spec] * 11,
        out_specs=(spec, spec, spec),
        scratch_shapes=[VMEM((6 * PW, channels), F32), VMEM((groups, 6 * PW, LANES), F32),
                        VMEM((PX, LANES), F32), VMEM((2, 128, LANES), F32)],
        input_output_aliases={10: 0},
        compiler_params=params,
        name="conv_scan",
    )(before, after, input_weight, kernel, cst, g, across, ha, hd, tails, own)
    near = swap(near, near_groups(rows, cols))

    far = pl.pallas_call(
        totals_kernel,
        out_shape=jax.ShapeDtypeStruct((FAR, 144, LANES), BF16),
        in_specs=[spec, spec],
        out_specs=spec,
        compiler_params=params,
        name="totals",
    )(near, whole)
    far = swap(far, far_groups(rows, cols))

    keep, give = pl.pallas_call(
        enter_kernel,
        out_shape=(jax.ShapeDtypeStruct((128, LANES), F32), jax.ShapeDtypeStruct((128, LANES), BF16)),
        in_specs=[spec, spec, spec],
        out_specs=(spec, spec),
        compiler_params=params,
        name="enter",
    )(near, far, whole)
    got = lax.ppermute(give, "row", [(i, i ^ 1) for i in range(rows)])

    acc, ahead, back = pl.pallas_call(
        own_axis_kernel,
        out_shape=(tile,) * 3,
        in_specs=[spec] * 4,
        out_specs=(spec,) * 3,
        compiler_params=params,
        cost_estimate=pl.CostEstimate(flops=6 * PX * width, bytes_accessed=2 * 2**20, transcendentals=0),
        name="own_axis",
    )(keep, cst, g, local)
    mixed = pl.pallas_call(
        finish_kernel,
        out_shape=jax.ShapeDtypeStruct((PX, channels), BF16),
        in_specs=[spec] * 9,
        out_specs=spec,
        scratch_shapes=[VMEM((groups, PX, LANES), F32), VMEM((128, LANES), F32), VMEM((PX, width), BF16)],
        compiler_params=params,
        name="finish",
    )(got, cst, g, acc, ahead, back, gate, flat, output_weight)
    return mixed.reshape(T, T, channels)


def solution(mesh):
    return jax.shard_map(
        body,
        mesh=mesh,
        in_specs=(P("row", "col", None), P(), P(), P(), P("row", "col"), P()),
        out_specs=P("row", "col", None),
        check_vma=False,
    )
```

```python
import jax
import jax.numpy as jnp
from jax import lax
from jax.experimental import pallas as pl
from jax.experimental.pallas import tpu as pltpu
from jax.sharding import PartitionSpec as P

T = 16
PX = T * T
PW = 24
LANES = 128
XS = 4
FAR = 8
F32 = jnp.float32
BF16 = jnp.bfloat16
VMEM = pltpu.VMEM


def position():
    row, col = lax.axis_index("row"), lax.axis_index("col")
    return row % 2, row // 2, col % XS, col // XS


def project(x, wv_ref, store):
    for half in range(wv_ref.shape[1] // 512):
        p = jnp.dot(x, wv_ref[:, half * 256:(half + 1) * 256], preferred_element_type=F32)
        p = p.astype(BF16).astype(F32)
        store(2 * half, p[:, :LANES])
        store(2 * half + 1, p[:, LANES:])


def add_taps(acc, v_ref, taps_ref, ct, lanes, jt, shifts):
    for b in shifts:
        tap = [taps_ref[a, pl.ds(b, 1), lanes] for a in range(7)]
        tap = [jnp.broadcast_to(t, (8, LANES)) for t in tap]
        for r in range(T + 6):
            x = v_ref[ct, pl.ds(r * PW + jt * 8 + b, 8), :]
            for a in range(7):
                i = r - a
                if 0 <= i < T:
                    acc[i] = tap[a] * x if acc[i] is None else acc[i] + tap[a] * x
    return acc


def fall(x):
    series = x * (1.0 - x / 2.0 * (1.0 - x / 3.0 * (1.0 - x / 4.0 * (1.0 - x / 5.0 * (1.0 - x / 6.0)))))
    return jnp.where(x < 0.1, series, 1.0 - jnp.exp(-x))


def spread_decays(table_ref, extra_ref, cst_ref, whole_ref, g_ref, across_ref, tails_ref, h_refs):
    table = table_ref[...]
    cst_ref[0:4] = jnp.exp(-table)
    cst_ref[4:8] = fall(2.0 * table)
    cst_ref[8:12] = jnp.exp(-2.0 * table)
    cst_ref[12:16] = jnp.exp(-float(T) * table)
    for d in range(4):
        for ct in range(table.shape[1] // LANES):
            whole_ref[d, ct * T:(ct + 1) * T] = jnp.broadcast_to(
                cst_ref[12 + d:13 + d, ct * LANES:(ct + 1) * LANES], (T, LANES))
    extra = extra_ref[...]
    diagonal = lax.broadcasted_iota(jnp.int32, (T, T), 0) == lax.broadcasted_iota(jnp.int32, (T, T), 1)
    down = jnp.zeros((T, LANES), F32)
    for i in range(T):
        line = jnp.broadcast_to(extra[i:i + 1], (T, T))
        line = jnp.sum(jnp.where(diagonal, line, 0.0), axis=1, keepdims=True)
        line = jnp.broadcast_to(line, (T, LANES))
        g_ref[i * T:(i + 1) * T] = jnp.exp(-line)
        h_refs[1][i * T:(i + 1) * T] = fall(2.0 * line)
        down = down + line
        line = jnp.broadcast_to(extra[:, i:i + 1], (T, LANES))
        across_ref[i * T:(i + 1) * T] = jnp.exp(-line)
        h_refs[0][i * T:(i + 1) * T] = fall(2.0 * line)
    across = jnp.broadcast_to(jnp.sum(extra, axis=1, keepdims=True), (T, LANES))
    lane = lax.broadcasted_iota(jnp.int32, (T, LANES), 1)
    for k, total in enumerate((across, down)):
        decay = jnp.exp(-total)
        high = decay.astype(BF16).astype(F32)
        tails_ref[k] = jnp.where(lane < 64, high, decay - high).astype(BF16)


def inner_kernel(above_ref, tok_ref, below_ref, weight_ref, taps_ref, table_ref, extra_ref,
                 acc_ref, cst_ref, whole_ref, g_ref, across_ref, tails_ref, ha_ref, hd_ref, v_ref):
    groups = v_ref.shape[0]
    spread_decays(table_ref, extra_ref, cst_ref, whole_ref, g_ref, across_ref, tails_ref, (ha_ref, hd_ref))
    for ct in range(groups):
        for r in range(T + 6):
            for j in (0, 2 * 8):
                v_ref[ct, pl.ds(r * PW + j, 8), :] = jnp.zeros((8, LANES), F32)
    for ref, first in ((above_ref, 0), (tok_ref, 3), (below_ref, T + 3)):
        count = ref.shape[0] // T

        def store(ct, p, first=first, count=count):
            for i in range(count):
                v_ref[ct, pl.ds((first + i) * PW + 3, T), :] = p[i * T:(i + 1) * T]

        project(ref[...], weight_ref, store)

    def group(ct, carry):
        lanes = pl.ds(pl.multiple_of(ct * LANES, LANES), LANES)
        for jt in range(2):
            acc = add_taps([None] * T, v_ref, taps_ref, ct, lanes, jt, range(7))
            for i in range(T):
                acc_ref[ct, pl.ds(i * T + jt * 8, 8), :] = acc[i]
        return carry

    lax.fori_loop(0, groups, group, 0)


def conv_scan_kernel(before_ref, after_ref, wv_ref, taps_ref, cst_ref, g_ref, across_ref, ha_ref, hd_ref,
                     tails_ref, own_ref, acc_ref, sum_ref, near_ref, side_ref, line_ref, val_ref, end_ref):
    del own_ref
    groups = line_ref.shape[0]
    side_ref[0:3 * PW] = before_ref[...].astype(F32)
    side_ref[3 * PW:] = after_ref[...].astype(F32)

    def keep_line(ct, p):
        line_ref[ct] = p

    project(side_ref[...].astype(BF16), wv_ref, keep_line)

    def group(ct, carry):
        lanes = pl.ds(pl.multiple_of(ct * LANES, LANES), LANES)
        cst = [cst_ref[pl.ds(k, 1), lanes] for k in range(12)]

        def flow(d, at, x):
            g, h = ((across_ref, ha_ref), (g_ref, hd_ref))[d // 2]
            q = cst[4 + d] + cst[8 + d] * h[at, :]
            return cst[d] * g[at, :], q * lax.rsqrt(q) * x

        for side in range(2):
            outs = range(3) if side == 0 else range(T - 3, T)
            added = {}
            for a in range(7):
                for k in range(3):
                    column = k if side == 0 else T + 3 + k
                    reads = [line_ref[ct, pl.ds((3 * side + k) * PW + it * 8 + a, 8), :] for it in range(2)]
                    for j in outs:
                        if 0 <= column - j < 7:
                            tap = taps_ref[a, pl.ds(column - j, 1), lanes]
                            for it in range(2):
                                term = tap * reads[it]
                                added[j, it] = added[j, it] + term if (j, it) in added else term
            for (j, it), x in added.items():
                at = pl.ds(it * 8 * T + j, 8, stride=T)
                acc_ref[ct, at, :] = acc_ref[ct, at, :] + x
        for jt in range(2):
            acc = [acc_ref[ct, pl.ds(i * T + jt * 8, 8), :] for i in range(T)]
            vals = [x / (1.0 + jnp.exp(-x)) for x in acc]
            for i in range(T):
                val_ref[pl.ds(i * T + jt * 8, 8), :] = vals[i]
        for it in range(2):
            values = [val_ref[pl.ds(it * 8 * T + j, 8, stride=T), :] for j in range(T)]
            state = jnp.zeros((8, LANES), F32)
            lefts = []
            for j in range(T):
                d, f = flow(0, pl.ds(j * T + it * 8, 8), values[j])
                state = d * state + f
                lefts.append(state)
            end_ref[0, pl.ds(0 + ct * T + it * 8, 8), :] = state
            state = jnp.zeros((8, LANES), F32)
            for j in reversed(range(T)):
                at = pl.ds(it * 8 * T + j, 8, stride=T)
                d, f = flow(1, pl.ds(j * T + it * 8, 8), values[j])
                state = d * state + f
                sum_ref[ct, at, :] = lefts[j] + state
            end_ref[0, pl.ds(64 + ct * T + it * 8, 8), :] = state
        for jt in range(2):
            state = jnp.zeros((8, LANES), F32)
            downs = []
            for i in range(T):
                at = pl.ds(i * T + jt * 8, 8)
                d, f = flow(2, at, val_ref[at, :])
                state = d * state + f
                downs.append(state)
            end_ref[1, pl.ds(0 + ct * T + jt * 8, 8), :] = state
            state = jnp.zeros((8, LANES), F32)
            for i in reversed(range(T)):
                at = pl.ds(i * T + jt * 8, 8)
                d, f = flow(3, at, val_ref[at, :])
                state = d * state + f
                sum_ref[ct, at, :] = sum_ref[ct, at, :] + (downs[i] + state)
            end_ref[1, pl.ds(64 + ct * T + jt * 8, 8), :] = state
        return carry

    lax.fori_loop(0, groups, group, 0)
    for peer in range(2 * XS):
        near_ref[peer, 0:128] = end_ref[peer // XS].astype(BF16)
        near_ref[peer, 128:144] = tails_ref[peer // XS]


def line_decay(block, at):
    decay = jnp.broadcast_to(block[128:144, at:at + 1], (T, LANES))
    return jnp.concatenate([decay] * 4, axis=0)


def pair_decay(block, at, gap):
    return line_decay(block, at) + line_decay(block, at + gap)


def totals_kernel(near_ref, whole_ref, far_ref):
    core, y, x, z = position()
    lane = lax.broadcasted_iota(jnp.int32, (T, LANES), 1)

    def spread(first, second):
        parts = []
        for d in (first, second):
            high = d[:T].astype(BF16).astype(F32)
            parts += [high, d[:T] - high]
        return jnp.where(lane < 32, parts[0], jnp.where(
            lane < 64, parts[1], jnp.where(lane < 96, parts[2], parts[3]))).astype(BF16)

    @pl.when(core == 0)
    def _():
        ahead, back = whole_ref[0], whole_ref[1]
        products = []
        for k in range(2):
            blocks = [near_ref[k * XS + i].astype(F32) for i in range(XS)]
            decays = [pair_decay(b, 0, 64) for b in blocks]
            former, product = blocks[0][:64], decays[0]
            for i in range(1, XS):
                former = ahead * decays[i] * former + blocks[i][:64]
                product = product * decays[i]
            latter = blocks[XS - 1][64:128]
            for i in reversed(range(XS - 1)):
                latter = back * decays[i] * latter + blocks[i][64:128]
            products.append(product)
            former, latter = former.astype(BF16), latter.astype(BF16)
            for peer in range(FAR):
                far_ref[peer, 64 * k:64 * k + 64] = jnp.where(peer > z, former, latter)
        tail = spread(products[0], products[1])
        for peer in range(FAR):
            far_ref[peer, 128:144] = tail

    @pl.when(core == 1)
    def _():
        first, second = near_ref[x].astype(F32), near_ref[XS + x].astype(F32)
        decays = [pair_decay(first, 0, 64), pair_decay(second, 0, 64)]
        former = (whole_ref[2] * decays[1] * first[:64] + second[:64]).astype(BF16)
        latter = (whole_ref[3] * decays[0] * second[64:128] + first[64:128]).astype(BF16)
        product = decays[0] * decays[1]
        tail = spread(product, product)
        for peer in range(FAR):
            far_ref[peer, 0:64] = jnp.where(peer > y, former, latter)
            far_ref[peer, 64:128] = jnp.zeros((64, LANES), BF16)
            far_ref[peer, 128:144] = tail


def enter_kernel(near_ref, far_ref, whole_ref, keep_ref, give_ref):
    core, y, x, z = position()

    def far_states(me, k, ahead, back):
        blocks = [far_ref[i].astype(F32) for i in range(FAR)]
        decays = [pair_decay(b, 64 * k, 32) for b in blocks]
        fore = jnp.zeros((64, LANES), F32)
        aft = jnp.zeros((64, LANES), F32)
        for i in range(FAR - 1):
            fore = jnp.where(i < me, ahead * decays[i] * fore + blocks[i][64 * k:64 * k + 64], fore)
        for i in reversed(range(1, FAR)):
            aft = jnp.where(i > me, back * decays[i] * aft + blocks[i][64 * k:64 * k + 64], aft)
        return fore, aft

    @pl.when(core == 0)
    def _():
        ahead, back = whole_ref[0], whole_ref[1]
        ahead_far, back_far = ahead, back
        for _ in range(2):
            ahead_far, back_far = ahead_far * ahead_far, back_far * back_far
        for k in range(2):
            fore, aft = far_states(z, k, ahead_far, back_far)
            blocks = [near_ref[k * XS + i].astype(F32) for i in range(XS)]
            decays = [pair_decay(b, 0, 64) for b in blocks]
            for i in range(XS - 1):
                fore = jnp.where(i < x, ahead * decays[i] * fore + blocks[i][:64], fore)
            for i in reversed(range(1, XS)):
                aft = jnp.where(i > x, back * decays[i] * aft + blocks[i][64:128], aft)
            if k == 0:
                keep_ref[0:64], keep_ref[64:128] = fore, aft
            else:
                give_ref[0:64], give_ref[64:128] = fore.astype(BF16), aft.astype(BF16)

    @pl.when(core == 1)
    def _():
        ahead, back = whole_ref[2], whole_ref[3]
        fore, aft = far_states(y, 0, ahead * ahead, back * back)
        first, second = near_ref[x].astype(F32), near_ref[XS + x].astype(F32)
        give_ref[0:64] = fore.astype(BF16)
        give_ref[64:128] = (back * pair_decay(second, 0, 64) * aft + second[64:128]).astype(BF16)
        keep_ref[0:64] = ahead * pair_decay(first, 0, 64) * fore + first[:64]
        keep_ref[64:128] = aft


def decay_rows(kind, first, cst_ref, g_ref, store):
    def group(ct, carry):
        lanes = pl.ds(pl.multiple_of(ct * LANES, LANES), LANES)
        ahead, back = cst_ref[pl.ds(2 * kind, 1), lanes], cst_ref[pl.ds(2 * kind + 1, 1), lanes]
        for half in range(2):
            fore = first(0, ct, half)
            aft = first(1, ct, half)

            def at(n):
                return pl.ds(half * 8 * T + n, 8, stride=T) if kind == 0 else pl.ds(n * T + half * 8, 8)

            fores = []
            for n in range(T):
                fore = fore * (ahead * g_ref[at(n), :])
                fores.append(fore)
            for n in reversed(range(T)):
                aft = aft * (back * g_ref[at(n), :])
                store(ct, at(n), fores[n] + aft)
        return carry

    lax.fori_loop(0, 4, group, 0)


def own_axis_kernel(keep_ref, cst_ref, g_ref, sum_ref, tok_ref, weight_ref,
                    acc_ref, ahead_ref, back_ref, gate_ref):
    groups = acc_ref.shape[0]
    width = groups * LANES
    for half in range(width // 256):
        at = slice(width + half * 256, width + (half + 1) * 256)
        pre = jnp.dot(tok_ref[...], weight_ref[:, at], preferred_element_type=F32)
        gate_ref[:, half * 256:(half + 1) * 256] = pre / (1.0 + jnp.exp(-pre))

    def first(side, ct, half):
        return keep_ref[pl.ds(64 * side + ct * T + half * 8, 8), :]

    def store(ct, at, x):
        acc_ref[ct, at, :] = sum_ref[ct, at, :] + x

    @pl.when(position()[0] == 0)
    def _():
        decay_rows(0, first, cst_ref, g_ref, store)

    @pl.when(position()[0] == 1)
    def _():
        decay_rows(1, first, cst_ref, g_ref, store)

        def group(ct, carry):
            lanes = pl.ds(pl.multiple_of(ct * LANES, LANES), LANES)
            for side, ref, order in ((0, ahead_ref, range(T)), (1, back_ref, reversed(range(T)))):
                base = cst_ref[pl.ds(side, 1), lanes]
                states = [jnp.ones((8, LANES), F32)] * 2
                for j in order:
                    for half in range(2):
                        at = pl.ds(half * 8 * T + j, 8, stride=T)
                        states[half] = states[half] * (base * g_ref[at, :])
                        ref[ct, at, :] = states[half]
            return carry

        lax.fori_loop(0, 4, group, 0)


def finish_kernel(got_ref, cst_ref, g_ref, sum_ref, ahead_ref, back_ref, gate_ref, tok_ref, wo_ref,
                  out_ref, acc_ref, enter_ref, gated_ref):
    groups = acc_ref.shape[0]
    enter_ref[...] = got_ref[...].astype(F32)

    def first(side, ct, half):
        return enter_ref[pl.ds(64 * side + ct * T + half * 8, 8), :]

    def store(ct, at, x):
        acc_ref[ct, at, :] = sum_ref[ct, at, :] + x

    @pl.when(position()[0] == 0)
    def _():
        decay_rows(1, first, cst_ref, g_ref, store)

    @pl.when(position()[0] == 1)
    def _():
        def group(ct, carry):
            for i in range(T):
                fore, aft = enter_ref[pl.ds(ct * T + i, 1), :], enter_ref[pl.ds(64 + ct * T + i, 1), :]
                for half in range(2):
                    at = pl.ds(i * T + half * 8, 8)
                    acc_ref[ct, at, :] = sum_ref[ct, at, :] + (fore * ahead_ref[ct, at, :] + aft * back_ref[ct, at, :])
            return carry

        lax.fori_loop(0, groups, group, 0)

    for ct in range(groups):
        lanes = slice(ct * LANES, (ct + 1) * LANES)
        gated_ref[:, lanes] = (acc_ref[ct] * gate_ref[:, lanes]).astype(BF16)
    mixed = jnp.dot(gated_ref[...], wo_ref[...], preferred_element_type=F32)
    out_ref[...] = (tok_ref[...].astype(F32) + mixed).astype(BF16)


def neighbours(x_first, x_last, axis):
    size = lax.axis_size(axis)
    up = [(i, i + 1) for i in range(size - 1)]
    down = [(i + 1, i) for i in range(size - 1)]
    return lax.ppermute(x_last, axis, up), lax.ppermute(x_first, axis, down)


def near_groups(rows, cols):
    return [[(2 * y + k) * cols + XS * z + x for k in range(2) for x in range(XS)]
            for y in range(rows // 2) for z in range(cols // XS)]


def far_groups(rows, cols):
    along_z = [[2 * y * cols + XS * z + x for z in range(cols // XS)]
               for y in range(rows // 2) for x in range(XS)]
    along_y = [[(2 * y + 1) * cols + c for y in range(rows // 2)] for c in range(cols)]
    return along_z + along_y


def swap(x, groups):
    return lax.all_to_all(x, ("row", "col"), 0, 0, axis_index_groups=groups, tiled=True)


def body(tokens, input_weight, kernel, direction_decay_table, pixel_extra_decay, output_weight):
    width = output_weight.shape[0]
    groups = width // LANES
    channels = tokens.shape[2]
    rows, cols = lax.axis_size("row"), lax.axis_size("col")
    table, extra = direction_decay_table, pixel_extra_decay
    flat = tokens.reshape(PX, channels)
    above, below = neighbours(tokens[:3], tokens[T - 3:], "row")

    def strip(at):
        x = jnp.concatenate([above[:, at], tokens[:, at], below[:, at],
                             jnp.zeros((PW - T - 6, 3, channels), BF16)], axis=0)
        return x.transpose(1, 0, 2).reshape(3 * PW, channels)

    before, after = neighbours(strip(slice(0, 3)), strip(slice(T - 3, T)), "col")

    spec = pl.BlockSpec(memory_space=VMEM)
    params = pltpu.CompilerParams(vmem_limit_bytes=16 * 2**20)
    tile = jax.ShapeDtypeStruct((groups, PX, LANES), F32)
    spread = jax.ShapeDtypeStruct((PX, LANES), F32)
    own, cst, whole, g, across, tails, ha, hd = pl.pallas_call(
        inner_kernel,
        out_shape=(tile, jax.ShapeDtypeStruct((16, width), F32),
                   jax.ShapeDtypeStruct((4, groups * T, LANES), F32),
                   spread, spread, jax.ShapeDtypeStruct((2, T, LANES), BF16),
                   spread, spread),
        in_specs=[spec] * 7,
        out_specs=(spec,) * 8,
        scratch_shapes=[VMEM((groups, PW * PW, LANES), F32)],
        compiler_params=params,
        cost_estimate=pl.CostEstimate(flops=2 * 608 * channels * width, bytes_accessed=4 * 2**20, transcendentals=0),
        name="inner",
    )(above.reshape(3 * T, channels), flat, below.reshape(3 * T, channels), input_weight, kernel, table, extra)
    _, local, near = pl.pallas_call(
        conv_scan_kernel,
        out_shape=(tile, tile, jax.ShapeDtypeStruct((2 * XS, 144, LANES), BF16)),
        in_specs=[spec] * 11,
        out_specs=(spec, spec, spec),
        scratch_shapes=[VMEM((6 * PW, channels), F32), VMEM((groups, 6 * PW, LANES), F32),
                        VMEM((PX, LANES), F32), VMEM((2, 128, LANES), F32)],
        input_output_aliases={10: 0},
        compiler_params=params,
        name="conv_scan",
    )(before, after, input_weight, kernel, cst, g, across, ha, hd, tails, own)
    near = swap(near, near_groups(rows, cols))

    far = pl.pallas_call(
        totals_kernel,
        out_shape=jax.ShapeDtypeStruct((FAR, 144, LANES), BF16),
        in_specs=[spec, spec],
        out_specs=spec,
        compiler_params=params,
        name="totals",
    )(near, whole)
    far = swap(far, far_groups(rows, cols))

    keep, give = pl.pallas_call(
        enter_kernel,
        out_shape=(jax.ShapeDtypeStruct((128, LANES), F32), jax.ShapeDtypeStruct((128, LANES), BF16)),
        in_specs=[spec, spec, spec],
        out_specs=(spec, spec),
        compiler_params=params,
        name="enter",
    )(near, far, whole)
    got = lax.ppermute(give, "row", [(i, i ^ 1) for i in range(rows)])

    acc, ahead, back, gate = pl.pallas_call(
        own_axis_kernel,
        out_shape=(tile, tile, tile, jax.ShapeDtypeStruct((PX, width), F32)),
        in_specs=[spec] * 6,
        out_specs=(spec,) * 4,
        compiler_params=params,
        cost_estimate=pl.CostEstimate(flops=6 * PX * width, bytes_accessed=2 * 2**20, transcendentals=0),
        name="own_axis",
    )(keep, cst, g, local, flat, input_weight)
    mixed = pl.pallas_call(
        finish_kernel,
        out_shape=jax.ShapeDtypeStruct((PX, channels), BF16),
        in_specs=[spec] * 9,
        out_specs=spec,
        scratch_shapes=[VMEM((groups, PX, LANES), F32), VMEM((128, LANES), F32), VMEM((PX, width), BF16)],
        compiler_params=params,
        name="finish",
    )(got, cst, g, acc, ahead, back, gate, flat, output_weight)
    return mixed.reshape(T, T, channels)


def solution(mesh):
    return jax.shard_map(
        body,
        mesh=mesh,
        in_specs=(P("row", "col", None), P(), P(), P(), P("row", "col"), P()),
        out_specs=P("row", "col", None),
        check_vma=False,
    )
```

```python
import jax
import jax.numpy as jnp
from jax import lax
from jax.experimental import pallas as pl
from jax.experimental.pallas import tpu as pltpu
from jax.sharding import PartitionSpec as P

T = 16
PX = T * T
PW = 24
LANES = 128
XS = 4
FAR = 8
F32 = jnp.float32
BF16 = jnp.bfloat16
VMEM = pltpu.VMEM


def position():
    row, col = lax.axis_index("row"), lax.axis_index("col")
    return row % 2, row // 2, col % XS, col // XS


def project(x, wv_ref, store):
    for half in range(wv_ref.shape[1] // 512):
        p = jnp.dot(x, wv_ref[:, half * 256:(half + 1) * 256], preferred_element_type=F32)
        p = p.astype(BF16).astype(F32)
        store(2 * half, p[:, :LANES])
        store(2 * half + 1, p[:, LANES:])


def add_taps(acc, v_ref, taps_ref, ct, lanes, jt, shifts):
    for b in shifts:
        tap = [taps_ref[a, pl.ds(b, 1), lanes] for a in range(7)]
        tap = [jnp.broadcast_to(t, (8, LANES)) for t in tap]
        for r in range(T + 6):
            x = v_ref[ct, pl.ds(r * PW + jt * 8 + b, 8), :]
            for a in range(7):
                i = r - a
                if 0 <= i < T:
                    acc[i] = tap[a] * x if acc[i] is None else acc[i] + tap[a] * x
    return acc


def fall(x):
    series = x * (1.0 - x / 2.0 * (1.0 - x / 3.0 * (1.0 - x / 4.0 * (1.0 - x / 5.0 * (1.0 - x / 6.0)))))
    return jnp.where(x < 0.1, series, 1.0 - jnp.exp(-x))


def spread_decays(table_ref, extra_ref, cst_ref, whole_ref, g_ref, across_ref, tails_ref, h_refs):
    table = table_ref[...]
    cst_ref[0:4] = jnp.exp(-table)
    cst_ref[4:8] = fall(2.0 * table)
    cst_ref[8:12] = jnp.exp(-2.0 * table)
    cst_ref[12:16] = jnp.exp(-float(T) * table)
    for d in range(4):
        for ct in range(table.shape[1] // LANES):
            whole_ref[d, ct * T:(ct + 1) * T] = jnp.broadcast_to(
                cst_ref[12 + d:13 + d, ct * LANES:(ct + 1) * LANES], (T, LANES))
    extra = extra_ref[...]
    diagonal = lax.broadcasted_iota(jnp.int32, (T, T), 0) == lax.broadcasted_iota(jnp.int32, (T, T), 1)
    down = jnp.zeros((T, LANES), F32)
    for i in range(T):
        line = jnp.broadcast_to(extra[i:i + 1], (T, T))
        line = jnp.sum(jnp.where(diagonal, line, 0.0), axis=1, keepdims=True)
        line = jnp.broadcast_to(line, (T, LANES))
        g_ref[i * T:(i + 1) * T] = jnp.exp(-line)
        h_refs[1][i * T:(i + 1) * T] = fall(2.0 * line)
        down = down + line
        line = jnp.broadcast_to(extra[:, i:i + 1], (T, LANES))
        across_ref[i * T:(i + 1) * T] = jnp.exp(-line)
        h_refs[0][i * T:(i + 1) * T] = fall(2.0 * line)
    across = jnp.broadcast_to(jnp.sum(extra, axis=1, keepdims=True), (T, LANES))
    lane = lax.broadcasted_iota(jnp.int32, (T, LANES), 1)
    for k, total in enumerate((across, down)):
        decay = jnp.exp(-total)
        high = decay.astype(BF16).astype(F32)
        tails_ref[k] = jnp.where(lane < 64, high, decay - high).astype(BF16)


def inner_kernel(above_ref, tok_ref, below_ref, weight_ref, taps_ref, table_ref, extra_ref,
                 acc_ref, cst_ref, whole_ref, g_ref, across_ref, tails_ref, ha_ref, hd_ref, v_ref):
    groups = v_ref.shape[0]
    spread_decays(table_ref, extra_ref, cst_ref, whole_ref, g_ref, across_ref, tails_ref, (ha_ref, hd_ref))
    for ct in range(groups):
        for r in range(T + 6):
            for j in (0, 2 * 8):
                v_ref[ct, pl.ds(r * PW + j, 8), :] = jnp.zeros((8, LANES), F32)

    def store(ct, p):
        for i in range(T + 6):
            v_ref[ct, pl.ds(i * PW + 3, T), :] = p[i * T:(i + 1) * T]

    project(jnp.concatenate([above_ref[...], tok_ref[...], below_ref[...]], axis=0), weight_ref, store)

    def group(ct, carry):
        lanes = pl.ds(pl.multiple_of(ct * LANES, LANES), LANES)
        for jt in range(2):
            acc = add_taps([None] * T, v_ref, taps_ref, ct, lanes, jt, range(7))
            for i in range(T):
                acc_ref[ct, pl.ds(i * T + jt * 8, 8), :] = acc[i]
        return carry

    lax.fori_loop(0, groups, group, 0)


def conv_scan_kernel(before_ref, after_ref, wv_ref, taps_ref, cst_ref, g_ref, across_ref, ha_ref, hd_ref,
                     tails_ref, own_ref, acc_ref, sum_ref, near_ref, side_ref, line_ref, val_ref, end_ref):
    del own_ref
    groups = line_ref.shape[0]
    side_ref[0:3 * PW] = before_ref[...].astype(F32)
    side_ref[3 * PW:] = after_ref[...].astype(F32)

    def keep_line(ct, p):
        line_ref[ct] = p

    project(side_ref[...].astype(BF16), wv_ref, keep_line)

    def group(ct, carry):
        lanes = pl.ds(pl.multiple_of(ct * LANES, LANES), LANES)
        cst = [cst_ref[pl.ds(k, 1), lanes] for k in range(12)]

        def flow(d, at, x):
            g, h = ((across_ref, ha_ref), (g_ref, hd_ref))[d // 2]
            q = cst[4 + d] + cst[8 + d] * h[at, :]
            return cst[d] * g[at, :], q * lax.rsqrt(q) * x

        for side in range(2):
            outs = range(3) if side == 0 else range(T - 3, T)
            added = {}
            for a in range(7):
                for k in range(3):
                    column = k if side == 0 else T + 3 + k
                    reads = [line_ref[ct, pl.ds((3 * side + k) * PW + it * 8 + a, 8), :] for it in range(2)]
                    for j in outs:
                        if 0 <= column - j < 7:
                            tap = taps_ref[a, pl.ds(column - j, 1), lanes]
                            for it in range(2):
                                term = tap * reads[it]
                                added[j, it] = added[j, it] + term if (j, it) in added else term
            for (j, it), x in added.items():
                at = pl.ds(it * 8 * T + j, 8, stride=T)
                acc_ref[ct, at, :] = acc_ref[ct, at, :] + x
        for jt in range(2):
            acc = [acc_ref[ct, pl.ds(i * T + jt * 8, 8), :] for i in range(T)]
            vals = [x / (1.0 + jnp.exp(-x)) for x in acc]
            for i in range(T):
                val_ref[pl.ds(i * T + jt * 8, 8), :] = vals[i]
        for it in range(2):
            values = [val_ref[pl.ds(it * 8 * T + j, 8, stride=T), :] for j in range(T)]
            state = jnp.zeros((8, LANES), F32)
            lefts = []
            for j in range(T):
                d, f = flow(0, pl.ds(j * T + it * 8, 8), values[j])
                state = d * state + f
                lefts.append(state)
            end_ref[0, pl.ds(0 + ct * T + it * 8, 8), :] = state
            state = jnp.zeros((8, LANES), F32)
            for j in reversed(range(T)):
                at = pl.ds(it * 8 * T + j, 8, stride=T)
                d, f = flow(1, pl.ds(j * T + it * 8, 8), values[j])
                state = d * state + f
                sum_ref[ct, at, :] = lefts[j] + state
            end_ref[0, pl.ds(64 + ct * T + it * 8, 8), :] = state
        for jt in range(2):
            state = jnp.zeros((8, LANES), F32)
            downs = []
            for i in range(T):
                at = pl.ds(i * T + jt * 8, 8)
                d, f = flow(2, at, val_ref[at, :])
                state = d * state + f
                downs.append(state)
            end_ref[1, pl.ds(0 + ct * T + jt * 8, 8), :] = state
            state = jnp.zeros((8, LANES), F32)
            for i in reversed(range(T)):
                at = pl.ds(i * T + jt * 8, 8)
                d, f = flow(3, at, val_ref[at, :])
                state = d * state + f
                sum_ref[ct, at, :] = sum_ref[ct, at, :] + (downs[i] + state)
            end_ref[1, pl.ds(64 + ct * T + jt * 8, 8), :] = state
        return carry

    lax.fori_loop(0, groups, group, 0)
    for peer in range(2 * XS):
        near_ref[peer, 0:128] = end_ref[peer // XS].astype(BF16)
        near_ref[peer, 128:144] = tails_ref[peer // XS]


def line_decay(block, at):
    decay = jnp.broadcast_to(block[128:144, at:at + 1], (T, LANES))
    return jnp.concatenate([decay] * 4, axis=0)


def pair_decay(block, at, gap):
    return line_decay(block, at) + line_decay(block, at + gap)


def totals_kernel(near_ref, whole_ref, far_ref):
    core, y, x, z = position()
    lane = lax.broadcasted_iota(jnp.int32, (T, LANES), 1)

    def spread(first, second):
        parts = []
        for d in (first, second):
            high = d[:T].astype(BF16).astype(F32)
            parts += [high, d[:T] - high]
        return jnp.where(lane < 32, parts[0], jnp.where(
            lane < 64, parts[1], jnp.where(lane < 96, parts[2], parts[3]))).astype(BF16)

    @pl.when(core == 0)
    def _():
        ahead, back = whole_ref[0], whole_ref[1]
        products = []
        for k in range(2):
            blocks = [near_ref[k * XS + i].astype(F32) for i in range(XS)]
            decays = [pair_decay(b, 0, 64) for b in blocks]
            former, product = blocks[0][:64], decays[0]
            for i in range(1, XS):
                former = ahead * decays[i] * former + blocks[i][:64]
                product = product * decays[i]
            latter = blocks[XS - 1][64:128]
            for i in reversed(range(XS - 1)):
                latter = back * decays[i] * latter + blocks[i][64:128]
            products.append(product)
            former, latter = former.astype(BF16), latter.astype(BF16)
            for peer in range(FAR):
                far_ref[peer, 64 * k:64 * k + 64] = jnp.where(peer > z, former, latter)
        tail = spread(products[0], products[1])
        for peer in range(FAR):
            far_ref[peer, 128:144] = tail

    @pl.when(core == 1)
    def _():
        first, second = near_ref[x].astype(F32), near_ref[XS + x].astype(F32)
        decays = [pair_decay(first, 0, 64), pair_decay(second, 0, 64)]
        former = (whole_ref[2] * decays[1] * first[:64] + second[:64]).astype(BF16)
        latter = (whole_ref[3] * decays[0] * second[64:128] + first[64:128]).astype(BF16)
        product = decays[0] * decays[1]
        tail = spread(product, product)
        for peer in range(FAR):
            far_ref[peer, 0:64] = jnp.where(peer > y, former, latter)
            far_ref[peer, 64:128] = jnp.zeros((64, LANES), BF16)
            far_ref[peer, 128:144] = tail


def enter_kernel(near_ref, far_ref, whole_ref, keep_ref, give_ref):
    core, y, x, z = position()

    def far_states(me, k, ahead, back):
        blocks = [far_ref[i].astype(F32) for i in range(FAR)]
        decays = [pair_decay(b, 64 * k, 32) for b in blocks]
        fore = jnp.zeros((64, LANES), F32)
        aft = jnp.zeros((64, LANES), F32)
        for i in range(FAR - 1):
            fore = jnp.where(i < me, ahead * decays[i] * fore + blocks[i][64 * k:64 * k + 64], fore)
        for i in reversed(range(1, FAR)):
            aft = jnp.where(i > me, back * decays[i] * aft + blocks[i][64 * k:64 * k + 64], aft)
        return fore, aft

    @pl.when(core == 0)
    def _():
        ahead, back = whole_ref[0], whole_ref[1]
        ahead_far, back_far = ahead, back
        for _ in range(2):
            ahead_far, back_far = ahead_far * ahead_far, back_far * back_far
        for k in range(2):
            fore, aft = far_states(z, k, ahead_far, back_far)
            blocks = [near_ref[k * XS + i].astype(F32) for i in range(XS)]
            decays = [pair_decay(b, 0, 64) for b in blocks]
            for i in range(XS - 1):
                fore = jnp.where(i < x, ahead * decays[i] * fore + blocks[i][:64], fore)
            for i in reversed(range(1, XS)):
                aft = jnp.where(i > x, back * decays[i] * aft + blocks[i][64:128], aft)
            if k == 0:
                keep_ref[0:64], keep_ref[64:128] = fore, aft
            else:
                give_ref[0:64], give_ref[64:128] = fore.astype(BF16), aft.astype(BF16)

    @pl.when(core == 1)
    def _():
        ahead, back = whole_ref[2], whole_ref[3]
        fore, aft = far_states(y, 0, ahead * ahead, back * back)
        first, second = near_ref[x].astype(F32), near_ref[XS + x].astype(F32)
        give_ref[0:64] = fore.astype(BF16)
        give_ref[64:128] = (back * pair_decay(second, 0, 64) * aft + second[64:128]).astype(BF16)
        keep_ref[0:64] = ahead * pair_decay(first, 0, 64) * fore + first[:64]
        keep_ref[64:128] = aft


def decay_rows(kind, first, cst_ref, g_ref, store):
    def group(ct, carry):
        lanes = pl.ds(pl.multiple_of(ct * LANES, LANES), LANES)
        ahead, back = cst_ref[pl.ds(2 * kind, 1), lanes], cst_ref[pl.ds(2 * kind + 1, 1), lanes]
        for half in range(2):
            fore = first(0, ct, half)
            aft = first(1, ct, half)

            def at(n):
                return pl.ds(half * 8 * T + n, 8, stride=T) if kind == 0 else pl.ds(n * T + half * 8, 8)

            fores = []
            for n in range(T):
                fore = fore * (ahead * g_ref[at(n), :])
                fores.append(fore)
            for n in reversed(range(T)):
                aft = aft * (back * g_ref[at(n), :])
                store(ct, at(n), fores[n] + aft)
        return carry

    lax.fori_loop(0, 4, group, 0)


def own_axis_kernel(keep_ref, cst_ref, g_ref, sum_ref, tok_ref, weight_ref,
                    acc_ref, ahead_ref, back_ref, gate_ref):
    groups = acc_ref.shape[0]
    width = groups * LANES
    for half in range(width // 256):
        at = slice(width + half * 256, width + (half + 1) * 256)
        pre = jnp.dot(tok_ref[...], weight_ref[:, at], preferred_element_type=F32)
        gate_ref[:, half * 256:(half + 1) * 256] = pre / (1.0 + jnp.exp(-pre))

    def first(side, ct, half):
        return keep_ref[pl.ds(64 * side + ct * T + half * 8, 8), :]

    def store(ct, at, x):
        acc_ref[ct, at, :] = sum_ref[ct, at, :] + x

    @pl.when(position()[0] == 0)
    def _():
        decay_rows(0, first, cst_ref, g_ref, store)

    @pl.when(position()[0] == 1)
    def _():
        decay_rows(1, first, cst_ref, g_ref, store)

        def group(ct, carry):
            lanes = pl.ds(pl.multiple_of(ct * LANES, LANES), LANES)
            for side, ref, order in ((0, ahead_ref, range(T)), (1, back_ref, reversed(range(T)))):
                base = cst_ref[pl.ds(side, 1), lanes]
                states = [jnp.ones((8, LANES), F32)] * 2
                for j in order:
                    for half in range(2):
                        at = pl.ds(half * 8 * T + j, 8, stride=T)
                        states[half] = states[half] * (base * g_ref[at, :])
                        ref[ct, at, :] = states[half]
            return carry

        lax.fori_loop(0, 4, group, 0)


def finish_kernel(got_ref, cst_ref, g_ref, sum_ref, ahead_ref, back_ref, gate_ref, tok_ref, wo_ref,
                  out_ref, acc_ref, enter_ref, gated_ref):
    groups = acc_ref.shape[0]
    enter_ref[...] = got_ref[...].astype(F32)

    def first(side, ct, half):
        return enter_ref[pl.ds(64 * side + ct * T + half * 8, 8), :]

    def store(ct, at, x):
        acc_ref[ct, at, :] = sum_ref[ct, at, :] + x

    @pl.when(position()[0] == 0)
    def _():
        decay_rows(1, first, cst_ref, g_ref, store)

    @pl.when(position()[0] == 1)
    def _():
        def group(ct, carry):
            for i in range(T):
                fore, aft = enter_ref[pl.ds(ct * T + i, 1), :], enter_ref[pl.ds(64 + ct * T + i, 1), :]
                for half in range(2):
                    at = pl.ds(i * T + half * 8, 8)
                    acc_ref[ct, at, :] = sum_ref[ct, at, :] + (fore * ahead_ref[ct, at, :] + aft * back_ref[ct, at, :])
            return carry

        lax.fori_loop(0, groups, group, 0)

    for ct in range(groups):
        lanes = slice(ct * LANES, (ct + 1) * LANES)
        gated_ref[:, lanes] = (acc_ref[ct] * gate_ref[:, lanes]).astype(BF16)
    mixed = jnp.dot(gated_ref[...], wo_ref[...], preferred_element_type=F32)
    out_ref[...] = (tok_ref[...].astype(F32) + mixed).astype(BF16)


def neighbours(x_first, x_last, axis):
    size = lax.axis_size(axis)
    up = [(i, i + 1) for i in range(size - 1)]
    down = [(i + 1, i) for i in range(size - 1)]
    return lax.ppermute(x_last, axis, up), lax.ppermute(x_first, axis, down)


def near_groups(rows, cols):
    return [[(2 * y + k) * cols + XS * z + x for k in range(2) for x in range(XS)]
            for y in range(rows // 2) for z in range(cols // XS)]


def far_groups(rows, cols):
    along_z = [[2 * y * cols + XS * z + x for z in range(cols // XS)]
               for y in range(rows // 2) for x in range(XS)]
    along_y = [[(2 * y + 1) * cols + c for y in range(rows // 2)] for c in range(cols)]
    return along_z + along_y


def swap(x, groups):
    return lax.all_to_all(x, ("row", "col"), 0, 0, axis_index_groups=groups, tiled=True)


def body(tokens, input_weight, kernel, direction_decay_table, pixel_extra_decay, output_weight):
    width = output_weight.shape[0]
    groups = width // LANES
    channels = tokens.shape[2]
    rows, cols = lax.axis_size("row"), lax.axis_size("col")
    table, extra = direction_decay_table, pixel_extra_decay
    flat = tokens.reshape(PX, channels)
    above, below = neighbours(tokens[:3], tokens[T - 3:], "row")

    def strip(at):
        x = jnp.concatenate([above[:, at], tokens[:, at], below[:, at],
                             jnp.zeros((PW - T - 6, 3, channels), BF16)], axis=0)
        return x.transpose(1, 0, 2).reshape(3 * PW, channels)

    before, after = neighbours(strip(slice(0, 3)), strip(slice(T - 3, T)), "col")

    spec = pl.BlockSpec(memory_space=VMEM)
    params = pltpu.CompilerParams(vmem_limit_bytes=16 * 2**20)
    tile = jax.ShapeDtypeStruct((groups, PX, LANES), F32)
    spread = jax.ShapeDtypeStruct((PX, LANES), F32)
    own, cst, whole, g, across, tails, ha, hd = pl.pallas_call(
        inner_kernel,
        out_shape=(tile, jax.ShapeDtypeStruct((16, width), F32),
                   jax.ShapeDtypeStruct((4, groups * T, LANES), F32),
                   spread, spread, jax.ShapeDtypeStruct((2, T, LANES), BF16),
                   spread, spread),
        in_specs=[spec] * 7,
        out_specs=(spec,) * 8,
        scratch_shapes=[VMEM((groups, PW * PW, LANES), F32)],
        compiler_params=params,
        cost_estimate=pl.CostEstimate(flops=2 * 608 * channels * width, bytes_accessed=4 * 2**20, transcendentals=0),
        name="inner",
    )(above.reshape(3 * T, channels), flat, below.reshape(3 * T, channels), input_weight, kernel, table, extra)
    _, local, near = pl.pallas_call(
        conv_scan_kernel,
        out_shape=(tile, tile, jax.ShapeDtypeStruct((2 * XS, 144, LANES), BF16)),
        in_specs=[spec] * 11,
        out_specs=(spec, spec, spec),
        scratch_shapes=[VMEM((6 * PW, channels), F32), VMEM((groups, 6 * PW, LANES), F32),
                        VMEM((PX, LANES), F32), VMEM((2, 128, LANES), F32)],
        input_output_aliases={10: 0},
        compiler_params=params,
        name="conv_scan",
    )(before, after, input_weight, kernel, cst, g, across, ha, hd, tails, own)
    near = swap(near, near_groups(rows, cols))

    far = pl.pallas_call(
        totals_kernel,
        out_shape=jax.ShapeDtypeStruct((FAR, 144, LANES), BF16),
        in_specs=[spec, spec],
        out_specs=spec,
        compiler_params=params,
        name="totals",
    )(near, whole)
    far = swap(far, far_groups(rows, cols))

    keep, give = pl.pallas_call(
        enter_kernel,
        out_shape=(jax.ShapeDtypeStruct((128, LANES), F32), jax.ShapeDtypeStruct((128, LANES), BF16)),
        in_specs=[spec, spec, spec],
        out_specs=(spec, spec),
        compiler_params=params,
        name="enter",
    )(near, far, whole)
    got = lax.ppermute(give, "row", [(i, i ^ 1) for i in range(rows)])

    acc, ahead, back, gate = pl.pallas_call(
        own_axis_kernel,
        out_shape=(tile, tile, tile, jax.ShapeDtypeStruct((PX, width), F32)),
        in_specs=[spec] * 6,
        out_specs=(spec,) * 4,
        compiler_params=params,
        cost_estimate=pl.CostEstimate(flops=6 * PX * width, bytes_accessed=2 * 2**20, transcendentals=0),
        name="own_axis",
    )(keep, cst, g, local, flat, input_weight)
    mixed = pl.pallas_call(
        finish_kernel,
        out_shape=jax.ShapeDtypeStruct((PX, channels), BF16),
        in_specs=[spec] * 9,
        out_specs=spec,
        scratch_shapes=[VMEM((groups, PX, LANES), F32), VMEM((128, LANES), F32), VMEM((PX, width), BF16)],
        compiler_params=params,
        name="finish",
    )(got, cst, g, acc, ahead, back, gate, flat, output_weight)
    return mixed.reshape(T, T, channels)


def solution(mesh):
    return jax.shard_map(
        body,
        mesh=mesh,
        in_specs=(P("row", "col", None), P(), P(), P(), P("row", "col"), P()),
        out_specs=P("row", "col", None),
        check_vma=False,
    )
```
